128 devices in a mesh: dp: 16 (over x, y_lo, core), ctx: 8 (over z, y_hi).
Axes of the slice: x: 4, y: 4 (y_hi: 2, y_lo: 2; y = y_hi * 2 + y_lo), z: 4, core: 2. Of those that a mesh axis runs over, the one named last changes fastest.
Arguments:
- tokens: bfloat16 [32, 1024, 1280], P('dp', 'ctx'), may hold values from -6 to 6
- lengths: int32 [32], P('dp'), may hold values from 256 to 1024, as said below
- cotangent: bfloat16 [32, 1024, 1280], P('dp', 'ctx'), may hold values from -6 to 6
- ln1_gain: bfloat16 [1280], P(('dp', 'ctx')), may hold values from 0.25 to 1.75
- ln1_bias: bfloat16 [1280], P(('dp', 'ctx')), may hold values from -1.75 to 1.75
- w_qkv: bfloat16 [1280, 3840], P(('dp', 'ctx')), may hold values from -0.15625 to 0.15625
- q_bias: bfloat16 [1280], P(('dp', 'ctx')), may hold values from -1.75 to 1.75
- v_bias: bfloat16 [1280], P(('dp', 'ctx')), may hold values from -0.625 to 0.625
- w_proj: bfloat16 [1280, 1280], P(('dp', 'ctx')), may hold values from -0.625 to 0.625
- proj_bias: bfloat16 [1280], P(('dp', 'ctx')), may hold values from -1.75 to 1.75
- ln2_gain: bfloat16 [1280], P(('dp', 'ctx')), may hold values from 0.25 to 1.75
- ln2_bias: bfloat16 [1280], P(('dp', 'ctx')), may hold values from -1.75 to 1.75
- w_fc: bfloat16 [1280, 5120], P(('dp', 'ctx')), may hold values from -0.15625 to 0.15625
- fc_bias: bfloat16 [5120], P(('dp', 'ctx')), may hold values from -1.75 to 1.75
- w_out: bfloat16 [5120, 1280], P(('dp', 'ctx')), may hold values from -0.078125 to 0.078125
- out_bias: bfloat16 [1280], P(('dp', 'ctx')), may hold values from -1.75 to 1.75
Outputs:
- layer_out: bfloat16 [32, 1024, 1280], P('dp', 'ctx')
- input_grad: float32 [32, 1024, 1280], P('dp', 'ctx')
- ln1_gain_grad: float32 [1280], P(('dp', 'ctx'))
- ln1_bias_grad: float32 [1280], P(('dp', 'ctx'))
- w_qkv_grad: float32 [1280, 3840], P(('dp', 'ctx'))
- q_bias_grad: float32 [1280], P(('dp', 'ctx'))
- v_bias_grad: float32 [1280], P(('dp', 'ctx'))
- w_proj_grad: float32 [1280, 1280], P(('dp', 'ctx'))
- proj_bias_grad: float32 [1280], P(('dp', 'ctx'))
- ln2_gain_grad: float32 [1280], P(('dp', 'ctx'))
- ln2_bias_grad: float32 [1280], P(('dp', 'ctx'))
- w_fc_grad: float32 [1280, 5120], P(('dp', 'ctx'))
- fc_bias_grad: float32 [5120], P(('dp', 'ctx'))
- w_out_grad: float32 [5120, 1280], P(('dp', 'ctx'))
- out_bias_grad: float32 [1280], P(('dp', 'ctx'))
The draws below stay inside these ranges and needn't reach their ends.
Inputs may be any that keep to these rules, and one draw needn't show every extreme that they name: `lengths`: in each aligned block of 2 entries (the sequences of one data group) one entry, at a place drawn from the seed, equals 1024.
All inputs are finite; a program needn't handle non-finite values.
Results may differ from the reference program's by a relative error of at most 0.039.
Values may be sent and summed in bfloat16 or wider, within the bound.
No kernel may reach another device: no remote copies, remote signals or barrier semaphores. Data moves between devices by JAX's collectives and lax.ppermute only.
A program may use at most 320 MiB of HBM per device.

```python
import math
import jax
import jax.numpy as jnp
from jax import lax

D = 1280
HEADS = 20
HEAD_DIM = 64
FF = 5120
SEQ_GRP = 2
LEN = 1024
SEQS = 32


def draw_lengths(key, part):
    key = jax.random.fold_in(key, 7)
    first_key, second_key = jax.random.split(key)
    group_count = SEQS // SEQ_GRP
    drawn = jax.random.randint(first_key, (SEQS,), LEN // 4, LEN + 1)
    chosen = jax.random.randint(second_key, (group_count,), 0, SEQ_GRP)
    slot_place = jnp.arange(SEQS) % SEQ_GRP
    full_slot = slot_place == jnp.repeat(chosen, SEQ_GRP, total_repeat_length=SEQS)
    return jnp.where(full_slot, LEN, drawn).astype(jnp.int32)


def shard_levels(rng, dims, cuts, low, high):
    factor_of = 1.0
    for dim, shards_of in cuts:
        heights = jax.random.uniform(jax.random.fold_in(jax.random.fold_in(rng, 6), dim), (shards_of,), jnp.float32, low / len(cuts), high / len(cuts))
        factor_of = factor_of * jnp.repeat(jnp.exp(heights), dims[dim] // shards_of).reshape((-1,) + (1,) * (len(dims) - 1 - dim))
    return factor_of


def noise(rng, extent, width, limit, cuts=(), dtype=jnp.bfloat16):
    array = jax.random.normal(rng, extent, jnp.float32) * width
    if len(cuts) > 0:
        array = shard_levels(rng, extent, cuts, -0.22, 0.18) * array
    return jnp.clip(array, min=-limit, max=limit).astype(dtype)


def setup_inputs(seed: int = 0) -> dict:
    key_of = jax.random.split(jax.random.key(seed), 17)
    tokens = noise(key_of[0], (SEQS, LEN, D), 1.0, 6.0, ((0, 16), (1, 8)))
    lengths = draw_lengths(jax.random.fold_in(key_of[16], 71), 0)
    cotangent = noise(key_of[2], (SEQS, LEN, D), 1.0, 6.0, ((0, 16), (1, 8)))
    ln1_gain = jnp.clip(1.0 + 0.15 * jax.random.normal(key_of[3], (D,), jnp.float32), 0.25, 1.75).astype(jnp.bfloat16)
    ln1_bias = noise(key_of[4], (D,), 0.3, 1.75, ((0, 128),))
    w_qkv = noise(key_of[5], (D, 3 * D), D ** -0.5, 0.15625, ((0, 128),))
    q_bias = noise(key_of[6], (D,), 0.3, 1.75, ((0, 128),))
    v_bias = noise(key_of[7], (D,), 0.1, 0.625, ((0, 128),))
    w_proj = noise(key_of[8], (D, D), (D // 16) ** -0.5, 0.625, ((0, 128),))
    proj_bias = noise(key_of[9], (D,), 0.3, 1.75, ((0, 128),))
    ln2_gain = jnp.clip(1.0 + 0.15 * jax.random.normal(key_of[10], (D,), jnp.float32), 0.25, 1.75).astype(jnp.bfloat16)
    ln2_bias = noise(key_of[11], (D,), 0.3, 1.75, ((0, 128),))
    w_fc = noise(key_of[12], (D, FF), D ** -0.5, 0.15625, ((0, 128),))
    fc_bias = noise(key_of[13], (FF,), 0.3, 1.75, ((0, 128),))
    w_out = noise(key_of[14], (FF, D), FF ** -0.5, 0.078125, ((0, 128),))
    out_bias = noise(key_of[15], (D,), 0.3, 1.75, ((0, 128),))
    return dict(tokens=tokens, lengths=lengths, cotangent=cotangent, ln1_gain=ln1_gain, ln1_bias=ln1_bias, w_qkv=w_qkv, q_bias=q_bias, v_bias=v_bias, w_proj=w_proj, proj_bias=proj_bias, ln2_gain=ln2_gain, ln2_bias=ln2_bias, w_fc=w_fc, fc_bias=fc_bias, w_out=w_out, out_bias=out_bias)


@jax.custom_vjp
def low(v):
    return lax.optimization_barrier(v.astype(jnp.bfloat16)).astype(jnp.float32)

@jax.custom_vjp
def low_back(v):
    return v

def low_keep(v):
    return (low(v), None)

def low_pass(kept, grad):
    return (grad,)

def back_keep(v):
    return (v, None)

def back_low(kept, grad):
    return (low(grad),)
low.defvjp(low_keep, low_pass)
low_back.defvjp(back_keep, back_low)
NORM_EPS = 1e-05
PRECISE = lax.Precision.HIGHEST

def layer_norm(token_rows, gain, shift):
    centre = lax.optimization_barrier(jnp.mean(token_rows, axis=-1, keepdims=True))
    centred = token_rows - centre
    spread = lax.optimization_barrier(jnp.mean(centred * centred, axis=-1, keepdims=True))
    return centred * lax.rsqrt(spread + NORM_EPS) * gain + shift

def matmul(left, right):
    return jnp.dot(left, right, precision=PRECISE, preferred_element_type=jnp.float32)

def forward(token_rows, params, seq_length):
    gain_one, shift_one, qkv_weight, query_bias, value_bias, proj_weight, proj_shift, gain_two, shift_two, fc_weight, fc_shift, out_weight, out_shift = params
    row_count, model_width = token_rows.shape
    normed_one = low(layer_norm(token_rows, gain_one, shift_one))
    qkv = matmul(normed_one, qkv_weight)
    query_rows = low_back(low(qkv[:, :model_width] + query_bias))
    key_rows = low_back(low(qkv[:, model_width:2 * model_width]))
    value_rows = low_back(low(qkv[:, 2 * model_width:] + value_bias))
    query_heads = query_rows.reshape(row_count, HEADS, HEAD_DIM)
    key_heads = key_rows.reshape(row_count, HEADS, HEAD_DIM)
    value_heads = value_rows.reshape(row_count, HEADS, HEAD_DIM)
    scores = jnp.einsum('qhd,khd->hqk', query_heads, key_heads, precision=PRECISE) * (1.0 / math.sqrt(HEAD_DIM))
    scores = low_back(scores)
    positions = jnp.arange(row_count)
    allowed = (positions[None, :] <= positions[:, None]) & (positions[None, :] < seq_length)
    scores = jnp.where(allowed[None], scores, -1000000000.0)
    probs = low(jax.nn.softmax(scores, axis=-1))
    attended = jnp.einsum('hqk,khd->qhd', probs, value_heads, precision=PRECISE)
    attended = low_back(low(attended.reshape(row_count, model_width)))
    residual = low_back(token_rows + matmul(attended, proj_weight) + proj_shift)
    normed_two = low(layer_norm(residual, gain_two, shift_two))
    pre_act = low_back(matmul(normed_two, fc_weight) + fc_shift)
    active = low(jax.nn.gelu(pre_act, approximate=True))
    return residual + matmul(active, out_weight) + out_shift

def reference(tokens, lengths, cotangent, ln1_gain, ln1_bias, w_qkv, q_bias, v_bias, w_proj, proj_bias, ln2_gain, ln2_bias, w_fc, fc_bias, w_out, out_bias):
    params = tuple((item.astype(jnp.float32) for item in (ln1_gain, ln1_bias, w_qkv, q_bias, v_bias, w_proj, proj_bias, ln2_gain, ln2_bias, w_fc, fc_bias, w_out, out_bias)))
    positions = jnp.arange(LEN)

    def one_sequence(totals, item):
        token_rows, seq_length, back_rows = item

        def run_layer(rows_in, params_in):
            return forward(rows_in, params_in, seq_length)
        result, pullback = jax.vjp(run_layer, token_rows.astype(jnp.float32), params)
        keep_rows = (positions < seq_length).astype(jnp.float32)[:, None]
        grad_rows, grad_params = pullback(back_rows.astype(jnp.float32) * keep_rows)
        totals = jax.tree.map(lambda left, right: left + right, totals, grad_params)
        return (totals, (result.astype(jnp.bfloat16), grad_rows))
    zeros = jax.tree.map(jnp.zeros_like, params)
    totals, (outputs, input_grads) = lax.scan(one_sequence, zeros, (tokens, lengths, cotangent))
    return (outputs, input_grads, totals[0], totals[1], totals[2], totals[3], totals[4], totals[5], totals[6], totals[7], totals[8], totals[9], totals[10], totals[11], totals[12])
```

```python
import functools
import math

import jax
import jax.numpy as jnp
from jax import lax
from jax.experimental import pallas as pl
from jax.experimental.pallas import tpu as pltpu
from jax.sharding import Mesh
from jax.sharding import PartitionSpec as P

HEADS = 20
NORM_EPS = 1e-05
MASKED = -1000000000.0

F32 = jnp.float32
BF16 = jnp.bfloat16

AXES = ("x", "yl", "c", "z", "yh")
SIZES = (4, 2, 2, 4, 2)
DP = ("x", "yl", "c")
CTX = ("z", "yh")
PLACE = ("z", "yh", "yl", "x", "c")

D = 1280
SPAN = 128
SEQ_GRP = 2
ROWS = SEQ_GRP * SPAN
CTX_N = 8
LEN = CTX_N * SPAN
HEAD_DIM = D // HEADS
GROUP_HEADS = 5
GROUP_W = GROUP_HEADS * HEAD_DIM
COLS = 640
BLK = 80
SCALE = 1.0 / math.sqrt(HEAD_DIM)
Q_BLOCK = 256
MB = 1 << 20


def place_of(dp):
    x, yl, c = dp // 4, (dp // 2) % 2, dp % 2
    return (yl * 4 + x) * 2 + c


def dot(left, right):
    return lax.dot_general(
        left, right, (((1,), (0,)), ((), ())), preferred_element_type=F32
    )


def dot_nt(left, right):
    return lax.dot_general(
        left, right, (((1,), (1,)), ((), ())), preferred_element_type=F32
    )


def norm_stats(rows):
    centre = jnp.mean(rows, axis=-1, keepdims=True)
    centred = rows - centre
    spread = jnp.mean(centred * centred, axis=-1, keepdims=True)
    scale = lax.rsqrt(spread + NORM_EPS)
    return centred * scale, scale


def norm_back(normed, scale, gain, grad):
    scaled = gain * grad
    mean_one = jnp.mean(scaled, axis=-1, keepdims=True)
    mean_two = jnp.mean(scaled * normed, axis=-1, keepdims=True)
    return (scaled - mean_one - normed * mean_two) * scale


def stack_rows(ref, *lead):
    return jnp.concatenate([ref[(*lead, place_of(dp))] for dp in range(16)], axis=0)


def params(vmem_mb):
    return pltpu.CompilerParams(vmem_limit_bytes=vmem_mb * MB)


def cost(flops, nbytes, trans=0):
    return pl.CostEstimate(flops=flops, bytes_accessed=nbytes, transcendentals=trans)


def whole(shape):
    return pl.BlockSpec(shape, lambda *i: (0,) * len(shape))


def qkv_kernel(tok_ref, gain_ref, shift_ref, bias_ref, w_ref, n1_ref, out_ref):
    @pl.when(pl.program_id(0) == 0)
    def _():
        normed, _ = norm_stats(tok_ref[...].astype(F32))
        n1_ref[...] = (normed * gain_ref[...] + shift_ref[...]).astype(BF16)

    rows = dot(n1_ref[...], stack_rows(w_ref, 0)) + bias_ref[...]
    turned = rows.T.astype(BF16)
    for group in range(2):
        for seq in range(SEQ_GRP):
            out_ref[seq, group, 0] = turned[
                group * GROUP_W : (group + 1) * GROUP_W, seq * SPAN : (seq + 1) * SPAN
            ]


def qkv_call(tok, gain, shift, bias, w_attn):
    return pl.pallas_call(
        qkv_kernel,
        grid=(6,),
        in_specs=[
            whole((ROWS, D)),
            whole((1, D)),
            whole((1, D)),
            pl.BlockSpec((1, COLS), lambda i: (0, i)),
            pl.BlockSpec((1, 16, BLK, COLS), lambda i: (i, 0, 0, 0)),
        ],
        out_specs=[
            whole((ROWS, D)),
            pl.BlockSpec(
                (SEQ_GRP, 2, 1, GROUP_W, SPAN), lambda i: (0, i % 2, i // 2, 0, 0)
            ),
        ],
        out_shape=[
            jax.ShapeDtypeStruct((ROWS, D), BF16),
            jax.ShapeDtypeStruct((SEQ_GRP, 4, 3, GROUP_W, SPAN), BF16),
        ],
        compiler_params=params(32),
        cost_estimate=cost(2 * ROWS * D * 3 * D, 12 * MB),
        name="qkv",
    )(tok, gain, shift, bias, w_attn)


def lanes(ref, which):
    return jnp.concatenate([ref[p, which] for p in range(CTX_N)], axis=1)


def turn(block):
    return block.astype(F32).T.astype(BF16)


def allowed_of(length, first_query, key_count, query_count):
    key_pos = lax.broadcasted_iota(jnp.int32, (key_count, query_count), 0)
    query_pos = first_query + lax.broadcasted_iota(
        jnp.int32, (key_count, query_count), 1
    )
    return (key_pos <= query_pos) & (key_pos < length)


def attend_kernel(len_ref, qkv_ref, out_ref, lse_ref):
    length = len_ref[0]
    query = lanes(qkv_ref, 0)
    key = turn(lanes(qkv_ref, 1))
    value = lanes(qkv_ref, 2)
    for block in range(LEN // Q_BLOCK):
        first = block * Q_BLOCK
        last = first + Q_BLOCK
        scores = dot(key[:last], query[:, first:last]) * SCALE
        scores = jnp.where(allowed_of(length, first, last, Q_BLOCK), scores, MASKED)
        top = jnp.max(scores, axis=0, keepdims=True)
        weights = jnp.exp(scores - top)
        total = jnp.sum(weights, axis=0, keepdims=True)
        result = dot(value[:, :last], weights.astype(BF16)) / total
        lse_ref[0, :, first:last] = top + jnp.log(total)
        result = result.astype(BF16)
        for part in range(Q_BLOCK // SPAN):
            out_ref[first // SPAN + part] = result[:, part * SPAN : (part + 1) * SPAN]


def attend_call(length, qkv):
    return pl.pallas_call(
        attend_kernel,
        grid=(GROUP_HEADS,),
        in_specs=[
            pl.BlockSpec(memory_space=pltpu.SMEM),
            pl.BlockSpec((CTX_N, 3, HEAD_DIM, SPAN), lambda h: (0, 0, h, 0)),
        ],
        out_specs=[
            pl.BlockSpec((CTX_N, HEAD_DIM, SPAN), lambda h: (0, h, 0)),
            pl.BlockSpec((1, 1, LEN), lambda h: (h, 0, 0)),
        ],
        out_shape=[
            jax.ShapeDtypeStruct((CTX_N, GROUP_W, SPAN), BF16),
            jax.ShapeDtypeStruct((GROUP_HEADS, 1, LEN), F32),
        ],
        compiler_params=params(40),
        cost_estimate=cost(6 * LEN * LEN * 4 * HEAD_DIM, 3 * MB, 3 * LEN * LEN),
        name="attend",
    )(length, qkv)


def attend_back_kernel(len_ref, qkv_ref, grad_ref, lse_ref, out_ref, gk_ref, gv_ref):
    length = len_ref[0]
    query = lanes(qkv_ref, 0)
    key_t = lanes(qkv_ref, 1)
    key = turn(key_t)
    value = turn(lanes(qkv_ref, 2))
    grad = jnp.concatenate([grad_ref[p] for p in range(CTX_N)], axis=1)
    gk_ref[...] = jnp.zeros_like(gk_ref)
    gv_ref[...] = jnp.zeros_like(gv_ref)
    for block in range(LEN // Q_BLOCK):
        first = block * Q_BLOCK
        last = first + Q_BLOCK
        query_b = query[:, first:last]
        grad_b = grad[:, first:last]
        scores = dot(key[:last], query_b) * SCALE
        probs = jnp.where(
            allowed_of(length, first, last, Q_BLOCK),
            jnp.exp(scores - lse_ref[0, :, first:last]),
            0.0,
        )
        grad_probs = dot(value[:last], grad_b)
        delta = jnp.sum(probs * grad_probs, axis=0, keepdims=True)
        grad_scores = (probs * (grad_probs - delta)).astype(BF16)
        grad_query = (dot(key_t[:, :last], grad_scores) * SCALE).astype(BF16)
        for part in range(Q_BLOCK // SPAN):
            out_ref[first // SPAN + part, 0] = grad_query[
                :, part * SPAN : (part + 1) * SPAN
            ]
        gk_ref[:, :last] += dot_nt(query_b, grad_scores)
        gv_ref[:, :last] += dot_nt(grad_b, probs.astype(BF16))
    for part in range(CTX_N):
        cut = slice(part * SPAN, (part + 1) * SPAN)
        out_ref[part, 1] = (gk_ref[:, cut] * SCALE).astype(BF16)
        out_ref[part, 2] = gv_ref[:, cut].astype(BF16)


def attend_back_call(length, qkv, grad, lse):
    return pl.pallas_call(
        attend_back_kernel,
        grid=(GROUP_HEADS,),
        in_specs=[
            pl.BlockSpec(memory_space=pltpu.SMEM),
            pl.BlockSpec((CTX_N, 3, HEAD_DIM, SPAN), lambda h: (0, 0, h, 0)),
            pl.BlockSpec((CTX_N, HEAD_DIM, SPAN), lambda h: (0, h, 0)),
            pl.BlockSpec((1, 1, LEN), lambda h: (h, 0, 0)),
        ],
        out_specs=pl.BlockSpec((CTX_N, 3, HEAD_DIM, SPAN), lambda h: (0, 0, h, 0)),
        out_shape=jax.ShapeDtypeStruct((CTX_N, 3, GROUP_W, SPAN), BF16),
        scratch_shapes=[pltpu.VMEM((HEAD_DIM, LEN), F32)] * 2,
        compiler_params=params(48),
        cost_estimate=cost(15 * LEN * LEN * 4 * HEAD_DIM, 5 * MB, 3 * LEN * LEN),
        name="attend_back",
    )(length, qkv, grad, lse)


def mlp_kernel(
    info_ref,
    tok_ref,
    cot_ref,
    att_ref,
    vec_ref,
    fc_bias_ref,
    wp_ref,
    wf_ref,
    wo_ref,
    out_ref,
    g_res_ref,
    g_att_ref,
    d_vec_ref,
    d_fc_bias_ref,
    d_wp_ref,
    d_wf_ref,
    d_wo_ref,
    res_ref,
    n2_ref,
    n2t_ref,
    g_out_ref,
    acc_ref,
    gn_ref,
):
    step = pl.program_id(0)
    proj_shift, gain, shift, out_shift = (vec_ref[k : k + 1] for k in range(4))

    @pl.when(step == 0)
    def _():
        att = jnp.concatenate([turn(att_ref[s]) for s in range(SEQ_GRP)], axis=0)
        for half in range(2):
            cut = slice(half * COLS, (half + 1) * COLS)
            res_ref[:, cut] = (
                tok_ref[:, cut].astype(F32)
                + dot(att, stack_rows(wp_ref, half))
                + proj_shift[:, cut]
            )
        residual = res_ref[...]
        normed, _ = norm_stats(residual)
        normed = normed * gain + shift
        n2_ref[...] = normed.astype(BF16)
        n2t_ref[...] = normed.T.astype(BF16)
        for seq in range(SEQ_GRP):
            cut = slice(seq * SPAN, (seq + 1) * SPAN)
            pos = info_ref[SEQ_GRP] + lax.broadcasted_iota(jnp.int32, (SPAN, D), 0)
            g_out_ref[cut] = jnp.where(
                pos < info_ref[seq], cot_ref[cut], jnp.zeros((SPAN, D), BF16)
            )
        acc_ref[...] = residual + out_shift
        gn_ref[...] = jnp.zeros_like(gn_ref)

    w_fc = stack_rows(wf_ref, 0)
    pre = dot(n2_ref[...], w_fc) + fc_bias_ref[...]
    root = math.sqrt(2.0 / math.pi)
    square = pre * pre
    bend = jnp.tanh(root * pre * (1.0 + 0.044715 * square))
    gate = 0.5 * (1.0 + bend)
    slope = gate + 0.5 * pre * (1.0 - bend * bend) * root * (
        1.0 + 3.0 * 0.044715 * square
    )
    act_f = pre * gate
    act = act_f.astype(BF16)
    act_t = act_f.T.astype(BF16)
    g_act = None
    for half in range(2):
        cut = slice(half * COLS, (half + 1) * COLS)
        w_out = jnp.concatenate(
            [wo_ref[z, half, 0, 0, c] for c in range(2) for z in range(4)], axis=0
        )
        acc_ref[:, cut] += dot(act, w_out)
        part = dot_nt(g_out_ref[:, cut], w_out)
        g_act = part if g_act is None else g_act + part
        d_w = dot(act_t, g_out_ref[:, cut]).astype(BF16)
        for c in range(2):
            for z in range(4):
                row = (c * 4 + z) * BLK
                d_wo_ref[c, z, half, 0, 0] = d_w[row : row + BLK]
    g_pre_f = g_act * slope
    g_pre = g_pre_f.astype(BF16)
    d_fc_bias_ref[...] = jnp.sum(g_pre.astype(F32), axis=0, keepdims=True)
    gn_ref[...] += dot_nt(g_pre, w_fc)
    d_w = dot(n2t_ref[...], g_pre).astype(BF16)
    for dp in range(16):
        d_wf_ref[dp % 2, 0, place_of(dp) // 2] = d_w[dp * BLK : (dp + 1) * BLK]

    @pl.when(step == pl.num_programs(0) - 1)
    def _():
        out_ref[...] = acc_ref[...].astype(BF16)
        normed, scale = norm_stats(res_ref[...])
        g_norm = gn_ref[...]
        g_out = g_out_ref[...].astype(F32)
        g_res = (g_out + norm_back(normed, scale, gain, g_norm)).astype(BF16)
        g_res_ref[...] = g_res
        d_vec_ref[0:1] = jnp.sum(g_res.astype(F32), axis=0, keepdims=True)
        d_vec_ref[1:2] = jnp.sum(g_norm * normed, axis=0, keepdims=True)
        d_vec_ref[2:3] = jnp.sum(g_norm, axis=0, keepdims=True)
        d_vec_ref[3:4] = jnp.sum(g_out, axis=0, keepdims=True)
        g_att = None
        for half in range(2):
            cut = slice(half * COLS, (half + 1) * COLS)
            part = dot_nt(g_res[:, cut], stack_rows(wp_ref, half))
            g_att = part if g_att is None else g_att + part
            d_w = None
            for seq in range(SEQ_GRP):
                part = dot(
                    att_ref[seq], g_res_ref[seq * SPAN : (seq + 1) * SPAN, cut]
                )
                d_w = part if d_w is None else d_w + part
            d_w = d_w.astype(BF16)
            for dp in range(16):
                d_wp_ref[dp % 2, half, place_of(dp) // 2] = d_w[
                    dp * BLK : (dp + 1) * BLK
                ]
        for seq in range(SEQ_GRP):
            g_att_ref[seq] = g_att[seq * SPAN : (seq + 1) * SPAN].T.astype(BF16)


def mlp_call(info, tok, cot, att, vecs, fc_bias, w_attn, w_mlp):
    w_mlp_parts = w_mlp.reshape(4, 2, 2, 4, 2, 2 * BLK, COLS)
    return pl.pallas_call(
        mlp_kernel,
        grid=(8,),
        in_specs=[
            pl.BlockSpec(memory_space=pltpu.SMEM),
            whole((ROWS, D)),
            whole((ROWS, D)),
            whole((SEQ_GRP, D, SPAN)),
            whole((4, D)),
            pl.BlockSpec((1, COLS), lambda j: (0, j)),
            pl.BlockSpec((2, 16, BLK, COLS), lambda j: (3, 0, 0, 0)),
            pl.BlockSpec((1, 16, BLK, COLS), lambda j: (j, 0, 0, 0)),
            pl.BlockSpec(
                (4, 2, 1, 1, 2, BLK, COLS), lambda j: (0, 0, j % 2, j // 2, 0, 1, 0)
            ),
        ],
        out_specs=[
            whole((ROWS, D)),
            whole((ROWS, D)),
            whole((SEQ_GRP, D, SPAN)),
            whole((4, D)),
            pl.BlockSpec((1, COLS), lambda j: (0, j)),
            whole((2, 2, 8, BLK, COLS)),
            pl.BlockSpec((2, 1, 8, BLK, COLS), lambda j: (0, j, 0, 0, 0)),
            pl.BlockSpec(
                (2, 4, 2, 1, 1, BLK, COLS), lambda j: (0, 0, 0, j % 2, j // 2, 0, 0)
            ),
        ],
        out_shape=[
            jax.ShapeDtypeStruct((ROWS, D), BF16),
            jax.ShapeDtypeStruct((ROWS, D), BF16),
            jax.ShapeDtypeStruct((SEQ_GRP, D, SPAN), BF16),
            jax.ShapeDtypeStruct((4, D), F32),
            jax.ShapeDtypeStruct((1, 4 * D), F32),
            jax.ShapeDtypeStruct((2, 2, 8, BLK, COLS), BF16),
            jax.ShapeDtypeStruct((2, 8, 8, BLK, COLS), BF16),
            jax.ShapeDtypeStruct((2, 4, 2, 2, 4, BLK, COLS), BF16),
        ],
        scratch_shapes=[
            pltpu.VMEM((ROWS, D), F32),
            pltpu.VMEM((ROWS, D), BF16),
            pltpu.VMEM((D, ROWS), BF16),
            pltpu.VMEM((ROWS, D), BF16),
            pltpu.VMEM((ROWS, D), F32),
            pltpu.VMEM((ROWS, D), F32),
        ],
        compiler_params=params(56),
        cost_estimate=cost(2 * ROWS * D * (24 * D + 3 * D), 62 * MB, 2 * ROWS * 4 * D),
        name="mlp",
    )(info, tok, cot, att, vecs, fc_bias, w_attn, w_mlp, w_mlp_parts)


def qkv_back_kernel(
    tok_ref,
    n1_ref,
    gain_ref,
    g_res_ref,
    g_ref,
    w_ref,
    in_grad_ref,
    d_bias_ref,
    d_norm_ref,
    d_w_ref,
    n1t_ref,
    gn_ref,
):
    step = pl.program_id(0)

    @pl.when(step == 0)
    def _():
        n1t_ref[...] = turn(n1_ref[...])
        gn_ref[...] = jnp.zeros_like(gn_ref)

    turned = jnp.concatenate(
        [
            jnp.concatenate([g_ref[s, group, 0] for s in range(SEQ_GRP)], axis=1)
            for group in range(2)
        ],
        axis=0,
    )
    rows_f = turned.astype(F32).T
    rows = rows_f.astype(BF16)
    d_bias_ref[...] = jnp.sum(rows_f, axis=0, keepdims=True)
    gn_ref[...] += dot_nt(rows, stack_rows(w_ref, 0))
    d_w = dot(n1t_ref[...], rows).astype(BF16)
    for dp in range(16):
        d_w_ref[dp % 2, 0, place_of(dp) // 2] = d_w[dp * BLK : (dp + 1) * BLK]

    @pl.when(step == pl.num_programs(0) - 1)
    def _():
        normed, scale = norm_stats(tok_ref[...].astype(F32))
        g_norm = gn_ref[...]
        in_grad_ref[...] = g_res_ref[...].astype(F32) + norm_back(
            normed, scale, gain_ref[...], g_norm
        )
        d_norm_ref[0:1] = jnp.sum(g_norm * normed, axis=0, keepdims=True)
        d_norm_ref[1:2] = jnp.sum(g_norm, axis=0, keepdims=True)


def qkv_back_call(tok, n1, gain, g_res, g_qkv, w_attn):
    return pl.pallas_call(
        qkv_back_kernel,
        grid=(6,),
        in_specs=[
            whole((ROWS, D)),
            whole((ROWS, D)),
            whole((1, D)),
            whole((ROWS, D)),
            pl.BlockSpec(
                (SEQ_GRP, 2, 1, GROUP_W, SPAN), lambda i: (0, i % 2, i // 2, 0, 0)
            ),
            pl.BlockSpec((1, 16, BLK, COLS), lambda i: (i, 0, 0, 0)),
        ],
        out_specs=[
            whole((ROWS, D)),
            pl.BlockSpec((1, COLS), lambda i: (0, i)),
            whole((2, D)),
            pl.BlockSpec((2, 1, 8, BLK, COLS), lambda i: (0, i, 0, 0, 0)),
        ],
        out_shape=[
            jax.ShapeDtypeStruct((ROWS, D), F32),
            jax.ShapeDtypeStruct((1, 3 * D), F32),
            jax.ShapeDtypeStruct((2, D), F32),
            jax.ShapeDtypeStruct((2, 6, 8, BLK, COLS), BF16),
        ],
        scratch_shapes=[
            pltpu.VMEM((D, ROWS), BF16),
            pltpu.VMEM((ROWS, D), F32),
        ],
        compiler_params=params(48),
        cost_estimate=cost(4 * ROWS * D * 3 * D, 24 * MB),
        name="qkv_back",
    )(tok, n1, gain, g_res, g_qkv, w_attn)


def ring_perm(axis):
    pairs = []
    for core in range(2):
        for pos in range(4):
            to = (pos + (1 if core == 0 else -1)) % 4
            if axis == "x":
                index = lambda p: p * 2 + core
            elif axis == "z":
                index = lambda p: core * 4 + p
            else:
                index = lambda p: ((p % 2) * 2 + core) * 2 + p // 2
            pairs.append((index(pos), index(to)))
    return {"x": ("x", "c"), "z": ("c", "z"), "y": ("yl", "c", "yh")}[axis], pairs


def swap_cores(array):
    return lax.ppermute(array, "c", [(0, 1), (1, 0)])


def reduce_scatter(grads, orders):
    core = lax.axis_index("c")
    way = 1 - 2 * core
    place = {
        "x": lax.axis_index("x"),
        "y": 2 * lax.axis_index("yh") + lax.axis_index("yl"),
        "z": lax.axis_index("z"),
    }
    dims = {"z": 0, "y": 1, "x": 2}
    theirs = [lax.dynamic_index_in_dim(g, 1 - core, 0, False) for g in grads]
    mine = [lax.dynamic_index_in_dim(g, core, 0, False) for g in grads]
    terms = [[m, swap_cores(t)] for m, t in zip(mine, theirs)]

    def local(colour, axis, block):
        total = None
        for term in terms[colour]:
            part = lax.dynamic_slice_in_dim(term, block, 1, dims[axis]).astype(F32)
            total = part if total is None else total + part
        return total

    for phase in range(3):
        axes = [order[phase] for order in orders]
        sent = [
            local(k, a, (place[a] - way) % 4).astype(BF16) for k, a in enumerate(axes)
        ]
        for step in range(3):
            for k, a in enumerate(axes):
                names, pairs = ring_perm(a)
                sent[k] = lax.ppermute(sent[k], names, pairs)
            for k, a in enumerate(axes):
                total = sent[k].astype(F32) + local(k, a, (place[a] - way * (2 + step)) % 4)
                sent[k] = total if phase == 2 and step == 2 else total.astype(BF16)
        terms = [[s] for s in sent]
    return [s.reshape(s.shape[-2:]) for s in sent]


def per_device(
    tokens,
    lengths,
    cotangent,
    ln1_gain,
    ln1_bias,
    w_qkv,
    q_bias,
    v_bias,
    w_proj,
    proj_bias,
    ln2_gain,
    ln2_bias,
    w_fc,
    fc_bias,
    w_out,
    out_bias,
):
    ctx_rank = lax.axis_index(CTX)
    tok = tokens.reshape(ROWS, D)
    cot = cotangent.reshape(ROWS, D)

    w_cols = jnp.stack([jnp.concatenate([w_qkv, w_proj], axis=1), w_fc], axis=0)
    w_cols = w_cols.reshape(2, 10, CTX_N, COLS).transpose(2, 0, 1, 3)
    w_cols = lax.all_to_all(w_cols, CTX, 0, 0, tiled=True)
    w_cols = w_cols.transpose(1, 0, 2, 3).reshape(2, BLK, COLS)
    w_rows = w_out.reshape(40, 2, COLS).transpose(1, 0, 2)
    w_rows = lax.all_to_all(w_rows, "yh", 0, 0, tiled=True).reshape(BLK, COLS)

    small = jnp.concatenate(
        [ln1_gain, ln1_bias, q_bias, v_bias, proj_bias, ln2_gain, ln2_bias, out_bias, fc_bias]
    )
    small = jnp.pad(small[None], ((0, 7), (0, COLS - 120)))
    attn_part = jnp.concatenate([w_cols[0], small], axis=0)
    mlp_part = jnp.concatenate([w_cols[1], w_rows], axis=0)
    w_attn = lax.all_gather(attn_part, PLACE, axis=0, tiled=False)
    mlp_part, w_attn = lax.optimization_barrier((mlp_part, w_attn))
    w_mlp = lax.all_gather(mlp_part, PLACE, axis=0, tiled=False)
    vecs = w_attn[:, BLK, :120].reshape(4, 2, 2, 4, 2, 120)
    vecs = vecs.transpose(3, 2, 4, 0, 1, 5).reshape(128, 120).astype(F32)
    fc_shift = vecs[:, 80:].reshape(1, 4 * D)
    vecs = vecs[:, :80].reshape(128, 8, 10).transpose(1, 0, 2).reshape(8, D)
    w_attn = w_attn.reshape(CTX_N, 16, BLK + 8, COLS)
    w_mlp = w_mlp.reshape(CTX_N, 16, 2 * BLK, COLS)

    qkv_bias = jnp.concatenate([vecs[2:3], jnp.zeros((1, D), F32), vecs[3:4]], axis=1)
    n1, qkv = qkv_call(tok, vecs[0:1], vecs[1:2], qkv_bias, w_attn)

    def exchange(array):
        return lax.all_to_all(array, CTX, 0, 0, tiled=True)

    length = lax.dynamic_slice_in_dim(lengths, ctx_rank // 4, 1)
    qkv = exchange(qkv.reshape(CTX_N, 3, GROUP_W, SPAN))
    att, lse = attend_call(length, qkv)
    att = exchange(att).reshape(SEQ_GRP, D, SPAN)

    info = jnp.concatenate([lengths, (ctx_rank * SPAN).astype(jnp.int32)[None]])
    layer_out, g_res, g_att, d_vecs, d_fc_bias, d_wp, d_wf, d_wo = mlp_call(
        info, tok, cot, att, vecs[4:8], fc_shift, w_attn, w_mlp
    )
    mlp_sums = reduce_scatter(
        [d_wf.reshape(2, 4, 4, 4, BLK, COLS), d_wo.reshape(2, 4, 4, 4, BLK, COLS)],
        ["xyz", "yzx"],
    )

    g_att = exchange(g_att.reshape(CTX_N, GROUP_W, SPAN))
    g_qkv = attend_back_call(length, qkv, g_att, lse)
    g_qkv = exchange(g_qkv).reshape(SEQ_GRP, 4, 3, GROUP_W, SPAN)
    input_grad, d_qkv_bias, d_norm, d_wqkv = qkv_back_call(
        tok, n1, vecs[0:1], g_res, g_qkv, w_attn
    )

    d_small = jnp.concatenate(
        [d_norm, d_qkv_bias[:, :D], d_qkv_bias[:, 2 * D :], d_vecs], axis=0
    )
    d_small = d_small.reshape(8, 128, 10).transpose(1, 0, 2).reshape(128, 80)
    d_small = jnp.concatenate([d_small, d_fc_bias.reshape(128, 40)], axis=1)
    d_small = d_small.reshape(4, 2, 2, 4, 2, 120).transpose(2, 3, 4, 1, 0, 5)
    d_small = jnp.pad(
        d_small.reshape(2, CTX_N, 8, 1, 120).astype(BF16),
        ((0, 0), (0, 0), (0, 0), (0, 7), (0, COLS - 120)),
    )
    d_attn = jnp.concatenate([d_wqkv, d_wp], axis=1)
    d_attn = jnp.concatenate([d_attn, d_small], axis=3)
    d_attn = d_attn.reshape(2, 4, 4, 4, BLK + 8, COLS)
    attn_sums = reduce_scatter(
        [d_attn[..., 0:32, :], d_attn[..., 32:64, :], d_attn[..., 64:88, :]],
        ["xyz", "yzx", "zxy"],
    )
    attn_sum = jnp.concatenate(attn_sums, axis=0)

    back = jnp.stack([attn_sum[:BLK], mlp_sums[0]], axis=0).astype(BF16)
    back = back.reshape(2, CTX_N, 10, COLS).transpose(1, 0, 2, 3)
    back = lax.all_to_all(back, CTX, 0, 0, tiled=True)
    back = back.transpose(1, 2, 0, 3).reshape(2, 10, CTX_N * COLS).astype(F32)
    d_w_out = mlp_sums[1].astype(BF16).reshape(2, 40, COLS)
    d_w_out = lax.all_to_all(d_w_out, "yh", 0, 0, tiled=True)
    d_w_out = d_w_out.transpose(1, 0, 2).reshape(40, D).astype(F32)
    small_sum = attn_sum[BLK, :120]
    names = ["g1", "b1", "q", "v", "proj", "g2", "b2", "out"]
    vec = {n: small_sum[10 * k : 10 * (k + 1)] for k, n in enumerate(names)}

    return (
        layer_out.reshape(tokens.shape),
        input_grad.reshape(tokens.shape),
        vec["g1"],
        vec["b1"],
        back[0, :, : 3 * D],
        vec["q"],
        vec["v"],
        back[0, :, 3 * D :],
        vec["proj"],
        vec["g2"],
        vec["b2"],
        back[1],
        small_sum[80:120],
        d_w_out,
        vec["out"],
    )


def solution(mesh):
    fine = Mesh(mesh.devices.reshape(SIZES), AXES)
    rows = P(DP, CTX, None)
    mat = P(AXES, None)
    vec = P(AXES)
    in_specs = (
        rows,
        P(DP),
        rows,
        vec,
        vec,
        mat,
        vec,
        vec,
        mat,
        vec,
        vec,
        vec,
        mat,
        vec,
        mat,
        vec,
    )
    out_specs = (
        rows,
        rows,
        vec,
        vec,
        mat,
        vec,
        vec,
        mat,
        vec,
        vec,
        vec,
        mat,
        vec,
        mat,
        vec,
    )
    return jax.shard_map(
        per_device, mesh=fine, in_specs=in_specs, out_specs=out_specs, check_vma=False
    )
```

```python
import functools
import math

import jax
import jax.numpy as jnp
from jax import lax
from jax.experimental import pallas as pl
from jax.experimental.pallas import tpu as pltpu
from jax.sharding import Mesh
from jax.sharding import PartitionSpec as P

HEADS = 20
NORM_EPS = 1e-05
MASKED = -1000000000.0

F32 = jnp.float32
BF16 = jnp.bfloat16

AXES = ("x", "yl", "c", "z", "yh")
SIZES = (4, 2, 2, 4, 2)
DP = ("x", "yl", "c")
CTX = ("z", "yh")
PLACE = ("z", "yh", "yl", "x", "c")

D = 1280
SPAN = 128
SEQ_GRP = 2
ROWS = SEQ_GRP * SPAN
CTX_N = 8
LEN = CTX_N * SPAN
HEAD_DIM = D // HEADS
GROUP_HEADS = 5
GROUP_W = GROUP_HEADS * HEAD_DIM
COLS = 640
BLK = 80
SCALE = 1.0 / math.sqrt(HEAD_DIM)
Q_BLOCK = 256
HEADS_W = 3 * GROUP_W
PIECE = 32
MB = 1 << 20


def place_of(dp):
    x, yl, c = dp // 4, (dp // 2) % 2, dp % 2
    return (yl * 4 + x) * 2 + c


def dot(left, right):
    return lax.dot_general(
        left, right, (((1,), (0,)), ((), ())), preferred_element_type=F32
    )


def dot_nt(left, right):
    return lax.dot_general(
        left, right, (((1,), (1,)), ((), ())), preferred_element_type=F32
    )


def norm_stats(rows):
    centre = jnp.mean(rows, axis=-1, keepdims=True)
    centred = rows - centre
    spread = jnp.mean(centred * centred, axis=-1, keepdims=True)
    scale = lax.rsqrt(spread + NORM_EPS)
    return centred * scale, scale


def norm_back(normed, scale, gain, grad):
    scaled = gain * grad
    mean_one = jnp.mean(scaled, axis=-1, keepdims=True)
    mean_two = jnp.mean(scaled * normed, axis=-1, keepdims=True)
    return (scaled - mean_one - normed * mean_two) * scale


def stack_rows(ref, *lead):
    return jnp.concatenate([ref[(*lead, place_of(dp))] for dp in range(16)], axis=0)


def params(vmem_mb):
    return pltpu.CompilerParams(vmem_limit_bytes=vmem_mb * MB)


def cost(flops, nbytes, trans=0):
    return pl.CostEstimate(flops=flops, bytes_accessed=nbytes, transcendentals=trans)


def whole(shape):
    return pl.BlockSpec(shape, lambda *i: (0,) * len(shape))


def turn(block):
    return block.astype(F32).T.astype(BF16)


def allowed_of(length, first_query, key_count, query_count):
    key_pos = lax.broadcasted_iota(jnp.int32, (key_count, query_count), 0)
    query_pos = first_query + lax.broadcasted_iota(
        jnp.int32, (key_count, query_count), 1
    )
    return (key_pos <= query_pos) & (key_pos < length)


def attend_kernel(
    len_ref, tok_ref, norm_ref, bias_ref, w_ref, qkv_ref, out_ref, lse_ref
):
    head = pl.program_id(0)

    @pl.when(head == 0)
    def _():
        weight = w_ref[...].reshape(D, HEADS_W)
        for block in range(LEN // Q_BLOCK):
            cut = slice(block * Q_BLOCK, (block + 1) * Q_BLOCK)
            normed, _ = norm_stats(tok_ref[cut].astype(F32))
            normed = (normed * norm_ref[0:1] + norm_ref[1:2]).astype(BF16)
            turned = (dot(normed, weight) + bias_ref[...]).T.astype(BF16)
            for row in range(3 * GROUP_HEADS):
                qkv_ref[row // GROUP_HEADS, row % GROUP_HEADS, :, cut] = turned[
                    row * HEAD_DIM : (row + 1) * HEAD_DIM
                ]

    length = len_ref[0]
    query = qkv_ref[0, head]
    key = turn(qkv_ref[1, head])
    value = qkv_ref[2, head]
    for block in range(LEN // Q_BLOCK):
        first = block * Q_BLOCK
        last = first + Q_BLOCK
        scores = dot(key[:last], query[:, first:last]) * SCALE
        scores = jnp.where(allowed_of(length, first, last, Q_BLOCK), scores, MASKED)
        top = jnp.max(scores, axis=0, keepdims=True)
        weights = jnp.exp(scores - top)
        total = jnp.sum(weights, axis=0, keepdims=True)
        result = dot(value[:, :last], weights.astype(BF16)) / total
        lse_ref[0, :, first:last] = top + jnp.log(total)
        result = result.astype(BF16)
        for part in range(Q_BLOCK // SPAN):
            out_ref[first // SPAN + part] = result[:, part * SPAN : (part + 1) * SPAN]


def attend_call(length, tok, norm, bias, w_qkv):
    return pl.pallas_call(
        attend_kernel,
        grid=(GROUP_HEADS,),
        in_specs=[
            pl.BlockSpec(memory_space=pltpu.SMEM),
            whole((LEN, D)),
            whole((2, D)),
            whole((1, HEADS_W)),
            whole((16, BLK, HEADS_W)),
        ],
        out_specs=[
            whole((3, GROUP_HEADS, HEAD_DIM, LEN)),
            pl.BlockSpec((CTX_N, HEAD_DIM, SPAN), lambda h: (0, h, 0)),
            pl.BlockSpec((1, 1, LEN), lambda h: (h, 0, 0)),
        ],
        out_shape=[
            jax.ShapeDtypeStruct((3, GROUP_HEADS, HEAD_DIM, LEN), BF16),
            jax.ShapeDtypeStruct((CTX_N, GROUP_W, SPAN), BF16),
            jax.ShapeDtypeStruct((GROUP_HEADS, 1, LEN), F32),
        ],
        compiler_params=params(56),
        cost_estimate=cost(
            6 * LEN * LEN * 4 * HEAD_DIM + 2 * LEN * D * HEADS_W, 8 * MB, 3 * LEN * LEN
        ),
        name="attend",
    )(length, tok, norm, bias, w_qkv)


def attend_back_kernel(
    len_ref,
    tok_ref,
    norm_ref,
    w_ref,
    qkv_ref,
    grad_ref,
    lse_ref,
    d_w_ref,
    d_bias_ref,
    g_norm_ref,
    g_ref,
    gk_ref,
    gv_ref,
    n1t_ref,
):
    head = pl.program_id(0)

    @pl.when(head == 0)
    def _():
        for block in range(LEN // Q_BLOCK):
            cut = slice(block * Q_BLOCK, (block + 1) * Q_BLOCK)
            normed, _ = norm_stats(tok_ref[cut].astype(F32))
            normed = normed * norm_ref[0:1] + norm_ref[1:2]
            n1t_ref[:, cut] = normed.T.astype(BF16)

    length = len_ref[0]
    query = qkv_ref[0, head]
    key_t = qkv_ref[1, head]
    key = turn(key_t)
    value = turn(qkv_ref[2, head])
    grad = jnp.concatenate([grad_ref[p] for p in range(CTX_N)], axis=1)
    gk_ref[...] = jnp.zeros_like(gk_ref)
    gv_ref[...] = jnp.zeros_like(gv_ref)
    for block in range(LEN // Q_BLOCK):
        first = block * Q_BLOCK
        last = first + Q_BLOCK
        query_b = query[:, first:last]
        grad_b = grad[:, first:last]
        scores = dot(key[:last], query_b) * SCALE
        probs = jnp.where(
            allowed_of(length, first, last, Q_BLOCK),
            jnp.exp(scores - lse_ref[0, :, first:last]),
            0.0,
        )
        grad_probs = dot(value[:last], grad_b)
        delta = jnp.sum(probs * grad_probs, axis=0, keepdims=True)
        grad_scores = (probs * (grad_probs - delta)).astype(BF16)
        g_ref[0, head, :, first:last] = (
            dot(key_t[:, :last], grad_scores) * SCALE
        ).astype(BF16)
        gk_ref[:, :last] += dot_nt(query_b, grad_scores)
        gv_ref[:, :last] += dot_nt(grad_b, probs.astype(BF16))
    g_ref[1, head] = (gk_ref[...] * SCALE).astype(BF16)
    g_ref[2, head] = gv_ref[...].astype(BF16)

    @pl.when(head == GROUP_HEADS - 1)
    def _():
        grads = g_ref[...].reshape(HEADS_W, LEN)
        d_bias_ref[...] = dot_nt(jnp.ones((8, LEN), BF16), grads)
        for part in range(4):
            rows = 4 * BLK
            d_w = dot_nt(n1t_ref[part * rows : (part + 1) * rows], grads)
            d_w_ref[part * 4 : (part + 1) * 4] = d_w.astype(BF16).reshape(
                4, BLK, HEADS_W
            )
        weight = w_ref[...].reshape(D, HEADS_W)
        for block in range(LEN // Q_BLOCK):
            cut = slice(block * Q_BLOCK, (block + 1) * Q_BLOCK)
            g_norm = dot_nt(turn(grads[:, cut]), weight).astype(BF16)
            for part in range(Q_BLOCK // SPAN):
                g_norm_ref[block * (Q_BLOCK // SPAN) + part] = g_norm[
                    part * SPAN : (part + 1) * SPAN
                ]


def attend_back_call(length, tok, norm, w_qkv, qkv, grad, lse):
    return pl.pallas_call(
        attend_back_kernel,
        grid=(GROUP_HEADS,),
        in_specs=[
            pl.BlockSpec(memory_space=pltpu.SMEM),
            whole((LEN, D)),
            whole((2, D)),
            whole((16, BLK, HEADS_W)),
            whole((3, GROUP_HEADS, HEAD_DIM, LEN)),
            pl.BlockSpec((CTX_N, HEAD_DIM, SPAN), lambda h: (0, h, 0)),
            pl.BlockSpec((1, 1, LEN), lambda h: (h, 0, 0)),
        ],
        out_specs=[
            whole((16, BLK, HEADS_W)),
            whole((8, HEADS_W)),
            whole((CTX_N, SPAN, D)),
        ],
        out_shape=[
            jax.ShapeDtypeStruct((16, BLK, HEADS_W), BF16),
            jax.ShapeDtypeStruct((8, HEADS_W), F32),
            jax.ShapeDtypeStruct((CTX_N, SPAN, D), BF16),
        ],
        scratch_shapes=[
            pltpu.VMEM((3, GROUP_HEADS, HEAD_DIM, LEN), BF16),
            pltpu.VMEM((HEAD_DIM, LEN), F32),
            pltpu.VMEM((HEAD_DIM, LEN), F32),
            pltpu.VMEM((D, LEN), BF16),
        ],
        compiler_params=params(56),
        cost_estimate=cost(
            15 * LEN * LEN * 4 * HEAD_DIM + 4 * LEN * D * HEADS_W,
            16 * MB,
            3 * LEN * LEN,
        ),
        name="attend_back",
    )(length, tok, norm, w_qkv, qkv, grad, lse)


def norm_back_kernel(
    tok_ref, gain_ref, g_res_ref, part_ref, in_grad_ref, d_norm_ref
):
    for seq in range(SEQ_GRP):
        cut = slice(seq * SPAN, (seq + 1) * SPAN)
        normed, scale = norm_stats(tok_ref[cut].astype(F32))
        g_norm = part_ref[4 * seq].astype(F32)
        for group in range(1, 4):
            g_norm = g_norm + part_ref[4 * seq + group].astype(F32)
        in_grad_ref[cut] = g_res_ref[cut].astype(F32) + norm_back(
            normed, scale, gain_ref[...], g_norm
        )
        d_gain = jnp.sum(g_norm * normed, axis=0, keepdims=True)
        d_shift = jnp.sum(g_norm, axis=0, keepdims=True)
        if seq == 0:
            d_norm_ref[0:1] = d_gain
            d_norm_ref[1:2] = d_shift
        else:
            d_norm_ref[0:1] += d_gain
            d_norm_ref[1:2] += d_shift


def norm_back_call(tok, gain, g_res, parts):
    return pl.pallas_call(
        norm_back_kernel,
        out_shape=[
            jax.ShapeDtypeStruct((ROWS, D), F32),
            jax.ShapeDtypeStruct((2, D), F32),
        ],
        compiler_params=params(32),
        cost_estimate=cost(40 * ROWS * D, 6 * MB),
        name="norm_back",
    )(tok, gain, g_res, parts)


def mlp_kernel(
    info_ref,
    tok_ref,
    cot_ref,
    att_ref,
    vec_ref,
    fc_bias_ref,
    wp_ref,
    wf_ref,
    wo_ref,
    out_ref,
    g_res_ref,
    g_att_ref,
    d_vec_ref,
    d_fc_bias_ref,
    d_wp_keep_ref,
    d_wp_give_ref,
    d_wf_keep_ref,
    d_wf_give_ref,
    d_wo_keep_ref,
    d_wo_give_ref,
    res_ref,
    n2_ref,
    n2t_ref,
    att_t_ref,
    act_t_ref,
    g_out_ref,
    acc_ref,
    gn_ref,
    wp_all_ref,
):
    step = pl.program_id(0)
    core = info_ref[SEQ_GRP + 1]
    proj_shift, gain, shift, out_shift = (vec_ref[k : k + 1] for k in range(4))

    @pl.when(step == 0)
    def _():
        att = jnp.concatenate([turn(att_ref[s]) for s in range(SEQ_GRP)], axis=0)
        for half in range(2):
            cut = slice(half * COLS, (half + 1) * COLS)
            pack = pack_of(half, (BLK, CTX_N * PIECE), 0, 1)
            for dp in range(16):
                pieces = wp_ref[:, place_of(dp)].reshape(CTX_N * PIECE, COLS)
                wp_all_ref[dp * BLK : (dp + 1) * BLK, cut] = dot(pack, pieces).astype(
                    BF16
                )
        res_ref[...] = (
            tok_ref[...].astype(F32) + dot(att, wp_all_ref[...]) + proj_shift
        )
        residual = res_ref[...]
        normed, _ = norm_stats(residual)
        normed = normed * gain + shift
        n2_ref[...] = normed.astype(BF16)
        by_core(n2t_ref, normed.T.astype(BF16))
        for seq in range(SEQ_GRP):
            cut = slice(seq * SPAN, (seq + 1) * SPAN)
            by_core(att_t_ref, att_ref[seq], cut)
            pos = info_ref[SEQ_GRP] + lax.broadcasted_iota(jnp.int32, (SPAN, D), 0)
            g_out_ref[cut] = jnp.where(
                pos < info_ref[seq], cot_ref[cut], jnp.zeros((SPAN, D), BF16)
            )
        acc_ref[...] = residual + out_shift
        gn_ref[...] = jnp.zeros_like(gn_ref)

    w_fc = stack_rows(wf_ref, 0)
    pre = dot(n2_ref[...], w_fc) + fc_bias_ref[...]
    root = math.sqrt(2.0 / math.pi)
    square = pre * pre
    bend = jnp.tanh(root * pre * (1.0 + 0.044715 * square))
    gate = 0.5 * (1.0 + bend)
    slope = gate + 0.5 * pre * (1.0 - bend * bend) * root * (
        1.0 + 3.0 * 0.044715 * square
    )
    act_f = pre * gate
    act = act_f.astype(BF16)
    act_t = act_f.T.astype(BF16)
    for c in range(2):
        act_t_ref[c] = act_t[c * 320 : (c + 1) * 320]
    g_act = None
    for half in range(2):
        cut = slice(half * COLS, (half + 1) * COLS)
        w_out = jnp.concatenate(
            [
                wo_ref[z, yh, 0, 0, c, half * 40 : (half + 1) * 40]
                for c in range(2)
                for z in range(4)
                for yh in range(2)
            ],
            axis=0,
        )
        acc_ref[:, cut] += dot(act, w_out)
        part = dot_nt(g_out_ref[:, cut], w_out)
        g_act = part if g_act is None else g_act + part
        for side, ref in ((core, d_wo_keep_ref), (1 - core, d_wo_give_ref)):
            d_w = dot(act_t_ref[side], g_out_ref[:, cut]).astype(BF16)
            for z in range(4):
                for yh in range(2):
                    row = (z * 2 + yh) * 40
                    ref[z, yh, 0, 0, half] = d_w[row : row + 40]
    g_pre = (g_act * slope).astype(BF16)
    d_fc_bias_ref[...] = jnp.sum(g_pre.astype(F32), axis=0, keepdims=True)
    gn_ref[...] += dot_nt(g_pre, w_fc)
    for side, ref in ((core, d_wf_keep_ref), (1 - core, d_wf_give_ref)):
        d_w = dot(n2t_ref[side].reshape(D // 2, ROWS), g_pre).astype(BF16)
        ref[0] = d_w.reshape(8, BLK, COLS)

    @pl.when(step == pl.num_programs(0) - 1)
    def _():
        out_ref[...] = acc_ref[...].astype(BF16)
        normed, scale = norm_stats(res_ref[...])
        g_norm = gn_ref[...]
        g_out = g_out_ref[...].astype(F32)
        g_res = (g_out + norm_back(normed, scale, gain, g_norm)).astype(BF16)
        g_res_ref[...] = g_res
        d_vec_ref[0:1] = jnp.sum(g_res.astype(F32), axis=0, keepdims=True)
        d_vec_ref[1:2] = jnp.sum(g_norm * normed, axis=0, keepdims=True)
        d_vec_ref[2:3] = jnp.sum(g_norm, axis=0, keepdims=True)
        d_vec_ref[3:4] = jnp.sum(g_out, axis=0, keepdims=True)
        g_att = dot_nt(g_res, wp_all_ref[...])
        for side, ref in ((core, d_wp_keep_ref), (1 - core, d_wp_give_ref)):
            d_w = dot(att_t_ref[side].reshape(D // 2, ROWS), g_res).astype(BF16)
            for chip in range(8):
                piece = None
                for half in range(2):
                    unpack = pack_of(half, (CTX_N * PIECE, BLK), 1, 0)
                    part = dot(
                        unpack,
                        d_w[
                            chip * BLK : (chip + 1) * BLK,
                            half * COLS : (half + 1) * COLS,
                        ],
                    )
                    piece = part if piece is None else piece + part
                ref[:, chip] = piece.astype(BF16).reshape(CTX_N, PIECE, COLS)
        for seq in range(SEQ_GRP):
            g_att_ref[seq] = g_att[seq * SPAN : (seq + 1) * SPAN].T.astype(BF16)


def pack_of(half, shape, row_dim, piece_dim):
    row = lax.broadcasted_iota(jnp.int32, shape, row_dim)
    place = lax.broadcasted_iota(jnp.int32, shape, piece_dim)
    offset = place - 22 * (row // 10) - 10 * half
    return (offset == row).astype(F32).astype(BF16)


def by_core(ref, turned, cut=slice(None)):
    for dp in range(16):
        ref[dp % 2, place_of(dp) // 2, :, cut] = turned[dp * BLK : (dp + 1) * BLK]


def mlp_call(info, tok, cot, att, vecs, fc_bias, weights):
    wp_block = whole((8, 8, PIECE, COLS))
    wf_block = pl.BlockSpec((1, 8, BLK, COLS), lambda j: (j, 0, 0, 0))
    wo_block = pl.BlockSpec(
        (4, 2, 1, 1, 2, 40, COLS), lambda j: (0, 0, j % 2, j // 2, 0, 0, 0)
    )
    small = jax.ShapeDtypeStruct((8, 8, PIECE, COLS), BF16)
    wide = jax.ShapeDtypeStruct((8, 8, BLK, COLS), BF16)
    tall = jax.ShapeDtypeStruct((4, 2, 2, 4, 2, 40, COLS), BF16)
    by_ctx = weights.reshape(CTX_N, 16, 2 * BLK + PIECE, COLS)
    by_chip = weights.reshape(4, 2, 2, 4, 2, 2 * BLK + PIECE, COLS)
    return pl.pallas_call(
        mlp_kernel,
        grid=(8,),
        in_specs=[
            pl.BlockSpec(memory_space=pltpu.SMEM),
            whole((ROWS, D)),
            whole((ROWS, D)),
            whole((SEQ_GRP, D, SPAN)),
            whole((4, D)),
            pl.BlockSpec((1, COLS), lambda j: (0, j)),
            pl.BlockSpec((CTX_N, 16, PIECE, COLS), lambda j: (0, 0, 5, 0)),
            pl.BlockSpec((1, 16, BLK, COLS), lambda j: (j, 0, 0, 0)),
            pl.BlockSpec(
                (4, 2, 1, 1, 2, BLK, COLS), lambda j: (0, 0, j % 2, j // 2, 0, 1, 0)
            ),
        ],
        out_specs=[
            whole((ROWS, D)),
            whole((ROWS, D)),
            whole((SEQ_GRP, D, SPAN)),
            whole((4, D)),
            pl.BlockSpec((1, COLS), lambda j: (0, j)),
            wp_block,
            wp_block,
            wf_block,
            wf_block,
            wo_block,
            wo_block,
        ],
        out_shape=[
            jax.ShapeDtypeStruct((ROWS, D), BF16),
            jax.ShapeDtypeStruct((ROWS, D), BF16),
            jax.ShapeDtypeStruct((SEQ_GRP, D, SPAN), BF16),
            jax.ShapeDtypeStruct((4, D), F32),
            jax.ShapeDtypeStruct((1, 4 * D), F32),
            small,
            small,
            wide,
            wide,
            tall,
            tall,
        ],
        scratch_shapes=[
            pltpu.VMEM((ROWS, D), F32),
            pltpu.VMEM((ROWS, D), BF16),
            pltpu.VMEM((2, 8, BLK, ROWS), BF16),
            pltpu.VMEM((2, 8, BLK, ROWS), BF16),
            pltpu.VMEM((2, 320, ROWS), BF16),
            pltpu.VMEM((ROWS, D), BF16),
            pltpu.VMEM((ROWS, D), F32),
            pltpu.VMEM((ROWS, D), F32),
            pltpu.VMEM((D, D), BF16),
        ],
        compiler_params=params(58),
        cost_estimate=cost(2 * ROWS * D * (24 * D + 3 * D), 62 * MB, 2 * ROWS * 4 * D),
        name="mlp",
    )(info, tok, cot, att, vecs, fc_bias, by_ctx, by_ctx, by_chip)


def ring_perm(axis):
    pairs = []
    for core in range(2):
        for pos in range(4):
            to = (pos + (1 if core == 0 else -1)) % 4
            if axis == "x":
                index = lambda p: p * 2 + core
            elif axis == "z":
                index = lambda p: core * 4 + p
            else:
                index = lambda p: ((p % 2) * 2 + core) * 2 + p // 2
            pairs.append((index(pos), index(to)))
    return {"x": ("x", "c"), "z": ("c", "z"), "y": ("yl", "c", "yh")}[axis], pairs


def swap_cores(array):
    return lax.ppermute(array, "c", [(0, 1), (1, 0)])


def shift_perm(axis, by):
    if axis != "y":
        return axis, [(p, (p + by) % 4) for p in range(4)]
    index = lambda p: (p % 2) * 2 + p // 2
    return ("yl", "yh"), [(index(p), index((p + by) % 4)) for p in range(4)]


class Sums:
    dims = {"z": 0, "y": 1, "x": 2}

    def __init__(self, colours):
        self.pieces = [pieces for pieces, _ in colours]
        self.orders = [order for _, order in colours]
        self.way = 1 - 2 * lax.axis_index("c")
        self.place = {
            "x": lax.axis_index("x"),
            "y": 2 * lax.axis_index("yh") + lax.axis_index("yl"),
            "z": lax.axis_index("z"),
        }
        self.phase = 0
        self.step = 0
        self.flight = None

    def local(self, colour, axis, block):
        parts = []
        for terms, first, last in self.pieces[colour]:
            total = None
            for term in terms:
                part = lax.dynamic_slice_in_dim(
                    term[..., first:last, :], block, 1, self.dims[axis]
                ).astype(F32)
                total = part if total is None else total + part
            parts.append(total)
        return parts[0] if len(parts) == 1 else jnp.concatenate(parts, axis=-2)

    def axes(self):
        return [order[self.phase] for order in self.orders]

    def start(self):
        if self.phase == 2:
            self.flight = [
                [
                    lax.ppermute(
                        self.local(k, a, (self.place[a] + by) % 4).astype(BF16),
                        *shift_perm(a, by),
                    )
                    for by in (1, 2, 3)
                ]
                for k, a in enumerate(self.axes())
            ]
            return
        if self.step == 0:
            self.sent = [
                self.local(k, a, (self.place[a] - self.way) % 4).astype(BF16)
                for k, a in enumerate(self.axes())
            ]
        self.flight = [
            lax.ppermute(self.sent[k], *ring_perm(a)) for k, a in enumerate(self.axes())
        ]

    def land(self):
        if self.phase == 2:
            return [
                (
                    self.local(k, a, self.place[a])
                    + sum(part.astype(F32) for part in self.flight[k])
                ).reshape(self.flight[k][0].shape[-2:])
                for k, a in enumerate(self.axes())
            ]
        self.sent = [
            (
                self.flight[k].astype(F32)
                + self.local(k, a, (self.place[a] - self.way * (2 + self.step)) % 4)
            ).astype(BF16)
            for k, a in enumerate(self.axes())
        ]
        self.step += 1
        if self.step == 3:
            self.pieces = [[([s], 0, s.shape[-2])] for s in self.sent]
            self.step, self.phase = 0, self.phase + 1
        return None

    def run(self):
        sums = None
        while sums is None:
            self.start()
            sums = self.land()
        return sums


def tie(first, second):
    return lax.optimization_barrier((first, second))


def per_device(
    tokens,
    lengths,
    cotangent,
    ln1_gain,
    ln1_bias,
    w_qkv,
    q_bias,
    v_bias,
    w_proj,
    proj_bias,
    ln2_gain,
    ln2_bias,
    w_fc,
    fc_bias,
    w_out,
    out_bias,
):
    ctx_rank = lax.axis_index(CTX)
    core = lax.axis_index("c")
    seq_rank = ctx_rank // 4
    head_group = ctx_rank % 4
    tok = tokens.reshape(ROWS, D)
    cot = cotangent.reshape(ROWS, D)

    def exchange(array):
        return lax.all_to_all(array, CTX, 0, 0, tiled=True)

    groups = w_qkv.reshape(10, 3, 4, GROUP_W).transpose(2, 0, 1, 3)
    groups = groups.reshape(4, 10, HEADS_W)
    vec_one = jnp.concatenate([ln1_gain, ln1_bias, q_bias, v_bias])
    vec_one = jnp.pad(vec_one[None, None], ((0, 0), (0, 0), (0, HEADS_W - 40)))
    groups = jnp.concatenate([groups, jnp.broadcast_to(vec_one, (4, 1, HEADS_W))], axis=1)
    groups = jnp.concatenate([groups, groups], axis=0)
    w_cols = w_fc.reshape(10, CTX_N, COLS).transpose(1, 0, 2)
    w_cols = jnp.pad(w_cols, ((0, 0), (0, 0), (0, HEADS_W - COLS)))
    shards = exchange(jnp.concatenate([groups, w_cols], axis=1))

    vec_two = jnp.concatenate([proj_bias, ln2_gain, ln2_bias, out_bias, fc_bias])
    vec_two = jnp.pad(vec_two[None], ((0, PIECE - 21), (0, COLS - 80)))
    part = jnp.concatenate(
        [
            shards[:, 11:, :COLS].reshape(BLK, COLS),
            w_out.reshape(40, 2, COLS).transpose(1, 0, 2).reshape(BLK, COLS),
            w_proj.reshape(10, 2, COLS).transpose(1, 0, 2).reshape(20, COLS),
            vec_two,
        ],
        axis=0,
    )
    part, shards = tie(part, shards)
    weights = lax.all_gather(part, PLACE, axis=0, tiled=False)

    w_group = jnp.concatenate(
        [shards[:, :10].reshape(BLK, HEADS_W), shards[:, 10]], axis=0
    )
    w_group = jnp.broadcast_to(w_group[None], (16, BLK + 8, HEADS_W))
    w_group = lax.all_to_all(w_group, DP, 0, 0, tiled=True)
    sequence = jnp.broadcast_to(tokens[:, None], (SEQ_GRP, 4, SPAN, D))
    w_group, sequence = tie(w_group, sequence)
    sequence = exchange(sequence.reshape(CTX_N, SPAN, D)).reshape(LEN, D)

    vecs = w_group[:, BLK:, :40].reshape(128, 4, 10).transpose(1, 0, 2)
    vecs = vecs.reshape(4, D).astype(F32)
    own = lax.dynamic_slice_in_dim(vecs[2:], head_group * GROUP_W, GROUP_W, 1)
    bias = jnp.concatenate([own[0:1], jnp.zeros((1, GROUP_W), F32), own[1:2]], axis=1)
    length = lax.dynamic_slice_in_dim(lengths, seq_rank, 1)
    qkv, att, lse = attend_call(length, sequence, vecs[:2], bias, w_group)
    att = exchange(att).reshape(SEQ_GRP, D, SPAN)

    more = weights[:, 2 * BLK + 20, :80].reshape(4, 2, 2, 4, 2, 80)
    more = more.transpose(3, 2, 4, 0, 1, 5).reshape(128, 80).astype(F32)
    fc_shift = more[:, 40:].reshape(1, 4 * D)
    more = more[:, :40].reshape(128, 4, 10).transpose(1, 0, 2).reshape(4, D)
    info = jnp.concatenate([lengths, jnp.stack([ctx_rank * SPAN, core]).astype(jnp.int32)])
    layer_out, g_res, g_att, d_vecs, d_fc_bias, *d_mats = mlp_call(
        info, tok, cot, att, more, fc_shift, weights
    )
    wp_keep, wp_give, wf_keep, wf_give, wo_keep, wo_give = d_mats

    given = [swap_cores(wf_give), swap_cores(wo_give), swap_cores(wp_give)]
    g_att = exchange(g_att.reshape(CTX_N, GROUP_W, SPAN))
    given, g_att = tie(given, g_att)
    sums = Sums(
        [
            ([([keep.reshape(4, 4, 4, -1, COLS), give.reshape(4, 4, 4, -1, COLS)], 0, rows)], order)
            for keep, give, rows, order in (
                (wf_keep, given[0], BLK, "xyz"),
                (wo_keep, given[1], BLK, "yzx"),
                (wp_keep, given[2], PIECE, "zxy"),
            )
        ]
    )
    sums.start()
    d_group, d_bias, g_norm = attend_back_call(
        length, sequence, vecs[:2], w_group, qkv, g_att, lse
    )
    sums.flight, g_norm = tie(sums.flight, g_norm)
    sums.land()
    sums.start()
    g_norm = exchange(g_norm)
    sums.flight, g_norm = tie(sums.flight, g_norm)
    sums.land()
    sums.start()
    input_grad, d_norm = norm_back_call(tok, vecs[:1], g_res, g_norm)

    d_heads = jnp.zeros((2, D), F32)
    d_heads = lax.dynamic_update_slice(
        d_heads,
        jnp.concatenate([d_bias[:1, :GROUP_W], d_bias[:1, 2 * GROUP_W :]], axis=0),
        (0, head_group * GROUP_W),
    )
    d_small = jnp.concatenate([d_norm, d_heads, d_vecs], axis=0)
    d_small = d_small.reshape(8, 128, 10).transpose(1, 0, 2).reshape(128, 80)
    d_small = jnp.concatenate([d_small, d_fc_bias.reshape(128, 40)], axis=1)
    d_small = jnp.pad(
        d_small.reshape(16, 8, 120).astype(BF16), ((0, 0), (0, 0), (0, HEADS_W - 120))
    )
    d_group = jnp.concatenate([d_group, d_small], axis=1)
    d_group = lax.all_to_all(d_group, DP, 0, 0, tiled=True)
    sums.flight, d_group = tie(sums.flight, d_group)
    sums.land()
    d_group = jnp.sum(d_group.astype(F32), axis=0).astype(BF16)
    d_group = jnp.concatenate(
        [d_group[:BLK].reshape(CTX_N, 10, HEADS_W), d_group[BLK:, None]], axis=1
    )
    d_group = exchange(d_group).astype(F32)
    d_qkv = (d_group[:4, :10] + d_group[4:, :10]).reshape(4, 10, 3, GROUP_W)
    d_qkv = d_qkv.transpose(1, 2, 0, 3).reshape(10, 3 * D)
    small = jnp.sum(d_group[:, 10, :120], axis=0)

    wf_sum, wo_sum, wp_sum = sums.run()
    d_fc = exchange(wf_sum.astype(BF16).reshape(CTX_N, 10, COLS))
    d_fc = d_fc.transpose(1, 0, 2).reshape(10, CTX_N * COLS).astype(F32)
    d_out = wo_sum.reshape(2, 40, COLS).transpose(1, 0, 2).reshape(40, D)
    d_proj = wp_sum[:20].reshape(2, 10, COLS).transpose(1, 0, 2).reshape(10, D)
    names = ["g1", "b1", "q", "v", "proj", "g2", "b2", "out"]
    vec = {n: small[10 * k : 10 * (k + 1)] for k, n in enumerate(names)}

    return (
        layer_out.reshape(tokens.shape),
        input_grad.reshape(tokens.shape),
        vec["g1"],
        vec["b1"],
        d_qkv,
        vec["q"],
        vec["v"],
        d_proj,
        vec["proj"],
        vec["g2"],
        vec["b2"],
        d_fc,
        small[80:120],
        d_out,
        vec["out"],
    )


def solution(mesh):
    fine = Mesh(mesh.devices.reshape(SIZES), AXES)
    rows = P(DP, CTX, None)
    mat = P(AXES, None)
    vec = P(AXES)
    in_specs = (
        rows,
        P(DP),
        rows,
        vec,
        vec,
        mat,
        vec,
        vec,
        mat,
        vec,
        vec,
        vec,
        mat,
        vec,
        mat,
        vec,
    )
    out_specs = (
        rows,
        rows,
        vec,
        vec,
        mat,
        vec,
        vec,
        mat,
        vec,
        vec,
        vec,
        mat,
        vec,
        mat,
        vec,
    )
    return jax.shard_map(
        per_device, mesh=fine, in_specs=in_specs, out_specs=out_specs, check_vma=False
    )
```

```python
import functools
import math

import jax
import jax.numpy as jnp
from jax import lax
from jax.experimental import pallas as pl
from jax.experimental.pallas import tpu as pltpu
from jax.sharding import Mesh
from jax.sharding import PartitionSpec as P

HEADS = 20
NORM_EPS = 1e-05
MASKED = -1000000000.0

F32 = jnp.float32
BF16 = jnp.bfloat16

AXES = ("x", "yl", "c", "z", "yh")
SIZES = (4, 2, 2, 4, 2)
DP = ("x", "yl", "c")
CTX = ("z", "yh")
PLACE = ("z", "yh", "yl", "x", "c")

D = 1280
SPAN = 128
SEQ_GRP = 2
ROWS = SEQ_GRP * SPAN
CTX_N = 8
LEN = CTX_N * SPAN
HEAD_DIM = D // HEADS
GROUP_HEADS = 5
GROUP_W = GROUP_HEADS * HEAD_DIM
COLS = 640
BLK = 80
SCALE = 1.0 / math.sqrt(HEAD_DIM)
Q_BLOCK = 256
HEADS_W = 3 * GROUP_W
PIECE = 32
LAST = 24
MB = 1 << 20


def place_of(dp):
    x, yl, c = dp // 4, (dp // 2) % 2, dp % 2
    return (yl * 4 + x) * 2 + c


def dot(left, right):
    return lax.dot_general(
        left, right, (((1,), (0,)), ((), ())), preferred_element_type=F32
    )


def dot_nt(left, right):
    return lax.dot_general(
        left, right, (((1,), (1,)), ((), ())), preferred_element_type=F32
    )


def norm_stats(rows):
    centre = jnp.mean(rows, axis=-1, keepdims=True)
    centred = rows - centre
    spread = jnp.mean(centred * centred, axis=-1, keepdims=True)
    scale = lax.rsqrt(spread + NORM_EPS)
    return centred * scale, scale


def norm_back(normed, scale, gain, grad):
    scaled = gain * grad
    mean_one = jnp.mean(scaled, axis=-1, keepdims=True)
    mean_two = jnp.mean(scaled * normed, axis=-1, keepdims=True)
    return (scaled - mean_one - normed * mean_two) * scale


def stack_rows(ref, *lead):
    return jnp.concatenate([ref[(*lead, place_of(dp))] for dp in range(16)], axis=0)


def params(vmem_mb):
    return pltpu.CompilerParams(vmem_limit_bytes=vmem_mb * MB)


def cost(flops, nbytes, trans=0):
    return pl.CostEstimate(flops=flops, bytes_accessed=nbytes, transcendentals=trans)


def whole(shape):
    return pl.BlockSpec(shape, lambda *i: (0,) * len(shape))


def turn(block):
    return block.astype(F32).T.astype(BF16)


def allowed_of(length, first_query, key_count, query_count):
    key_pos = lax.broadcasted_iota(jnp.int32, (key_count, query_count), 0)
    query_pos = first_query + lax.broadcasted_iota(
        jnp.int32, (key_count, query_count), 1
    )
    return (key_pos <= query_pos) & (key_pos < length)


def attend_kernel(
    len_ref, tok_ref, norm_ref, bias_ref, w_ref, qkv_ref, out_ref, lse_ref
):
    head = pl.program_id(0)

    @pl.when(head == 0)
    def _():
        weight = w_ref[...].reshape(D, HEADS_W)
        for block in range(LEN // Q_BLOCK):
            cut = slice(block * Q_BLOCK, (block + 1) * Q_BLOCK)
            normed, _ = norm_stats(tok_ref[cut].astype(F32))
            normed = (normed * norm_ref[0:1] + norm_ref[1:2]).astype(BF16)
            turned = (dot(normed, weight) + bias_ref[...]).T.astype(BF16)
            for row in range(3 * GROUP_HEADS):
                qkv_ref[row // GROUP_HEADS, row % GROUP_HEADS, :, cut] = turned[
                    row * HEAD_DIM : (row + 1) * HEAD_DIM
                ]

    length = len_ref[0]
    query = qkv_ref[0, head]
    key = turn(qkv_ref[1, head])
    value = qkv_ref[2, head]
    for block in range(LEN // Q_BLOCK):
        first = block * Q_BLOCK
        last = first + Q_BLOCK
        scores = dot(key[:last], query[:, first:last]) * SCALE
        scores = jnp.where(allowed_of(length, first, last, Q_BLOCK), scores, MASKED)
        top = jnp.max(scores, axis=0, keepdims=True)
        weights = jnp.exp(scores - top)
        total = jnp.sum(weights, axis=0, keepdims=True)
        result = dot(value[:, :last], weights.astype(BF16)) / total
        lse_ref[0, :, first:last] = top + jnp.log(total)
        result = result.astype(BF16)
        for part in range(Q_BLOCK // SPAN):
            out_ref[first // SPAN + part] = result[:, part * SPAN : (part + 1) * SPAN]


def attend_call(length, tok, norm, bias, w_qkv):
    return pl.pallas_call(
        attend_kernel,
        grid=(GROUP_HEADS,),
        in_specs=[
            pl.BlockSpec(memory_space=pltpu.SMEM),
            whole((LEN, D)),
            whole((2, D)),
            whole((1, HEADS_W)),
            whole((16, BLK, HEADS_W)),
        ],
        out_specs=[
            whole((3, GROUP_HEADS, HEAD_DIM, LEN)),
            pl.BlockSpec((CTX_N, HEAD_DIM, SPAN), lambda h: (0, h, 0)),
            pl.BlockSpec((1, 1, LEN), lambda h: (h, 0, 0)),
        ],
        out_shape=[
            jax.ShapeDtypeStruct((3, GROUP_HEADS, HEAD_DIM, LEN), BF16),
            jax.ShapeDtypeStruct((CTX_N, GROUP_W, SPAN), BF16),
            jax.ShapeDtypeStruct((GROUP_HEADS, 1, LEN), F32),
        ],
        compiler_params=params(56),
        cost_estimate=cost(
            6 * LEN * LEN * 4 * HEAD_DIM + 2 * LEN * D * HEADS_W, 8 * MB, 3 * LEN * LEN
        ),
        name="attend",
    )(length, tok, norm, bias, w_qkv)


def attend_back_kernel(len_ref, qkv_ref, grad_ref, lse_ref, g_ref, gk_ref, gv_ref):
    length = len_ref[0]
    query = qkv_ref[0, 0]
    key_t = qkv_ref[1, 0]
    key = turn(key_t)
    value = turn(qkv_ref[2, 0])
    grad = jnp.concatenate([grad_ref[p] for p in range(CTX_N)], axis=1)
    gk_ref[...] = jnp.zeros_like(gk_ref)
    gv_ref[...] = jnp.zeros_like(gv_ref)
    for block in range(LEN // Q_BLOCK):
        first = block * Q_BLOCK
        last = first + Q_BLOCK
        query_b = query[:, first:last]
        grad_b = grad[:, first:last]
        scores = dot(key[:last], query_b) * SCALE
        probs = jnp.where(
            allowed_of(length, first, last, Q_BLOCK),
            jnp.exp(scores - lse_ref[0, :, first:last]),
            0.0,
        )
        grad_probs = dot(value[:last], grad_b)
        delta = jnp.sum(probs * grad_probs, axis=0, keepdims=True)
        grad_scores = (probs * (grad_probs - delta)).astype(BF16)
        g_ref[0, 0, :, first:last] = (dot(key_t[:, :last], grad_scores) * SCALE).astype(
            BF16
        )
        gk_ref[:, :last] += dot_nt(query_b, grad_scores)
        gv_ref[:, :last] += dot_nt(grad_b, probs.astype(BF16))
    g_ref[1, 0] = (gk_ref[...] * SCALE).astype(BF16)
    g_ref[2, 0] = gv_ref[...].astype(BF16)


def attend_back_call(length, qkv, grad, lse):
    heads = pl.BlockSpec((3, 1, HEAD_DIM, LEN), lambda h: (0, h, 0, 0))
    return pl.pallas_call(
        attend_back_kernel,
        grid=(GROUP_HEADS,),
        in_specs=[
            pl.BlockSpec(memory_space=pltpu.SMEM),
            heads,
            pl.BlockSpec((CTX_N, HEAD_DIM, SPAN), lambda h: (0, h, 0)),
            pl.BlockSpec((1, 1, LEN), lambda h: (h, 0, 0)),
        ],
        out_specs=heads,
        out_shape=jax.ShapeDtypeStruct((3, GROUP_HEADS, HEAD_DIM, LEN), BF16),
        scratch_shapes=[pltpu.VMEM((HEAD_DIM, LEN), F32)] * 2,
        compiler_params=params(48),
        cost_estimate=cost(15 * LEN * LEN * 4 * HEAD_DIM, 5 * MB, 3 * LEN * LEN),
        name="attend_back",
    )(length, qkv, grad, lse)


def norm_grad_kernel(w_ref, g_ref, out_ref):
    weight = w_ref[...].reshape(D, HEADS_W)
    grads = turn(g_ref[...].reshape(HEADS_W, Q_BLOCK))
    g_norm = dot_nt(grads, weight).astype(BF16)
    for part in range(Q_BLOCK // SPAN):
        out_ref[part] = g_norm[part * SPAN : (part + 1) * SPAN]


def norm_grad_call(w_qkv, g_qkv):
    return pl.pallas_call(
        norm_grad_kernel,
        grid=(LEN // Q_BLOCK,),
        in_specs=[
            whole((16, BLK, HEADS_W)),
            pl.BlockSpec((3, GROUP_HEADS, HEAD_DIM, Q_BLOCK), lambda i: (0, 0, 0, i)),
        ],
        out_specs=pl.BlockSpec((Q_BLOCK // SPAN, SPAN, D), lambda i: (i, 0, 0)),
        out_shape=jax.ShapeDtypeStruct((CTX_N, SPAN, D), BF16),
        compiler_params=params(48),
        cost_estimate=cost(2 * LEN * D * HEADS_W, 8 * MB),
        name="norm_grad",
    )(w_qkv, g_qkv)


def qkv_grad_kernel(
    info_ref, tok_ref, norm_ref, g_ref, keep_ref, give_ref, d_bias_ref, n1t_ref
):
    core = info_ref[SEQ_GRP + 1]
    for block in range(LEN // Q_BLOCK):
        cut = slice(block * Q_BLOCK, (block + 1) * Q_BLOCK)
        normed, _ = norm_stats(tok_ref[cut].astype(F32))
        turned = (normed * norm_ref[0:1] + norm_ref[1:2]).T.astype(BF16)
        for dp in range(16):
            n1t_ref[dp % 2, dp // 2, :, cut] = turned[dp * BLK : (dp + 1) * BLK]
    grads = g_ref[...].reshape(HEADS_W, LEN)
    d_bias_ref[...] = dot_nt(jnp.ones((8, LEN), BF16), grads)
    for side, ref in ((core, keep_ref), (1 - core, give_ref)):
        for half in range(2):
            rows = n1t_ref[side, 4 * half : 4 * half + 4].reshape(4 * BLK, LEN)
            ref[4 * half : 4 * half + 4] = (
                dot_nt(rows, grads).astype(BF16).reshape(4, BLK, HEADS_W)
            )


def qkv_grad_call(info, tok, norm, g_qkv):
    half = jax.ShapeDtypeStruct((8, BLK, HEADS_W), BF16)
    vmem = pl.BlockSpec(memory_space=pltpu.VMEM)
    return pl.pallas_call(
        qkv_grad_kernel,
        in_specs=[pl.BlockSpec(memory_space=pltpu.SMEM), vmem, vmem, vmem],
        out_specs=[vmem, vmem, vmem],
        out_shape=[half, half, jax.ShapeDtypeStruct((8, HEADS_W), F32)],
        scratch_shapes=[pltpu.VMEM((2, 8, BLK, LEN), BF16)],
        compiler_params=params(48),
        cost_estimate=cost(2 * LEN * D * HEADS_W, 8 * MB),
        name="qkv_grad",
    )(info, tok, norm, g_qkv)


def norm_back_kernel(
    tok_ref, gain_ref, g_res_ref, part_ref, in_grad_ref, d_norm_ref
):
    for seq in range(SEQ_GRP):
        cut = slice(seq * SPAN, (seq + 1) * SPAN)
        normed, scale = norm_stats(tok_ref[cut].astype(F32))
        g_norm = part_ref[4 * seq].astype(F32)
        for group in range(1, 4):
            g_norm = g_norm + part_ref[4 * seq + group].astype(F32)
        in_grad_ref[cut] = g_res_ref[cut].astype(F32) + norm_back(
            normed, scale, gain_ref[...], g_norm
        )
        d_gain = jnp.sum(g_norm * normed, axis=0, keepdims=True)
        d_shift = jnp.sum(g_norm, axis=0, keepdims=True)
        if seq == 0:
            d_norm_ref[0:1] = d_gain
            d_norm_ref[1:2] = d_shift
        else:
            d_norm_ref[0:1] += d_gain
            d_norm_ref[1:2] += d_shift


def norm_back_call(tok, gain, g_res, parts):
    return pl.pallas_call(
        norm_back_kernel,
        out_shape=[
            jax.ShapeDtypeStruct((ROWS, D), F32),
            jax.ShapeDtypeStruct((2, D), F32),
        ],
        compiler_params=params(32),
        cost_estimate=cost(40 * ROWS * D, 6 * MB),
        name="norm_back",
    )(tok, gain, g_res, parts)


def mlp_kernel(
    info_ref,
    tok_ref,
    cot_ref,
    att_ref,
    vec_ref,
    fc_bias_ref,
    wp_ref,
    wf_ref,
    wo_ref,
    out_ref,
    g_res_ref,
    g_att_ref,
    d_vec_ref,
    d_fc_bias_ref,
    rows_ref,
    keep_ref,
    give_ref,
    n2_ref,
    g_out_ref,
    res_ref,
    acc_ref,
    gn_ref,
    wp_all_ref,
    turned_ref,
):
    step = pl.program_id(0)
    core = info_ref[SEQ_GRP + 1]
    proj_shift, gain, shift, out_shift = (vec_ref[k : k + 1] for k in range(4))

    def by_core(turned, first):
        for dp in range(16):
            turned_ref[dp % 2, place_of(dp) // 2] = turned[dp * BLK : (dp + 1) * BLK]
        keep_ref[first : first + 8] = turned_ref[core]
        give_ref[first : first + 8] = turned_ref[1 - core]

    @pl.when(step == 0)
    def _():
        att = jnp.concatenate([turn(att_ref[s]) for s in range(SEQ_GRP)], axis=0)
        for half in range(2):
            cut = slice(half * COLS, (half + 1) * COLS)
            pack = pack_of(half, PIECE, (BLK, CTX_N * PIECE), 0, 1)
            for dp in range(16):
                pieces = wp_ref[:, place_of(dp)].reshape(CTX_N * PIECE, COLS)
                wp_all_ref[dp * BLK : (dp + 1) * BLK, cut] = dot(pack, pieces).astype(
                    BF16
                )
        residual = tok_ref[...].astype(F32) + dot(att, wp_all_ref[...]) + proj_shift
        res_ref[...] = residual
        normed, _ = norm_stats(residual)
        normed = normed * gain + shift
        n2_ref[...] = normed.astype(BF16)
        by_core(normed.T.astype(BF16), 32)
        by_core(jnp.concatenate([att_ref[s] for s in range(SEQ_GRP)], axis=1), 40)
        for seq in range(SEQ_GRP):
            cut = slice(seq * SPAN, (seq + 1) * SPAN)
            pos = info_ref[SEQ_GRP] + lax.broadcasted_iota(jnp.int32, (SPAN, D), 0)
            g_out_ref[cut] = jnp.where(
                pos < info_ref[seq], cot_ref[cut], jnp.zeros((SPAN, D), BF16)
            )
        rows_ref[:, 4 * D : 5 * D] = g_out_ref[...]
        acc_ref[...] = residual + out_shift
        gn_ref[...] = jnp.zeros_like(gn_ref)

    w_fc = stack_rows(wf_ref, 0)
    pre = dot(n2_ref[...], w_fc) + fc_bias_ref[...]
    root = math.sqrt(2.0 / math.pi)
    square = pre * pre
    bend = jnp.tanh(root * pre * (1.0 + 0.044715 * square))
    gate = 0.5 * (1.0 + bend)
    slope = gate + 0.5 * pre * (1.0 - bend * bend) * root * (
        1.0 + 3.0 * 0.044715 * square
    )
    act = pre * gate
    act_t = act.T.astype(BF16).reshape(2, 4, BLK, ROWS)
    act = act.astype(BF16)
    turned_ref[:, 0:4] = act_t
    keep_ref[pl.ds(step * 4, 4)] = turned_ref[core, 0:4]
    give_ref[pl.ds(step * 4, 4)] = turned_ref[1 - core, 0:4]
    g_act = None
    for half in range(2):
        cut = slice(half * COLS, (half + 1) * COLS)
        w_out = jnp.concatenate(
            [
                wo_ref[z, yh, 0, 0, c, half * 40 : (half + 1) * 40]
                for c in range(2)
                for z in range(4)
                for yh in range(2)
            ],
            axis=0,
        )
        acc_ref[:, cut] += dot(act, w_out)
        part = dot_nt(g_out_ref[:, cut], w_out)
        g_act = part if g_act is None else g_act + part
    g_pre = (g_act * slope).astype(BF16)
    rows_ref[:, pl.ds(pl.multiple_of(step * COLS, COLS), COLS)] = g_pre
    d_fc_bias_ref[...] = jnp.sum(g_pre.astype(F32), axis=0, keepdims=True)
    gn_ref[...] += dot_nt(g_pre, w_fc)

    @pl.when(step == pl.num_programs(0) - 1)
    def _():
        out_ref[...] = acc_ref[...].astype(BF16)
        normed, scale = norm_stats(res_ref[...])
        g_norm = gn_ref[...]
        g_out = g_out_ref[...].astype(F32)
        g_res = (g_out + norm_back(normed, scale, gain, g_norm)).astype(BF16)
        g_res_ref[...] = g_res
        rows_ref[:, 5 * D :] = g_res
        d_vec_ref[0:1] = jnp.sum(g_res.astype(F32), axis=0, keepdims=True)
        d_vec_ref[1:2] = jnp.sum(g_norm * normed, axis=0, keepdims=True)
        d_vec_ref[2:3] = jnp.sum(g_norm, axis=0, keepdims=True)
        d_vec_ref[3:4] = jnp.sum(g_out, axis=0, keepdims=True)
        g_att = dot_nt(g_res, wp_all_ref[...])
        for seq in range(SEQ_GRP):
            g_att_ref[seq] = g_att[seq * SPAN : (seq + 1) * SPAN].T.astype(BF16)


def pack_of(half, piece, shape, row_dim, piece_dim):
    row = lax.broadcasted_iota(jnp.int32, shape, row_dim)
    place = lax.broadcasted_iota(jnp.int32, shape, piece_dim)
    offset = place - (piece - 10) * (row // 10) - 10 * half
    return (offset == row).astype(F32).astype(BF16)


def mlp_call(info, tok, cot, att, vecs, fc_bias, weights):
    by_ctx = weights.reshape(CTX_N, 16, 2 * BLK + PIECE, COLS)
    by_chip = weights.reshape(4, 2, 2, 4, 2, 2 * BLK + PIECE, COLS)
    rows = jax.ShapeDtypeStruct((ROWS, D), BF16)
    turned = jax.ShapeDtypeStruct((48, BLK, ROWS), BF16)
    return pl.pallas_call(
        mlp_kernel,
        grid=(8,),
        in_specs=[
            pl.BlockSpec(memory_space=pltpu.SMEM),
            whole((ROWS, D)),
            whole((ROWS, D)),
            whole((SEQ_GRP, D, SPAN)),
            whole((4, D)),
            pl.BlockSpec((1, COLS), lambda j: (0, j)),
            pl.BlockSpec((CTX_N, 16, PIECE, COLS), lambda j: (0, 0, 5, 0)),
            pl.BlockSpec((1, 16, BLK, COLS), lambda j: (j, 0, 0, 0)),
            pl.BlockSpec(
                (4, 2, 1, 1, 2, BLK, COLS), lambda j: (0, 0, j % 2, j // 2, 0, 1, 0)
            ),
        ],
        out_specs=[
            whole((ROWS, D)),
            whole((ROWS, D)),
            whole((SEQ_GRP, D, SPAN)),
            whole((4, D)),
            pl.BlockSpec((1, COLS), lambda j: (0, j)),
            whole((ROWS, 6 * D)),
            whole((48, BLK, ROWS)),
            whole((48, BLK, ROWS)),
        ],
        out_shape=[
            rows,
            rows,
            jax.ShapeDtypeStruct((SEQ_GRP, D, SPAN), BF16),
            jax.ShapeDtypeStruct((4, D), F32),
            jax.ShapeDtypeStruct((1, 4 * D), F32),
            jax.ShapeDtypeStruct((ROWS, 6 * D), BF16),
            turned,
            turned,
        ],
        scratch_shapes=[
            pltpu.VMEM((ROWS, D), BF16),
            pltpu.VMEM((ROWS, D), BF16),
            pltpu.VMEM((ROWS, D), F32),
            pltpu.VMEM((ROWS, D), F32),
            pltpu.VMEM((ROWS, D), F32),
            pltpu.VMEM((D, D), BF16),
            pltpu.VMEM((2, 8, BLK, ROWS), BF16),
        ],
        compiler_params=params(58),
        cost_estimate=cost(2 * ROWS * D * (16 * D + 2 * D), 38 * MB, 2 * ROWS * 4 * D),
        name="mlp",
    )(info, tok, cot, att, vecs, fc_bias, by_ctx, by_ctx, by_chip)


def both(ref, other_ref, axis):
    return jnp.concatenate([ref[...], other_ref[...]], axis=axis)


def fc_grad_kernel(n2_ref, n2_other_ref, g_ref, g_other_ref, out_ref):
    left = both(n2_ref, n2_other_ref, 2).reshape(D // 2, 2 * ROWS)
    d_w = dot(left, both(g_ref, g_other_ref, 0)).astype(BF16).reshape(8, BLK, COLS)
    for chip in range(8):
        out_ref[chip % 4, 0, chip // 4] = d_w[chip]


def fc_grad_call(turned, turned_other, rows, rows_other):
    n2_block = pl.BlockSpec((8, BLK, ROWS), lambda j: (4, 0, 0))
    g_block = pl.BlockSpec((ROWS, COLS), lambda j: (0, j))
    return pl.pallas_call(
        fc_grad_kernel,
        grid=(8,),
        in_specs=[n2_block, n2_block, g_block, g_block],
        out_specs=pl.BlockSpec((4, 1, 2, BLK, COLS), lambda j: (0, j, 0, 0, 0)),
        out_shape=jax.ShapeDtypeStruct((4, 8, 2, BLK, COLS), BF16),
        compiler_params=params(40),
        cost_estimate=cost(8 * ROWS * D * D, 12 * MB),
        name="fc_grad",
    )(turned, turned_other, rows, rows_other)


def out_grad_kernel(
    act_ref,
    act_other_ref,
    att_ref,
    att_other_ref,
    g_ref,
    g_other_ref,
    one_ref,
    two_ref,
):
    g_both = both(g_ref, g_other_ref, 0)
    act = both(act_ref, act_other_ref, 2).reshape(4 * BLK, 2 * ROWS)
    d_w = dot(act, g_both[:, :D]).astype(BF16)
    for z in range(4):
        for yh in range(2):
            row = (z * 2 + yh) * 40
            one_ref[yh, 0, z, 0] = d_w[row : row + 40, :COLS]
            two_ref[z, 0, yh, 0, :40] = d_w[row : row + 40, COLS:]
    att = both(att_ref, att_other_ref, 2).reshape(BLK, 2 * ROWS)
    d_w = dot(att, g_both[:, D:]).astype(BF16)
    piece = None
    for half in range(2):
        unpack = pack_of(half, LAST, (CTX_N * LAST, BLK), 1, 0)
        part = dot(unpack, d_w[:, half * COLS : (half + 1) * COLS])
        piece = part if piece is None else piece + part
    piece = piece.astype(BF16)
    for z in range(4):
        for yh in range(2):
            row = (z * 2 + yh) * LAST
            two_ref[z, 0, yh, 0, 40:] = piece[row : row + LAST]


def out_grad_call(turned, turned_other, rows, rows_other):
    act_block = pl.BlockSpec((4, BLK, ROWS), lambda j: (j, 0, 0))
    att_block = pl.BlockSpec((1, BLK, ROWS), lambda j: (40 + (j % 2) * 4 + j // 2, 0, 0))
    g_block = pl.BlockSpec((ROWS, 2 * D), lambda j: (0, 2))
    return pl.pallas_call(
        out_grad_kernel,
        grid=(8,),
        in_specs=[act_block, act_block, att_block, att_block, g_block, g_block],
        out_specs=[
            pl.BlockSpec(
                (2, 1, 4, 1, 40, COLS), lambda j: (0, j % 2, 0, j // 2, 0, 0)
            ),
            pl.BlockSpec(
                (4, 1, 2, 1, 40 + LAST, COLS), lambda j: (0, j // 2, 0, j % 2, 0, 0)
            ),
        ],
        out_shape=[
            jax.ShapeDtypeStruct((2, 2, 4, 4, 40, COLS), BF16),
            jax.ShapeDtypeStruct((4, 4, 2, 2, 40 + LAST, COLS), BF16),
        ],
        compiler_params=params(40),
        cost_estimate=cost(10 * ROWS * D * D, 14 * MB),
        name="out_grad",
    )(turned, turned_other, turned, turned_other, rows, rows_other)


def ring_perm(axis):
    pairs = []
    for core in range(2):
        for pos in range(4):
            to = (pos + (1 if core == 0 else -1)) % 4
            if axis == "x":
                index = lambda p: p * 2 + core
            elif axis == "z":
                index = lambda p: core * 4 + p
            else:
                index = lambda p: ((p % 2) * 2 + core) * 2 + p // 2
            pairs.append((index(pos), index(to)))
    return {"x": ("x", "c"), "z": ("c", "z"), "y": ("yl", "c", "yh")}[axis], pairs


def swap_cores(array):
    return lax.ppermute(array, "c", [(0, 1), (1, 0)])


def shift_perm(axis, by):
    if axis != "y":
        return axis, [(p, (p + by) % 4) for p in range(4)]
    index = lambda p: (p % 2) * 2 + p // 2
    return ("yl", "yh"), [(index(p), index((p + by) % 4)) for p in range(4)]


class Sums:
    def __init__(self, colours):
        self.terms = [array for array, _, _ in colours]
        self.orders = [order for _, order, _ in colours]
        self.after = [after for _, _, after in colours]
        self.way = 1 - 2 * lax.axis_index("c")
        self.place = {
            "x": lax.axis_index("x"),
            "y": 2 * lax.axis_index("yh") + lax.axis_index("yl"),
            "z": lax.axis_index("z"),
        }
        self.phase = 0
        self.step = 0
        self.first_blocks()

    def local(self, colour, block):
        return lax.dynamic_index_in_dim(self.terms[colour], block % 4, 0, False)

    def axes(self):
        return list(enumerate(order[self.phase] for order in self.orders))

    def first_blocks(self):
        self.sent = [self.local(k, self.place[a] - self.way) for k, a in self.axes()]

    def start(self):
        if self.phase < 2:
            self.flight = [
                lax.ppermute(self.sent[k], *ring_perm(a)) for k, a in self.axes()
            ]
            return
        self.flight = [
            [
                lax.ppermute(self.local(k, self.place[a] + by), *shift_perm(a, by))
                for by in (1, 2, 3)
            ]
            for k, a in self.axes()
        ]

    def land(self):
        if self.phase == 2:
            return [
                self.local(k, self.place[a]).astype(F32)
                + sum(part.astype(F32) for part in self.flight[k])
                for k, a in self.axes()
            ]
        self.sent = [
            (
                self.flight[k].astype(F32)
                + self.local(k, self.place[a] - self.way * (2 + self.step)).astype(F32)
            ).astype(BF16)
            for k, a in self.axes()
        ]
        self.step += 1
        if self.step == 3:
            self.terms = self.sent
            if self.phase == 0:
                self.terms = [after(t) for after, t in zip(self.after, self.terms)]
            self.step, self.phase = 0, self.phase + 1
            if self.phase < 2:
                self.first_blocks()
        return None

    def advance(self, other):
        self.flight, other = tie(self.flight, other)
        self.land()
        self.sent, other = tie(self.sent, other)
        self.start()
        return other

    def run(self):
        sums = self.land()
        while sums is None:
            self.start()
            sums = self.land()
        return sums


def tie(first, second):
    return lax.optimization_barrier((first, second))


def per_device(
    tokens,
    lengths,
    cotangent,
    ln1_gain,
    ln1_bias,
    w_qkv,
    q_bias,
    v_bias,
    w_proj,
    proj_bias,
    ln2_gain,
    ln2_bias,
    w_fc,
    fc_bias,
    w_out,
    out_bias,
):
    ctx_rank = lax.axis_index(CTX)
    core = lax.axis_index("c")
    seq_rank = ctx_rank // 4
    head_group = ctx_rank % 4
    tok = tokens.reshape(ROWS, D)
    cot = cotangent.reshape(ROWS, D)

    def exchange(array):
        return lax.all_to_all(array, CTX, 0, 0, tiled=True)

    w_cols = exchange(w_fc.reshape(10, CTX_N, COLS).transpose(1, 0, 2))

    vec_two = jnp.concatenate([proj_bias, ln2_gain, ln2_bias, out_bias, fc_bias])
    vec_two = jnp.pad(vec_two[None], ((0, PIECE - 21), (0, COLS - 80)))
    part = jnp.concatenate(
        [
            w_cols.reshape(BLK, COLS),
            w_out.reshape(40, 2, COLS).transpose(1, 0, 2).reshape(BLK, COLS),
            w_proj.reshape(10, 2, COLS).transpose(1, 0, 2).reshape(20, COLS),
            vec_two,
        ],
        axis=0,
    )
    part, w_qkv, tokens = lax.optimization_barrier((part, w_qkv, tokens))
    weights = lax.all_gather(part, PLACE, axis=0, tiled=False)

    groups = w_qkv.reshape(10, 3, 4, GROUP_W).transpose(2, 0, 1, 3)
    groups = groups.reshape(4, 10, HEADS_W)
    vec_one = jnp.concatenate([ln1_gain, ln1_bias, q_bias, v_bias])
    vec_one = jnp.pad(vec_one[None, None], ((0, 0), (0, 0), (0, HEADS_W - 40)))
    groups = jnp.concatenate([groups, jnp.broadcast_to(vec_one, (4, 1, HEADS_W))], axis=1)
    shards = exchange(jnp.concatenate([groups, groups], axis=0))
    w_group = jnp.concatenate(
        [shards[:, :10].reshape(BLK, HEADS_W), shards[:, 10]], axis=0
    )
    w_group = jnp.broadcast_to(w_group[None], (8, BLK + 8, HEADS_W))
    w_group = lax.all_to_all(w_group, ("x", "yl"), 0, 0, tiled=True)
    sequence = jnp.broadcast_to(tokens[:, None], (SEQ_GRP, 4, SPAN, D))
    w_group, sequence = tie(w_group, sequence)
    other = swap_cores(w_group)
    first = jnp.where(core == 0, w_group, other)
    second = jnp.where(core == 0, other, w_group)
    w_group = jnp.stack([first, second], axis=1).reshape(16, BLK + 8, HEADS_W)
    sequence = exchange(sequence.reshape(CTX_N, SPAN, D)).reshape(LEN, D)

    vecs = w_group[:, BLK:, :40].reshape(128, 4, 10).transpose(1, 0, 2)
    vecs = vecs.reshape(4, D).astype(F32)
    own = lax.dynamic_slice_in_dim(vecs[2:], head_group * GROUP_W, GROUP_W, 1)
    bias = jnp.concatenate([own[0:1], jnp.zeros((1, GROUP_W), F32), own[1:2]], axis=1)
    length = lax.dynamic_slice_in_dim(lengths, seq_rank, 1)
    qkv, att, lse = attend_call(length, sequence, vecs[:2], bias, w_group)
    att = exchange(att).reshape(SEQ_GRP, D, SPAN)

    more = weights[:, 2 * BLK + 20, :80].reshape(4, 2, 2, 4, 2, 80)
    more = more.transpose(3, 2, 4, 0, 1, 5).reshape(128, 80).astype(F32)
    fc_shift = more[:, 40:].reshape(1, 4 * D)
    more = more[:, :40].reshape(128, 4, 10).transpose(1, 0, 2).reshape(4, D)
    info = jnp.concatenate([lengths, jnp.stack([ctx_rank * SPAN, core]).astype(jnp.int32)])
    layer_out, g_res, g_att, d_vecs, d_fc_bias, rows, turned, turned_give = mlp_call(
        info, tok, cot, att, more, fc_shift, weights
    )

    turned_other = swap_cores(turned_give)
    rows_other = swap_cores(rows)
    g_att = exchange(g_att.reshape(CTX_N, GROUP_W, SPAN))
    d_fc = fc_grad_call(turned, turned_other, rows, rows_other)
    d_one, d_two = out_grad_call(turned, turned_other, rows, rows_other)

    def to_owners(array):
        array = array.reshape(8, 2, 4, 2, 10, COLS).transpose(3, 1, 2, 0, 4, 5)
        return array.reshape(4, 4, BLK, COLS)

    same = lambda array: array
    sums = Sums(
        [
            (d_fc, "xyz", to_owners),
            (d_one.reshape(4, 4, 4, 40, COLS), "yzx", same),
            (d_two.reshape(4, 4, 4, 40 + LAST, COLS), "zxy", same),
        ]
    )
    sums.sent, g_att = tie(sums.sent, g_att)
    sums.start()
    g_qkv = attend_back_call(length, qkv, g_att, lse)
    g_qkv = sums.advance(g_qkv)
    g_norm = exchange(norm_grad_call(w_group, g_qkv))
    group_keep, group_give, d_bias = qkv_grad_call(info, sequence, vecs[:2], g_qkv)
    group_give = sums.advance(group_give)
    group_given = swap_cores(group_give)
    input_grad, d_norm = norm_back_call(tok, vecs[:1], g_res, g_norm)
    d_norm = sums.advance(d_norm)

    d_heads = jnp.zeros((2, D), F32)
    d_heads = lax.dynamic_update_slice(
        d_heads,
        jnp.concatenate([d_bias[:1, :GROUP_W], d_bias[:1, 2 * GROUP_W :]], axis=0),
        (0, head_group * GROUP_W),
    )
    d_small = jnp.concatenate([d_norm, d_heads, d_vecs], axis=0)
    d_small = d_small.reshape(8, 128, 10).transpose(1, 0, 2).reshape(128, 80)
    d_small = jnp.concatenate([d_small, d_fc_bias.reshape(128, 40)], axis=1)
    d_small = d_small.reshape(8, 2, 8, 120).astype(BF16)
    small_keep = lax.dynamic_index_in_dim(d_small, core, 1, False)
    small_given = swap_cores(lax.dynamic_index_in_dim(d_small, 1 - core, 1, False))
    d_group = (group_keep.astype(F32) + group_given.astype(F32)).astype(BF16)
    d_small = (small_keep.astype(F32) + small_given.astype(F32)).astype(BF16)
    d_small = jnp.pad(d_small, ((0, 0), (0, 0), (0, HEADS_W - 120)))
    d_group = jnp.concatenate([d_group, d_small], axis=1)
    d_group = lax.all_to_all(d_group, ("x", "yl"), 0, 0, tiled=True)
    d_group = jnp.sum(d_group.astype(F32), axis=0).astype(BF16)
    d_group = jnp.concatenate(
        [d_group[:BLK].reshape(CTX_N, 10, HEADS_W), d_group[BLK:, None]], axis=1
    )
    d_group = exchange(d_group).astype(F32)
    d_qkv = (d_group[:4, :10] + d_group[4:, :10]).reshape(4, 10, 3, GROUP_W)
    d_qkv = d_qkv.transpose(1, 2, 0, 3).reshape(10, 3 * D)
    small = jnp.sum(d_group[:, 10, :120], axis=0)

    fc_sum, one_sum, two_sum = sums.run()
    d_fc = fc_sum.reshape(CTX_N, 10, COLS).transpose(1, 0, 2).reshape(10, CTX_N * COLS)
    d_out = jnp.concatenate([one_sum, two_sum[:40]], axis=1)
    d_proj = two_sum[40:60].reshape(2, 10, COLS).transpose(1, 0, 2).reshape(10, D)
    names = ["g1", "b1", "q", "v", "proj", "g2", "b2", "out"]
    vec = {n: small[10 * k : 10 * (k + 1)] for k, n in enumerate(names)}

    return (
        layer_out.reshape(tokens.shape),
        input_grad.reshape(tokens.shape),
        vec["g1"],
        vec["b1"],
        d_qkv,
        vec["q"],
        vec["v"],
        d_proj,
        vec["proj"],
        vec["g2"],
        vec["b2"],
        d_fc,
        small[80:120],
        d_out,
        vec["out"],
    )


def solution(mesh):
    fine = Mesh(mesh.devices.reshape(SIZES), AXES)
    rows = P(DP, CTX, None)
    mat = P(AXES, None)
    vec = P(AXES)
    in_specs = (
        rows,
        P(DP),
        rows,
        vec,
        vec,
        mat,
        vec,
        vec,
        mat,
        vec,
        vec,
        vec,
        mat,
        vec,
        mat,
        vec,
    )
    out_specs = (
        rows,
        rows,
        vec,
        vec,
        mat,
        vec,
        vec,
        mat,
        vec,
        vec,
        vec,
        mat,
        vec,
        mat,
        vec,
    )
    return jax.shard_map(
        per_device, mesh=fine, in_specs=in_specs, out_specs=out_specs, check_vma=False
    )
```

```python
import functools
import math

import jax
import jax.numpy as jnp
from jax import lax
from jax.experimental import pallas as pl
from jax.experimental.pallas import tpu as pltpu
from jax.sharding import Mesh
from jax.sharding import PartitionSpec as P

HEADS = 20
NORM_EPS = 1e-05
MASKED = -1000000000.0

F32 = jnp.float32
BF16 = jnp.bfloat16

AXES = ("x", "yl", "c", "z", "yh")
SIZES = (4, 2, 2, 4, 2)
DP = ("x", "yl", "c")
CTX = ("z", "yh")
PLACE = ("z", "yh", "yl", "x", "c")

D = 1280
SPAN = 128
SEQ_GRP = 2
ROWS = SEQ_GRP * SPAN
CTX_N = 8
LEN = CTX_N * SPAN
HEAD_DIM = D // HEADS
GROUP_HEADS = 5
GROUP_W = GROUP_HEADS * HEAD_DIM
COLS = 640
BLK = 80
SCALE = 1.0 / math.sqrt(HEAD_DIM)
Q_BLOCK = 256
HEADS_W = 3 * GROUP_W
PIECE = 32
LAST = 24
MB = 1 << 20
SHORT = 1000


def place_of(dp):
    x, yl, c = dp // 4, (dp // 2) % 2, dp % 2
    return (yl * 4 + x) * 2 + c


def dot(left, right):
    return lax.dot_general(
        left, right, (((1,), (0,)), ((), ())), preferred_element_type=F32
    )


def dot_nt(left, right):
    return lax.dot_general(
        left, right, (((1,), (1,)), ((), ())), preferred_element_type=F32
    )


def norm_stats(rows):
    centre = jnp.mean(rows, axis=-1, keepdims=True)
    centred = rows - centre
    spread = jnp.mean(centred * centred, axis=-1, keepdims=True)
    scale = lax.rsqrt(spread + NORM_EPS)
    return centred * scale, scale


def norm_back(normed, scale, gain, grad):
    scaled = gain * grad
    mean_one = jnp.mean(scaled, axis=-1, keepdims=True)
    mean_two = jnp.mean(scaled * normed, axis=-1, keepdims=True)
    return (scaled - mean_one - normed * mean_two) * scale


def stack_rows(ref, *lead):
    return jnp.concatenate([ref[(*lead, place_of(dp))] for dp in range(16)], axis=0)


def params(vmem_mb):
    return pltpu.CompilerParams(vmem_limit_bytes=vmem_mb * MB)


def cost(flops, nbytes, trans=0):
    return pl.CostEstimate(
        flops=flops // SHORT, bytes_accessed=nbytes // SHORT, transcendentals=trans // SHORT
    )


def whole(shape):
    return pl.BlockSpec(shape, lambda *i: (0,) * len(shape))


def turn(block):
    return block.astype(F32).T.astype(BF16)


def allowed_of(length, first_query, key_count, query_count):
    key_pos = lax.broadcasted_iota(jnp.int32, (key_count, query_count), 0)
    query_pos = first_query + lax.broadcasted_iota(
        jnp.int32, (key_count, query_count), 1
    )
    return (key_pos <= query_pos) & (key_pos < length)


def attend_kernel(
    len_ref, tok_ref, norm_ref, bias_ref, w_ref, qkv_ref, out_ref, lse_ref
):
    head = pl.program_id(0)

    @pl.when(head == 0)
    def _():
        weight = w_ref[...].reshape(D, HEADS_W)
        for block in range(LEN // Q_BLOCK):
            cut = slice(block * Q_BLOCK, (block + 1) * Q_BLOCK)
            normed, _ = norm_stats(tok_ref[cut].astype(F32))
            normed = (normed * norm_ref[0:1] + norm_ref[1:2]).astype(BF16)
            turned = (dot(normed, weight) + bias_ref[...]).T.astype(BF16)
            for row in range(3 * GROUP_HEADS):
                qkv_ref[row // GROUP_HEADS, row % GROUP_HEADS, :, cut] = turned[
                    row * HEAD_DIM : (row + 1) * HEAD_DIM
                ]

    length = len_ref[0]
    query = qkv_ref[0, head]
    key = turn(qkv_ref[1, head])
    value = qkv_ref[2, head]
    for block in range(LEN // Q_BLOCK):
        first = block * Q_BLOCK
        last = first + Q_BLOCK
        scores = dot(key[:last], query[:, first:last]) * SCALE
        scores = jnp.where(allowed_of(length, first, last, Q_BLOCK), scores, MASKED)
        top = jnp.max(scores, axis=0, keepdims=True)
        weights = jnp.exp(scores - top)
        total = jnp.sum(weights, axis=0, keepdims=True)
        result = dot(value[:, :last], weights.astype(BF16)) / total
        lse_ref[0, :, first:last] = top + jnp.log(total)
        result = result.astype(BF16)
        for part in range(Q_BLOCK // SPAN):
            out_ref[first // SPAN + part] = result[:, part * SPAN : (part + 1) * SPAN]


def attend_call(length, tok, norm, bias, w_qkv):
    return pl.pallas_call(
        attend_kernel,
        grid=(GROUP_HEADS,),
        in_specs=[
            pl.BlockSpec(memory_space=pltpu.SMEM),
            whole((LEN, D)),
            whole((2, D)),
            whole((1, HEADS_W)),
            whole((16, BLK, HEADS_W)),
        ],
        out_specs=[
            whole((3, GROUP_HEADS, HEAD_DIM, LEN)),
            pl.BlockSpec((CTX_N, HEAD_DIM, SPAN), lambda h: (0, h, 0)),
            pl.BlockSpec((1, 1, LEN), lambda h: (h, 0, 0)),
        ],
        out_shape=[
            jax.ShapeDtypeStruct((3, GROUP_HEADS, HEAD_DIM, LEN), BF16),
            jax.ShapeDtypeStruct((CTX_N, GROUP_W, SPAN), BF16),
            jax.ShapeDtypeStruct((GROUP_HEADS, 1, LEN), F32),
        ],
        compiler_params=params(60),
        cost_estimate=cost(
            6 * LEN * LEN * 4 * HEAD_DIM + 2 * LEN * D * HEADS_W, 8 * MB, 3 * LEN * LEN
        ),
        name="attend",
    )(length, tok, norm, bias, w_qkv)


def attend_back_kernel(len_ref, qkv_ref, grad_ref, lse_ref, g_ref, gk_ref, gv_ref):
    length = len_ref[0]
    query = qkv_ref[0, 0]
    key_t = qkv_ref[1, 0]
    key = turn(key_t)
    value = turn(qkv_ref[2, 0])
    grad = jnp.concatenate([grad_ref[p] for p in range(CTX_N)], axis=1)
    gk_ref[...] = jnp.zeros_like(gk_ref)
    gv_ref[...] = jnp.zeros_like(gv_ref)
    for block in range(LEN // Q_BLOCK):
        first = block * Q_BLOCK
        last = first + Q_BLOCK
        query_b = query[:, first:last]
        grad_b = grad[:, first:last]
        scores = dot(key[:last], query_b) * SCALE
        probs = jnp.where(
            allowed_of(length, first, last, Q_BLOCK),
            jnp.exp(scores - lse_ref[0, :, first:last]),
            0.0,
        )
        grad_probs = dot(value[:last], grad_b)
        delta = jnp.sum(probs * grad_probs, axis=0, keepdims=True)
        grad_scores = (probs * (grad_probs - delta)).astype(BF16)
        g_ref[0, 0, :, first:last] = (dot(key_t[:, :last], grad_scores) * SCALE).astype(
            BF16
        )
        gk_ref[:, :last] += dot_nt(query_b, grad_scores)
        gv_ref[:, :last] += dot_nt(grad_b, probs.astype(BF16))
    g_ref[1, 0] = (gk_ref[...] * SCALE).astype(BF16)
    g_ref[2, 0] = gv_ref[...].astype(BF16)


def attend_back_call(length, qkv, grad, lse):
    heads = pl.BlockSpec((3, 1, HEAD_DIM, LEN), lambda h: (0, h, 0, 0))
    return pl.pallas_call(
        attend_back_kernel,
        grid=(GROUP_HEADS,),
        in_specs=[
            pl.BlockSpec(memory_space=pltpu.SMEM),
            heads,
            pl.BlockSpec((CTX_N, HEAD_DIM, SPAN), lambda h: (0, h, 0)),
            pl.BlockSpec((1, 1, LEN), lambda h: (h, 0, 0)),
        ],
        out_specs=heads,
        out_shape=jax.ShapeDtypeStruct((3, GROUP_HEADS, HEAD_DIM, LEN), BF16),
        scratch_shapes=[pltpu.VMEM((HEAD_DIM, LEN), F32)] * 2,
        compiler_params=params(60),
        cost_estimate=cost(15 * LEN * LEN * 4 * HEAD_DIM, 5 * MB, 3 * LEN * LEN),
        name="attend_back",
    )(length, qkv, grad, lse)


def norm_grad_kernel(tok_ref, w_ref, g_ref, out_ref, d_norm_ref):
    weight = w_ref[...].reshape(D, HEADS_W)
    grads = turn(g_ref[...].reshape(HEADS_W, Q_BLOCK))
    g_norm = dot_nt(grads, weight)
    normed, _ = norm_stats(tok_ref[...].astype(F32))

    @pl.when(pl.program_id(0) == 0)
    def _():
        d_norm_ref[...] = jnp.zeros_like(d_norm_ref)

    d_norm_ref[0:1] += jnp.sum(g_norm * normed, axis=0, keepdims=True)
    d_norm_ref[1:2] += jnp.sum(g_norm, axis=0, keepdims=True)
    g_norm = g_norm.astype(BF16)
    for part in range(Q_BLOCK // SPAN):
        out_ref[part] = g_norm[part * SPAN : (part + 1) * SPAN]


def norm_grad_call(tok, w_qkv, g_qkv):
    return pl.pallas_call(
        norm_grad_kernel,
        grid=(LEN // Q_BLOCK,),
        in_specs=[
            pl.BlockSpec((Q_BLOCK, D), lambda i: (i, 0)),
            whole((16, BLK, HEADS_W)),
            pl.BlockSpec((3, GROUP_HEADS, HEAD_DIM, Q_BLOCK), lambda i: (0, 0, 0, i)),
        ],
        out_specs=[
            pl.BlockSpec((Q_BLOCK // SPAN, SPAN, D), lambda i: (i, 0, 0)),
            whole((2, D)),
        ],
        out_shape=[
            jax.ShapeDtypeStruct((CTX_N, SPAN, D), BF16),
            jax.ShapeDtypeStruct((2, D), F32),
        ],
        compiler_params=params(60),
        cost_estimate=cost(2 * LEN * D * HEADS_W, 10 * MB),
        name="norm_grad",
    )(tok, w_qkv, g_qkv)


def qkv_grad_kernel(
    info_ref,
    tok_ref,
    norm_ref,
    g_ref,
    d_norm_ref,
    d_vec_ref,
    d_fc_bias_ref,
    keep_ref,
    give_ref,
    n1t_ref,
    small_ref,
):
    core = info_ref[SEQ_GRP + 1]
    for block in range(LEN // Q_BLOCK):
        cut = slice(block * Q_BLOCK, (block + 1) * Q_BLOCK)
        normed, _ = norm_stats(tok_ref[cut].astype(F32))
        turned = (normed * norm_ref[0:1] + norm_ref[1:2]).T.astype(BF16)
        for dp in range(16):
            n1t_ref[dp % 2, dp // 2, :, cut] = turned[dp * BLK : (dp + 1) * BLK]
    grads = g_ref[...].reshape(HEADS_W, LEN)

    d_bias = dot_nt(jnp.ones((8, LEN), BF16), grads)
    own = lax.broadcasted_iota(jnp.int32, (1, D), 1) // GROUP_W == info_ref[SEQ_GRP + 4]
    vectors = [d_norm_ref[0:1], d_norm_ref[1:2]]
    for third in (0, 2):
        part = d_bias[0:1, third * GROUP_W : (third + 1) * GROUP_W]
        vectors.append(jnp.where(own, jnp.concatenate([part] * 4, axis=1), 0.0))
    vectors += [d_vec_ref[k : k + 1] for k in range(4)]
    small = None
    for k, vector in enumerate(vectors + [d_fc_bias_ref[...]]):
        each = 10 if k < 8 else 40
        width = 128 * each
        owner = lax.broadcasted_iota(jnp.int32, (128, width), 1) // each
        mask = owner == lax.broadcasted_iota(jnp.int32, (128, width), 0)
        feature = lax.broadcasted_iota(jnp.int32, (width, 128), 0) % each
        lane = lax.broadcasted_iota(jnp.int32, (width, 128), 1)
        place = (feature + 10 * k == lane).astype(F32).astype(BF16)
        part = dot(jnp.where(mask, vector, 0.0).astype(BF16), place)
        small = part if small is None else small + part
    for dp in range(16):
        small_ref[dp % 2, dp // 2] = small[dp * 8 : (dp + 1) * 8]

    for side, ref in ((core, keep_ref), (1 - core, give_ref)):
        for half in range(2):
            rows = n1t_ref[side, 4 * half : 4 * half + 4].reshape(4 * BLK, LEN)
            ref[4 * half : 4 * half + 4, :BLK] = (
                dot_nt(rows, grads).astype(BF16).reshape(4, BLK, HEADS_W)
            )
        ref[:, BLK:] = jnp.zeros((8, 16, HEADS_W), BF16)
        ref[:, BLK : BLK + 8, :128] = small_ref[side].astype(BF16)


def qkv_grad_call(info, tok, norm, g_qkv, d_norm, d_vecs, d_fc_bias):
    half = jax.ShapeDtypeStruct((8, BLK + 16, HEADS_W), BF16)
    vmem = pl.BlockSpec(memory_space=pltpu.VMEM)
    return pl.pallas_call(
        qkv_grad_kernel,
        in_specs=[pl.BlockSpec(memory_space=pltpu.SMEM)] + [vmem] * 6,
        out_specs=[vmem, vmem],
        out_shape=[half, half],
        scratch_shapes=[
            pltpu.VMEM((2, 8, BLK, LEN), BF16),
            pltpu.VMEM((2, 8, 8, 128), F32),
        ],
        compiler_params=params(60),
        cost_estimate=cost(2 * LEN * D * HEADS_W, 8 * MB),
        name="qkv_grad",
    )(info, tok, norm, g_qkv, d_norm, d_vecs, d_fc_bias)


def norm_back_kernel(
    seq_ref, tok_ref, gain_ref, g_res_ref, own_ref, other_ref, in_grad_ref
):
    for seq, ref in ((seq_ref[0], own_ref), (1 - seq_ref[0], other_ref)):
        cut = pl.ds(pl.multiple_of(seq * SPAN, SPAN), SPAN)
        normed, scale = norm_stats(tok_ref[cut].astype(F32))
        in_grad_ref[cut] = g_res_ref[cut].astype(F32) + norm_back(
            normed, scale, gain_ref[...], ref[...].astype(F32)
        )


def norm_back_call(seq, tok, gain, g_res, own, other):
    vmem = pl.BlockSpec(memory_space=pltpu.VMEM)
    return pl.pallas_call(
        norm_back_kernel,
        in_specs=[pl.BlockSpec(memory_space=pltpu.SMEM)] + [vmem] * 5,
        out_specs=vmem,
        out_shape=jax.ShapeDtypeStruct((ROWS, D), F32),
        compiler_params=params(60),
        cost_estimate=cost(40 * ROWS * D, 4 * MB),
        name="norm_back",
    )(seq, tok, gain, g_res, own, other)


def mlp_kernel(
    info_ref,
    tok_ref,
    cot_ref,
    att_ref,
    vec_ref,
    fc_bias_ref,
    wp_ref,
    wf_ref,
    wo_ref,
    out_ref,
    g_res_ref,
    g_att_ref,
    d_vec_ref,
    d_fc_bias_ref,
    rows_ref,
    keep_ref,
    give_ref,
    n2_ref,
    g_out_ref,
    res_ref,
    acc_ref,
    gn_ref,
    wp_all_ref,
    turned_ref,
):
    step = pl.program_id(0)
    core = info_ref[SEQ_GRP + 1]
    proj_shift, gain, shift, out_shift = (vec_ref[k : k + 1] for k in range(4))

    def by_core(turned, first):
        for dp in range(16):
            turned_ref[dp % 2, place_of(dp) // 2] = turned[dp * BLK : (dp + 1) * BLK]
        keep_ref[first : first + 8] = turned_ref[core]
        give_ref[first : first + 8] = turned_ref[1 - core]

    @pl.when(step == 0)
    def _():
        turned = jnp.concatenate(
            [
                jnp.concatenate([att_ref[g, s] for g in range(4)], axis=0)
                for s in range(SEQ_GRP)
            ],
            axis=1,
        )
        att = turn(turned)
        for half in range(2):
            cut = slice(half * COLS, (half + 1) * COLS)
            pack = pack_of(half, PIECE, (BLK, CTX_N * PIECE), 0, 1)
            for dp in range(16):
                pieces = wp_ref[:, place_of(dp)].reshape(CTX_N * PIECE, COLS)
                wp_all_ref[dp * BLK : (dp + 1) * BLK, cut] = dot(pack, pieces).astype(
                    BF16
                )
        residual = tok_ref[...].astype(F32) + dot(att, wp_all_ref[...]) + proj_shift
        res_ref[...] = residual
        normed, _ = norm_stats(residual)
        normed = normed * gain + shift
        n2_ref[...] = normed.astype(BF16)
        by_core(normed.T.astype(BF16), 32)
        by_core(turned, 40)
        for seq in range(SEQ_GRP):
            cut = slice(seq * SPAN, (seq + 1) * SPAN)
            pos = info_ref[SEQ_GRP] + lax.broadcasted_iota(jnp.int32, (SPAN, D), 0)
            g_out_ref[cut] = jnp.where(
                pos < info_ref[seq], cot_ref[cut], jnp.zeros((SPAN, D), BF16)
            )
        rows_ref[:, 4 * D : 5 * D] = g_out_ref[...]
        acc_ref[...] = residual + out_shift
        gn_ref[...] = jnp.zeros_like(gn_ref)

    w_fc = jnp.concatenate([stack_rows(wf_ref, 0), stack_rows(wf_ref, 1)], axis=1)
    pre = dot(n2_ref[...], w_fc) + fc_bias_ref[...]
    root = math.sqrt(2.0 / math.pi)
    square = pre * pre
    bend = jnp.tanh(root * pre * (1.0 + 0.044715 * square))
    gate = 0.5 * (1.0 + bend)
    slope = gate + 0.5 * pre * (1.0 - bend * bend) * root * (
        1.0 + 3.0 * 0.044715 * square
    )
    act = pre * gate
    act_t = act.T.astype(BF16).reshape(2, 2, 4, BLK, ROWS)
    act = act.astype(BF16)
    for c in range(2):
        turned_ref[c] = act_t[:, c].reshape(8, BLK, ROWS)
    keep_ref[pl.ds(step * 8, 8)] = turned_ref[core]
    give_ref[pl.ds(step * 8, 8)] = turned_ref[1 - core]
    w_out = jnp.concatenate(
        [
            jnp.concatenate(
                [
                    wo_ref[z, yh, yl, 0, c, half * 40 : (half + 1) * 40]
                    for yl in range(2)
                    for c in range(2)
                    for z in range(4)
                    for yh in range(2)
                ],
                axis=0,
            )
            for half in range(2)
        ],
        axis=1,
    )
    acc_ref[...] += dot(act, w_out)
    g_act = dot_nt(g_out_ref[...], w_out)
    g_pre = (g_act * slope).astype(BF16)
    rows_ref[:, pl.ds(pl.multiple_of(step * D, D), D)] = g_pre
    d_fc_bias_ref[...] = jnp.sum(g_pre.astype(F32), axis=0, keepdims=True)
    gn_ref[...] += dot_nt(g_pre, w_fc)

    @pl.when(step == pl.num_programs(0) - 1)
    def _():
        out_ref[...] = acc_ref[...].astype(BF16)
        normed, scale = norm_stats(res_ref[...])
        g_norm = gn_ref[...]
        g_out = g_out_ref[...].astype(F32)
        g_res = (g_out + norm_back(normed, scale, gain, g_norm)).astype(BF16)
        g_res_ref[...] = g_res
        rows_ref[:, 5 * D :] = g_res
        d_vec_ref[0:1] = jnp.sum(g_res.astype(F32), axis=0, keepdims=True)
        d_vec_ref[1:2] = jnp.sum(g_norm * normed, axis=0, keepdims=True)
        d_vec_ref[2:3] = jnp.sum(g_norm, axis=0, keepdims=True)
        d_vec_ref[3:4] = jnp.sum(g_out, axis=0, keepdims=True)
        g_att = dot_nt(g_res, wp_all_ref[...])
        for seq in range(SEQ_GRP):
            turned = g_att[seq * SPAN : (seq + 1) * SPAN].T.astype(BF16)
            for g in range(4):
                g_att_ref[g, seq] = turned[g * GROUP_W : (g + 1) * GROUP_W]


def pack_of(half, piece, shape, row_dim, piece_dim):
    row = lax.broadcasted_iota(jnp.int32, shape, row_dim)
    place = lax.broadcasted_iota(jnp.int32, shape, piece_dim)
    offset = place - (piece - 10) * (row // 10) - 10 * half
    return (offset == row).astype(F32).astype(BF16)


def mlp_call(info, tok, cot, att, vecs, fc_bias, weights):
    by_ctx = weights.reshape(CTX_N, 16, 2 * BLK + PIECE, COLS)
    by_chip = weights.reshape(4, 2, 2, 4, 2, 2 * BLK + PIECE, COLS)
    rows = jax.ShapeDtypeStruct((ROWS, D), BF16)
    turned = jax.ShapeDtypeStruct((48, BLK, ROWS), BF16)
    return pl.pallas_call(
        mlp_kernel,
        grid=(4,),
        in_specs=[
            pl.BlockSpec(memory_space=pltpu.SMEM),
            whole((ROWS, D)),
            whole((ROWS, D)),
            whole((4, SEQ_GRP, GROUP_W, SPAN)),
            whole((4, D)),
            pl.BlockSpec((1, D), lambda j: (0, j)),
            pl.BlockSpec((CTX_N, 16, PIECE, COLS), lambda j: (0, 0, 5, 0)),
            pl.BlockSpec((2, 16, BLK, COLS), lambda j: (j, 0, 0, 0)),
            pl.BlockSpec(
                (4, 2, 2, 1, 2, BLK, COLS), lambda j: (0, 0, 0, j, 0, 1, 0)
            ),
        ],
        out_specs=[
            whole((ROWS, D)),
            whole((ROWS, D)),
            whole((4, SEQ_GRP, GROUP_W, SPAN)),
            whole((4, D)),
            pl.BlockSpec((1, D), lambda j: (0, j)),
            whole((ROWS, 6 * D)),
            whole((48, BLK, ROWS)),
            whole((48, BLK, ROWS)),
        ],
        out_shape=[
            rows,
            rows,
            jax.ShapeDtypeStruct((4, SEQ_GRP, GROUP_W, SPAN), BF16),
            jax.ShapeDtypeStruct((4, D), F32),
            jax.ShapeDtypeStruct((1, 4 * D), F32),
            jax.ShapeDtypeStruct((ROWS, 6 * D), BF16),
            turned,
            turned,
        ],
        scratch_shapes=[
            pltpu.VMEM((ROWS, D), BF16),
            pltpu.VMEM((ROWS, D), BF16),
            pltpu.VMEM((ROWS, D), F32),
            pltpu.VMEM((ROWS, D), F32),
            pltpu.VMEM((ROWS, D), F32),
            pltpu.VMEM((D, D), BF16),
            pltpu.VMEM((2, 8, BLK, ROWS), BF16),
        ],
        compiler_params=params(60),
        cost_estimate=cost(2 * ROWS * D * (16 * D + 2 * D), 38 * MB, 2 * ROWS * 4 * D),
        name="mlp",
    )(info, tok, cot, att, vecs, fc_bias, by_ctx, by_ctx, by_chip)


def both(ref, other_ref, axis):
    return jnp.concatenate([ref[...], other_ref[...]], axis=axis)


def fc_grad_kernel(
    n2_ref,
    n2_other_ref,
    g_ref,
    g_other_ref,
    att_ref,
    att_other_ref,
    g_res_ref,
    g_res_other_ref,
    out_ref,
    proj_ref,
):
    step = pl.program_id(0)

    @pl.when(step == 0)
    def _():
        att = both(att_ref, att_other_ref, 2).reshape(D // 2, 2 * ROWS)
        d_w = dot(att, both(g_res_ref, g_res_other_ref, 0)).astype(BF16)
        for chip in range(8):
            piece = None
            for half in range(2):
                unpack = pack_of(half, LAST, (CTX_N * LAST, BLK), 1, 0)
                part = dot(
                    unpack,
                    d_w[
                        chip * BLK : (chip + 1) * BLK, half * COLS : (half + 1) * COLS
                    ],
                )
                piece = part if piece is None else piece + part
            proj_ref[:, chip] = piece.astype(BF16).reshape(CTX_N, LAST, COLS)

    left = both(n2_ref, n2_other_ref, 2).reshape(D // 2, 2 * ROWS)
    d_w = dot(left, both(g_ref, g_other_ref, 0)).astype(BF16)
    for chip in range(8):
        for part in range(2):
            out_ref[chip % 4, part, chip // 4, :BLK] = d_w[
                chip * BLK : (chip + 1) * BLK, part * COLS : (part + 1) * COLS
            ]
            out_ref[chip % 4, part, chip // 4, BLK:] = proj_ref[2 * step + part, chip]


def fc_grad_call(turned, turned_other, rows, rows_other):
    n2_block = pl.BlockSpec((8, BLK, ROWS), lambda j: (4, 0, 0))
    g_block = pl.BlockSpec((ROWS, D), lambda j: (0, j))
    att_block = pl.BlockSpec((8, BLK, ROWS), lambda j: (5, 0, 0))
    g_res_block = pl.BlockSpec((ROWS, D), lambda j: (0, 5))
    last = BLK + LAST
    return pl.pallas_call(
        fc_grad_kernel,
        grid=(4,),
        in_specs=[
            n2_block,
            n2_block,
            g_block,
            g_block,
            att_block,
            att_block,
            g_res_block,
            g_res_block,
        ],
        out_specs=pl.BlockSpec((4, 2, 2, last, COLS), lambda j: (0, j, 0, 0, 0)),
        out_shape=jax.ShapeDtypeStruct((4, 8, 2, last, COLS), BF16),
        scratch_shapes=[pltpu.VMEM((CTX_N, 8, LAST, COLS), BF16)],
        compiler_params=params(60),
        cost_estimate=cost(10 * ROWS * D * D, 16 * MB),
        name="fc_grad",
    )(
        turned, turned_other, rows, rows_other, turned, turned_other, rows, rows_other
    )


def owners_kernel(place_ref, in_ref, out_ref, first_ref):
    rows = 8 * BLK
    row = lax.broadcasted_iota(jnp.int32, (rows, rows), 0)
    source = lax.broadcasted_iota(jnp.int32, (rows, rows), 1)
    wanted = (row // 10) % 8 * BLK + row // BLK * 10 + row % 10
    turn_rows = (source == wanted).astype(F32).astype(BF16)
    result = dot(turn_rows, in_ref[:, 0, :BLK].reshape(rows, COLS)).astype(BF16)
    for z in range(4):
        for yh in range(2):
            ctx = z * 2 + yh
            out_ref[yh, 0, z, :BLK] = result[ctx * BLK : (ctx + 1) * BLK]
            out_ref[yh, 0, z, BLK:] = in_ref[ctx, 0, BLK:]

    @pl.when(pl.program_id(0) == place_ref[0] % 2)
    def _():
        first_ref[...] = out_ref[place_ref[0] // 2, 0]


def owners_call(place, array):
    last = BLK + LAST
    return pl.pallas_call(
        owners_kernel,
        grid=(2,),
        in_specs=[
            pl.BlockSpec(memory_space=pltpu.SMEM),
            pl.BlockSpec((8, 1, last, COLS), lambda i: (0, i, 0, 0)),
        ],
        out_specs=[
            pl.BlockSpec((2, 1, 4, last, COLS), lambda i: (0, i, 0, 0, 0)),
            whole((4, last, COLS)),
        ],
        out_shape=[
            jax.ShapeDtypeStruct((2, 2, 4, last, COLS), BF16),
            jax.ShapeDtypeStruct((4, last, COLS), BF16),
        ],
        compiler_params=params(60),
        cost_estimate=cost(4 * 640**3, 5 * MB),
        name="owners",
    )(place, array)


def out_grad_kernel(
    info_ref, act_ref, act_other_ref, g_ref, g_other_ref, out_ref, first_ref
):
    act = both(act_ref, act_other_ref, 2).reshape(8 * BLK, 2 * ROWS)
    d_w = dot(act, both(g_ref, g_other_ref, 0)).astype(BF16)
    for yl in range(2):
        for z in range(4):
            for yh in range(2):
                row = yl * 4 * BLK + (z * 2 + yh) * 40
                out_ref[yh, yl, z, 0, :40] = d_w[row : row + 40, :COLS]
                out_ref[yh, yl, z, 0, 40:] = d_w[row : row + 40, COLS:]
    first = info_ref[SEQ_GRP + 2]
    first_ref[...] = out_ref[first // 2, first % 2]


def out_grad_call(info, turned, turned_other, rows, rows_other):
    act_block = pl.BlockSpec((8, BLK, ROWS), lambda j: (j, 0, 0))
    g_block = pl.BlockSpec((ROWS, D), lambda j: (0, 4))
    return pl.pallas_call(
        out_grad_kernel,
        grid=(4,),
        in_specs=[
            pl.BlockSpec(memory_space=pltpu.SMEM),
            act_block,
            act_block,
            g_block,
            g_block,
        ],
        out_specs=[
            pl.BlockSpec((2, 2, 4, 1, BLK, COLS), lambda j: (0, 0, 0, j, 0, 0)),
            pl.BlockSpec((4, 1, BLK, COLS), lambda j: (0, j, 0, 0)),
        ],
        out_shape=[
            jax.ShapeDtypeStruct((2, 2, 4, 4, BLK, COLS), BF16),
            jax.ShapeDtypeStruct((4, 4, BLK, COLS), BF16),
        ],
        compiler_params=params(60),
        cost_estimate=cost(8 * ROWS * D * D, 16 * MB),
        name="out_grad",
    )(info, turned, turned_other, rows, rows_other)


def add_kernel(mode, at, place_ref, arrived_ref, terms_ref, *refs):
    total = (arrived_ref[...].astype(F32) + terms_ref[0].astype(F32)).astype(BF16)
    if mode == "plain":
        refs[0][...] = total
    elif mode == "spread":
        *blocks, held = refs
        held[...] = total
        for by in range(4):
            blocks[by][...] = held[(place_ref[at + 1] + by) % 4]
    else:
        out_ref, first_ref = refs
        out_ref[...] = total

        @pl.when(pl.program_id(0) == place_ref[at + 1] // 2)
        def _():
            first_ref[...] = out_ref[pl.ds(place_ref[at + 1] % 2 * 4, 4)]


def add_call(place, at, arrived, terms, mode):
    tall, rows, cols = arrived.shape
    part = min(tall, 8)

    def spec(count):
        return pl.BlockSpec((part, count, cols), lambda i, place: (i, 0, 0))

    like = jax.ShapeDtypeStruct
    in_specs = [
        spec(rows),
        pl.BlockSpec((1, part, rows, cols), lambda i, place: (place[at], i, 0, 0)),
    ]
    scratch = []
    if mode == "spread":
        out_specs = [pl.BlockSpec((rows, cols), lambda i, place: (0, 0))] * 4
        out_shape = [like((rows, cols), BF16)] * 4
        scratch = [pltpu.VMEM((part, rows, cols), BF16)]
    elif mode == "first":
        out_specs = [spec(rows), pl.BlockSpec((4, rows, cols), lambda i, place: (0, 0, 0))]
        out_shape = [like((tall, rows, cols), BF16), like((4, rows, cols), BF16)]
    else:
        out_specs = [spec(rows)]
        out_shape = [like((tall, rows, cols), BF16)]
    nbytes = 6 * tall * rows * cols
    return pl.pallas_call(
        functools.partial(add_kernel, mode, at),
        grid_spec=pltpu.PrefetchScalarGridSpec(
            num_scalar_prefetch=1,
            grid=(tall // part,),
            in_specs=in_specs,
            out_specs=out_specs,
            scratch_shapes=scratch,
        ),
        out_shape=out_shape,
        compiler_params=params(60),
        cost_estimate=cost(nbytes // 4, nbytes),
        name="add_blocks",
    )(place, arrived, terms)


def ring_perm(axis):
    pairs = []
    for core in range(2):
        for pos in range(4):
            to = (pos + (1 if core == 0 else -1)) % 4
            if axis == "x":
                index = lambda p: p * 2 + core
            elif axis == "z":
                index = lambda p: core * 4 + p
            else:
                index = lambda p: ((p % 2) * 2 + core) * 2 + p // 2
            pairs.append((index(pos), index(to)))
    return {"x": ("x", "c"), "z": ("c", "z"), "y": ("yl", "c", "yh")}[axis], pairs


def swap_cores(array):
    return lax.ppermute(array, "c", [(0, 1), (1, 0)])


def shift_perm(axis, by):
    if axis != "y":
        return axis, [(p, (p + by) % 4) for p in range(4)]
    index = lambda p: (p % 2) * 2 + p // 2
    return ("yl", "yh"), [(index(p), index((p + by) % 4)) for p in range(4)]


RINGS = [
    (order, phase, step)
    for order in ("yzx", "yz")
    for phase in range(len(order) - 1)
    for step in range(3)
]


def index_of(order, phase, step):
    return RINGS.index((order, phase, step))


def ring_places():
    way = 1 - 2 * lax.axis_index("c")
    place = {
        "x": lax.axis_index("x"),
        "y": 2 * lax.axis_index("yh") + lax.axis_index("yl"),
        "z": lax.axis_index("z"),
    }
    numbers = []
    for order, phase, step in RINGS:
        last = phase == len(order) - 2
        numbers.append((place[order[phase]] - way * (2 + step)) % 4)
        numbers.append((place[order[phase + 1]] - (0 if last else way)) % 4)
    return jnp.stack(numbers).astype(jnp.int32)


class Sum:
    def __init__(self, terms, first, order, place):
        self.terms = terms
        self.sent = first
        self.order = order
        self.place = place
        self.phase = 0
        self.step = 0

    def start(self):
        axis = self.order[self.phase]
        if self.phase < len(self.order) - 1:
            self.flight = lax.ppermute(self.sent, *ring_perm(axis))
        else:
            self.flight = [
                lax.ppermute(self.sent[by], *shift_perm(axis, by)) for by in (1, 2, 3)
            ]

    def land(self):
        if self.phase == len(self.order) - 1:
            return self.sent[0].astype(F32) + sum(f.astype(F32) for f in self.flight)
        mode = "plain"
        if self.step == 2:
            mode = "first" if self.phase == 0 and len(self.order) == 3 else "spread"
        at = 2 * index_of(self.order, self.phase, self.step)
        outs = add_call(self.place, at, self.flight, self.terms, mode)
        self.step += 1
        if mode == "plain":
            self.sent = outs[0]
            return None
        self.step, self.phase = 0, self.phase + 1
        if mode == "first":
            self.terms = outs[0].reshape(4, 4, *outs[0].shape[1:])
            self.sent = outs[1]
        else:
            self.sent = outs
        return None

    def advance(self, other):
        self.flight, other = tie(self.flight, other)
        self.land()
        self.sent, other = tie(self.sent, other)
        self.start()
        return other


def tie(first, second):
    return lax.optimization_barrier((first, second))


def per_device(
    tokens,
    lengths,
    cotangent,
    ln1_gain,
    ln1_bias,
    w_qkv,
    q_bias,
    v_bias,
    w_proj,
    proj_bias,
    ln2_gain,
    ln2_bias,
    w_fc,
    fc_bias,
    w_out,
    out_bias,
):
    ctx_rank = lax.axis_index(CTX)
    core = lax.axis_index("c")
    seq_rank = lax.axis_index("yh")
    head_group = lax.axis_index("z")
    tok = tokens.reshape(ROWS, D)
    cot = cotangent.reshape(ROWS, D)

    def exchange(array):
        return lax.all_to_all(array, CTX, 0, 0, tiled=True)

    w_cols = exchange(w_fc.reshape(10, CTX_N, COLS).transpose(1, 0, 2))

    vec_two = jnp.concatenate([proj_bias, ln2_gain, ln2_bias, out_bias, fc_bias])
    vec_two = jnp.pad(vec_two[None], ((0, PIECE - 21), (0, COLS - 80)))
    part = jnp.concatenate(
        [
            w_cols.reshape(BLK, COLS),
            w_out.reshape(40, 2, COLS).transpose(1, 0, 2).reshape(BLK, COLS),
            w_proj.reshape(10, 2, COLS).transpose(1, 0, 2).reshape(20, COLS),
            vec_two,
        ],
        axis=0,
    )
    part, w_qkv, tokens = lax.optimization_barrier((part, w_qkv, tokens))
    weights = lax.all_gather(part, PLACE, axis=0, tiled=False)

    theirs = lax.dynamic_index_in_dim(tokens, 1 - seq_rank, 0, False)
    mine = lax.dynamic_index_in_dim(tokens, seq_rank, 0, False)
    theirs = lax.ppermute(theirs, "yh", [(0, 1), (1, 0)])
    sequence = jnp.where(
        seq_rank == 0, jnp.stack([mine, theirs]), jnp.stack([theirs, mine])
    )
    sequence = jnp.broadcast_to(sequence[None], (4, 2, SPAN, D))
    groups = w_qkv.reshape(10, 3, 4, GROUP_W).transpose(2, 0, 1, 3)
    groups = groups.reshape(4, 10, HEADS_W)
    vec_one = jnp.concatenate([ln1_gain, ln1_bias, q_bias, v_bias])
    vec_one = jnp.pad(vec_one[None, None], ((0, 0), (0, 0), (0, HEADS_W - 40)))
    groups = jnp.concatenate([groups, jnp.broadcast_to(vec_one, (4, 1, HEADS_W))], axis=1)
    groups = jnp.broadcast_to(groups[:, None], (4, 2, 11, HEADS_W))
    shards = exchange(groups.reshape(CTX_N, 11, HEADS_W))
    w_group = jnp.concatenate(
        [shards[:, :10].reshape(BLK, HEADS_W), shards[:, 10]], axis=0
    )
    w_group = jnp.broadcast_to(w_group[None], (8, BLK + 8, HEADS_W))
    w_group = lax.all_to_all(w_group, ("x", "yl"), 0, 0, tiled=True)
    w_group, sequence = tie(w_group, sequence)
    other = swap_cores(w_group)
    first = jnp.where(core == 0, w_group, other)
    second = jnp.where(core == 0, other, w_group)
    w_group = jnp.stack([first, second], axis=1).reshape(16, BLK + 8, HEADS_W)
    sequence = lax.all_to_all(sequence, "z", 0, 0, tiled=True).reshape(LEN, D)

    vecs = w_group[:, BLK:, :40].reshape(128, 4, 10).transpose(1, 0, 2)
    vecs = vecs.reshape(4, D).astype(F32)
    own = lax.dynamic_slice_in_dim(vecs[2:], head_group * GROUP_W, GROUP_W, 1)
    bias = jnp.concatenate([own[0:1], jnp.zeros((1, GROUP_W), F32), own[1:2]], axis=1)
    length = lax.dynamic_slice_in_dim(lengths, seq_rank, 1)
    qkv, att, lse = attend_call(length, sequence, vecs[:2], bias, w_group)
    att = exchange(att).reshape(4, SEQ_GRP, GROUP_W, SPAN)

    more = weights[:, 2 * BLK + 20, :80].reshape(4, 2, 2, 4, 2, 80)
    more = more.transpose(3, 2, 4, 0, 1, 5).reshape(128, 80).astype(F32)
    fc_shift = more[:, 40:].reshape(1, 4 * D)
    more = more[:, :40].reshape(128, 4, 10).transpose(1, 0, 2).reshape(4, D)
    way = 1 - 2 * core
    chip_y = 2 * lax.axis_index("yh") + lax.axis_index("yl")
    first_sent = [(p - way) % 4 for p in (chip_y, lax.axis_index("z"))]
    first_y = first_sent[0].astype(jnp.int32)[None]
    info = jnp.stack([ctx_rank * SPAN, core, *first_sent, head_group]).astype(jnp.int32)
    info = jnp.concatenate([lengths, info])
    layer_out, g_res, g_att, d_vecs, d_fc_bias, rows, turned, turned_give = mlp_call(
        info, tok, cot, att, more, fc_shift, weights
    )

    turned_other = swap_cores(turned_give)
    rows_other = swap_cores(rows)
    g_att = exchange(g_att.reshape(CTX_N, GROUP_W, SPAN))
    g_att, rows_other = tie(g_att, rows_other)
    d_fc = fc_grad_call(turned, turned_other, rows, rows_other)
    d_fc, rows_other = tie(d_fc, rows_other)
    d_fc = lax.psum_scatter(d_fc, "x", scatter_dimension=0, tiled=False)
    d_out, first = out_grad_call(info, turned, turned_other, rows, rows_other)
    places = ring_places()
    out_sum = Sum(
        d_out.reshape(4, 16, BLK, COLS), first.reshape(16, BLK, COLS), "yzx", places
    )
    out_sum.sent, g_att = tie(out_sum.sent, g_att)
    out_sum.start()
    g_qkv = attend_back_call(length, qkv, g_att, lse)
    g_qkv = out_sum.advance(g_qkv)
    g_norm, d_norm = norm_grad_call(sequence, w_group, g_qkv)
    d_norm, g_qkv = tie(d_norm, g_qkv)
    g_norm = lax.all_to_all(
        g_norm.reshape(4, 2, SPAN, D), "z", 0, 0, tiled=True
    )
    group_keep, group_give = qkv_grad_call(
        info, sequence, vecs[:2], g_qkv, d_norm, d_vecs, d_fc_bias
    )
    group_keep, group_give = out_sum.advance((group_keep, group_give))
    group_given = swap_cores(group_give)
    d_group = (group_keep.astype(F32) + group_given.astype(F32)).astype(BF16)
    g_norm = jnp.sum(g_norm.astype(F32), axis=0).astype(BF16)
    g_own = lax.dynamic_index_in_dim(g_norm, seq_rank, 0, False)
    g_give = lax.dynamic_index_in_dim(g_norm, 1 - seq_rank, 0, False)
    g_other = lax.ppermute(g_give, "yh", [(0, 1), (1, 0)])
    d_group = out_sum.advance(d_group)
    d_group = lax.all_to_all(d_group, ("x", "yl"), 0, 0, tiled=True)
    input_grad = norm_back_call(
        seq_rank.astype(jnp.int32)[None], tok, vecs[:1], g_res, g_own, g_other
    )
    d_fc = out_sum.advance(d_fc)
    d_fc, first_fc = owners_call(first_y, d_fc)
    last = BLK + LAST
    fc_sum = Sum(
        d_fc.reshape(4, 4, last, COLS), first_fc, "yz", places
    )
    fc_sum.start()
    out_sum.advance(())
    fc_sum.advance(())
    out_sum.advance(())
    fc_sum.advance(())
    last_sum = out_sum.land()
    fc_sum.advance(())
    d_fc = fc_sum.land()
    d_group = jnp.sum(d_group.astype(F32), axis=0).astype(BF16)
    d_group = jnp.concatenate(
        [d_group[:BLK].reshape(CTX_N, 10, HEADS_W), d_group[BLK : BLK + 8, None]], axis=1
    )
    d_group = exchange(d_group)
    d_group = d_group.astype(F32)
    d_qkv = jnp.sum(d_group[:, :10].reshape(4, 2, 10, HEADS_W), axis=1)
    d_qkv = d_qkv.reshape(4, 10, 3, GROUP_W)
    d_qkv = d_qkv.transpose(1, 2, 0, 3).reshape(10, 3 * D)
    small = jnp.sum(d_group[:, 10, :120], axis=0)

    d_proj = d_fc[BLK : BLK + 20].reshape(2, 10, COLS).transpose(1, 0, 2).reshape(10, D)
    d_fc = d_fc[:BLK].reshape(CTX_N, 10, COLS).transpose(1, 0, 2)
    d_fc = d_fc.reshape(10, CTX_N * COLS)
    d_out = jnp.concatenate([last_sum[:40], last_sum[40:BLK]], axis=1)
    names = ["g1", "b1", "q", "v", "proj", "g2", "b2", "out"]
    vec = {n: small[10 * k : 10 * (k + 1)] for k, n in enumerate(names)}

    return (
        layer_out.reshape(tokens.shape),
        input_grad.reshape(tokens.shape),
        vec["g1"],
        vec["b1"],
        d_qkv,
        vec["q"],
        vec["v"],
        d_proj,
        vec["proj"],
        vec["g2"],
        vec["b2"],
        d_fc,
        small[80:120],
        d_out,
        vec["out"],
    )


def solution(mesh):
    fine = Mesh(mesh.devices.reshape(SIZES), AXES)
    rows = P(DP, CTX, None)
    mat = P(AXES, None)
    vec = P(AXES)
    in_specs = (
        rows,
        P(DP),
        rows,
        vec,
        vec,
        mat,
        vec,
        vec,
        mat,
        vec,
        vec,
        vec,
        mat,
        vec,
        mat,
        vec,
    )
    out_specs = (
        rows,
        rows,
        vec,
        vec,
        mat,
        vec,
        vec,
        mat,
        vec,
        vec,
        vec,
        mat,
        vec,
        mat,
        vec,
    )
    return jax.shard_map(
        per_device, mesh=fine, in_specs=in_specs, out_specs=out_specs, check_vma=False
    )
```

```python
import functools
import math

import jax
import jax.numpy as jnp
from jax import lax
from jax.experimental import pallas as pl
from jax.experimental.pallas import tpu as pltpu
from jax.sharding import Mesh
from jax.sharding import PartitionSpec as P

HEADS = 20
NORM_EPS = 1e-05
MASKED = -1000000000.0

F32 = jnp.float32
BF16 = jnp.bfloat16

AXES = ("x", "yl", "c", "z", "yh")
SIZES = (4, 2, 2, 4, 2)
DP = ("x", "yl", "c")
CTX = ("z", "yh")
PLACE = ("z", "yh", "yl", "x", "c")

D = 1280
SPAN = 128
SEQ_GRP = 2
ROWS = SEQ_GRP * SPAN
CTX_N = 8
LEN = CTX_N * SPAN
HEAD_DIM = D // HEADS
GROUP_HEADS = 5
GROUP_W = GROUP_HEADS * HEAD_DIM
COLS = 640
BLK = 80
SCALE = 1.0 / math.sqrt(HEAD_DIM)
Q_BLOCK = 256
HEADS_W = 3 * GROUP_W
PIECE = 32
LAST = 24
MB = 1 << 20
SHORT = 1000


def place_of(dp):
    x, yl, c = dp // 4, (dp // 2) % 2, dp % 2
    return (yl * 4 + x) * 2 + c


def dot(left, right):
    return lax.dot_general(
        left, right, (((1,), (0,)), ((), ())), preferred_element_type=F32
    )


def dot_nt(left, right):
    return lax.dot_general(
        left, right, (((1,), (1,)), ((), ())), preferred_element_type=F32
    )


def norm_stats(rows):
    centre = jnp.mean(rows, axis=-1, keepdims=True)
    centred = rows - centre
    spread = jnp.mean(centred * centred, axis=-1, keepdims=True)
    scale = lax.rsqrt(spread + NORM_EPS)
    return centred * scale, scale


def norm_back(normed, scale, gain, grad):
    scaled = gain * grad
    mean_one = jnp.mean(scaled, axis=-1, keepdims=True)
    mean_two = jnp.mean(scaled * normed, axis=-1, keepdims=True)
    return (scaled - mean_one - normed * mean_two) * scale


def stack_rows(ref, *lead):
    return jnp.concatenate([ref[(*lead, place_of(dp))] for dp in range(16)], axis=0)


def params(vmem_mb):
    return pltpu.CompilerParams(vmem_limit_bytes=vmem_mb * MB)


def cost(flops, nbytes, trans=0):
    return pl.CostEstimate(
        flops=flops // SHORT, bytes_accessed=nbytes // SHORT, transcendentals=trans // SHORT
    )


def whole(shape):
    return pl.BlockSpec(shape, lambda *i: (0,) * len(shape))


def turn(block):
    return block.astype(F32).T.astype(BF16)


def allowed_of(length, first_query, key_count, query_count):
    key_pos = lax.broadcasted_iota(jnp.int32, (key_count, query_count), 0)
    query_pos = first_query + lax.broadcasted_iota(
        jnp.int32, (key_count, query_count), 1
    )
    return (key_pos <= query_pos) & (key_pos < length)


def attend_kernel(
    len_ref, tok_ref, norm_ref, bias_ref, w_ref, qkv_ref, out_ref, lse_ref
):
    head = pl.program_id(0)

    @pl.when(head == 0)
    def _():
        weight = w_ref[...].reshape(D, HEADS_W)
        for block in range(LEN // Q_BLOCK):
            cut = slice(block * Q_BLOCK, (block + 1) * Q_BLOCK)
            normed, _ = norm_stats(tok_ref[cut].astype(F32))
            normed = (normed * norm_ref[0:1] + norm_ref[1:2]).astype(BF16)
            turned = (dot(normed, weight) + bias_ref[...]).T.astype(BF16)
            for row in range(3 * GROUP_HEADS):
                qkv_ref[row // GROUP_HEADS, row % GROUP_HEADS, :, cut] = turned[
                    row * HEAD_DIM : (row + 1) * HEAD_DIM
                ]

    length = len_ref[0]
    query = qkv_ref[0, head]
    key = turn(qkv_ref[1, head])
    value = qkv_ref[2, head]
    for block in range(LEN // Q_BLOCK):
        first = block * Q_BLOCK
        last = first + Q_BLOCK
        scores = dot(key[:last], query[:, first:last]) * SCALE
        scores = jnp.where(allowed_of(length, first, last, Q_BLOCK), scores, MASKED)
        top = jnp.max(scores, axis=0, keepdims=True)
        weights = jnp.exp(scores - top)
        total = jnp.sum(weights, axis=0, keepdims=True)
        result = dot(value[:, :last], weights.astype(BF16)) / total
        lse_ref[0, :, first:last] = top + jnp.log(total)
        result = result.astype(BF16)
        for part in range(Q_BLOCK // SPAN):
            out_ref[first // SPAN + part] = result[:, part * SPAN : (part + 1) * SPAN]


def attend_call(length, tok, norm, bias, w_qkv):
    return pl.pallas_call(
        attend_kernel,
        grid=(GROUP_HEADS,),
        in_specs=[
            pl.BlockSpec(memory_space=pltpu.SMEM),
            whole((LEN, D)),
            whole((2, D)),
            whole((1, HEADS_W)),
            whole((16, BLK, HEADS_W)),
        ],
        out_specs=[
            whole((3, GROUP_HEADS, HEAD_DIM, LEN)),
            pl.BlockSpec((CTX_N, HEAD_DIM, SPAN), lambda h: (0, h, 0)),
            pl.BlockSpec((1, 1, LEN), lambda h: (h, 0, 0)),
        ],
        out_shape=[
            jax.ShapeDtypeStruct((3, GROUP_HEADS, HEAD_DIM, LEN), BF16),
            jax.ShapeDtypeStruct((CTX_N, GROUP_W, SPAN), BF16),
            jax.ShapeDtypeStruct((GROUP_HEADS, 1, LEN), F32),
        ],
        compiler_params=params(60),
        cost_estimate=cost(
            6 * LEN * LEN * 4 * HEAD_DIM + 2 * LEN * D * HEADS_W, 8 * MB, 3 * LEN * LEN
        ),
        name="attend",
    )(length, tok, norm, bias, w_qkv)


def attend_back_kernel(len_ref, qkv_ref, grad_ref, lse_ref, g_ref, gk_ref, gv_ref):
    length = len_ref[0]
    query = qkv_ref[0, 0]
    key_t = qkv_ref[1, 0]
    key = turn(key_t)
    value = turn(qkv_ref[2, 0])
    grad = jnp.concatenate([grad_ref[p] for p in range(CTX_N)], axis=1)
    gk_ref[...] = jnp.zeros_like(gk_ref)
    gv_ref[...] = jnp.zeros_like(gv_ref)
    for block in range(LEN // Q_BLOCK):
        first = block * Q_BLOCK
        last = first + Q_BLOCK
        query_b = query[:, first:last]
        grad_b = grad[:, first:last]
        scores = dot(key[:last], query_b) * SCALE
        probs = jnp.where(
            allowed_of(length, first, last, Q_BLOCK),
            jnp.exp(scores - lse_ref[0, :, first:last]),
            0.0,
        )
        grad_probs = dot(value[:last], grad_b)
        delta = jnp.sum(probs * grad_probs, axis=0, keepdims=True)
        grad_scores = (probs * (grad_probs - delta)).astype(BF16)
        g_ref[0, 0, :, first:last] = (dot(key_t[:, :last], grad_scores) * SCALE).astype(
            BF16
        )
        gk_ref[:, :last] += dot_nt(query_b, grad_scores)
        gv_ref[:, :last] += dot_nt(grad_b, probs.astype(BF16))
    g_ref[1, 0] = (gk_ref[...] * SCALE).astype(BF16)
    g_ref[2, 0] = gv_ref[...].astype(BF16)


def attend_back_call(length, qkv, grad, lse):
    heads = pl.BlockSpec((3, 1, HEAD_DIM, LEN), lambda h: (0, h, 0, 0))
    return pl.pallas_call(
        attend_back_kernel,
        grid=(GROUP_HEADS,),
        in_specs=[
            pl.BlockSpec(memory_space=pltpu.SMEM),
            heads,
            pl.BlockSpec((CTX_N, HEAD_DIM, SPAN), lambda h: (0, h, 0)),
            pl.BlockSpec((1, 1, LEN), lambda h: (h, 0, 0)),
        ],
        out_specs=heads,
        out_shape=jax.ShapeDtypeStruct((3, GROUP_HEADS, HEAD_DIM, LEN), BF16),
        scratch_shapes=[pltpu.VMEM((HEAD_DIM, LEN), F32)] * 2,
        compiler_params=params(60),
        cost_estimate=cost(15 * LEN * LEN * 4 * HEAD_DIM, 5 * MB, 3 * LEN * LEN),
        name="attend_back",
    )(length, qkv, grad, lse)


def norm_grad_kernel(place_ref, tok_ref, w_ref, g_ref, *refs):
    *blocks, d_norm_ref = refs
    step = pl.program_id(0)
    weight = w_ref[...].reshape(D, HEADS_W)
    grads = turn(g_ref[...].reshape(HEADS_W, Q_BLOCK))
    g_norm = dot_nt(grads, weight)
    normed, _ = norm_stats(tok_ref[...].astype(F32))

    @pl.when(step == 0)
    def _():
        d_norm_ref[...] = jnp.zeros_like(d_norm_ref)

    d_norm_ref[0:1] += jnp.sum(g_norm * normed, axis=0, keepdims=True)
    d_norm_ref[1:2] += jnp.sum(g_norm, axis=0, keepdims=True)
    g_norm = g_norm.astype(BF16).reshape(2, SPAN, D)
    for by in range(4):

        @pl.when(step == (place_ref[2] + by) % 4)
        def _():
            blocks[by][...] = g_norm


def norm_grad_call(place, tok, w_qkv, g_qkv):
    return pl.pallas_call(
        norm_grad_kernel,
        grid=(LEN // Q_BLOCK,),
        in_specs=[
            pl.BlockSpec(memory_space=pltpu.SMEM),
            pl.BlockSpec((Q_BLOCK, D), lambda i: (i, 0)),
            whole((16, BLK, HEADS_W)),
            pl.BlockSpec((3, GROUP_HEADS, HEAD_DIM, Q_BLOCK), lambda i: (0, 0, 0, i)),
        ],
        out_specs=[whole((2, SPAN, D))] * 4 + [whole((2, D))],
        out_shape=[jax.ShapeDtypeStruct((2, SPAN, D), BF16)] * 4
        + [jax.ShapeDtypeStruct((2, D), F32)],
        compiler_params=params(60),
        cost_estimate=cost(2 * LEN * D * HEADS_W, 10 * MB),
        name="norm_grad",
    )(place, tok, w_qkv, g_qkv)


def qkv_grad_kernel(
    info_ref,
    tok_ref,
    norm_ref,
    g_ref,
    d_norm_ref,
    d_vec_ref,
    d_fc_bias_ref,
    keep_ref,
    give_ref,
    n1t_ref,
    small_ref,
):
    core = info_ref[SEQ_GRP + 1]
    for block in range(LEN // Q_BLOCK):
        cut = slice(block * Q_BLOCK, (block + 1) * Q_BLOCK)
        normed, _ = norm_stats(tok_ref[cut].astype(F32))
        turned = (normed * norm_ref[0:1] + norm_ref[1:2]).T.astype(BF16)
        for dp in range(16):
            n1t_ref[dp % 2, dp // 2, :, cut] = turned[dp * BLK : (dp + 1) * BLK]
    grads = g_ref[...].reshape(HEADS_W, LEN)

    d_bias = dot_nt(jnp.ones((8, LEN), BF16), grads)
    own = lax.broadcasted_iota(jnp.int32, (1, D), 1) // GROUP_W == info_ref[SEQ_GRP + 3]
    vectors = [d_norm_ref[0:1], d_norm_ref[1:2]]
    for third in (0, 2):
        part = d_bias[0:1, third * GROUP_W : (third + 1) * GROUP_W]
        vectors.append(jnp.where(own, jnp.concatenate([part] * 4, axis=1), 0.0))
    vectors += [d_vec_ref[k : k + 1] for k in range(4)]
    small = None
    for k, vector in enumerate(vectors + [d_fc_bias_ref[...]]):
        each = 10 if k < 8 else 40
        width = 128 * each
        owner = lax.broadcasted_iota(jnp.int32, (128, width), 1) // each
        mask = owner == lax.broadcasted_iota(jnp.int32, (128, width), 0)
        feature = lax.broadcasted_iota(jnp.int32, (width, 128), 0) % each
        lane = lax.broadcasted_iota(jnp.int32, (width, 128), 1)
        place = (feature + 10 * k == lane).astype(F32).astype(BF16)
        part = dot(jnp.where(mask, vector, 0.0).astype(BF16), place)
        small = part if small is None else small + part
    for dp in range(16):
        small_ref[dp % 2, dp // 2] = small[dp * 8 : (dp + 1) * 8]

    for side, ref in ((core, keep_ref), (1 - core, give_ref)):
        for half in range(2):
            rows = n1t_ref[side, 4 * half : 4 * half + 4].reshape(4 * BLK, LEN)
            ref[4 * half : 4 * half + 4, :BLK] = (
                dot_nt(rows, grads).astype(BF16).reshape(4, BLK, HEADS_W)
            )
        ref[:, BLK:] = jnp.zeros((8, 16, HEADS_W), BF16)
        ref[:, BLK : BLK + 8, :128] = small_ref[side].astype(BF16)


def qkv_grad_call(info, tok, norm, g_qkv, d_norm, d_vecs, d_fc_bias):
    half = jax.ShapeDtypeStruct((8, BLK + 16, HEADS_W), BF16)
    vmem = pl.BlockSpec(memory_space=pltpu.VMEM)
    return pl.pallas_call(
        qkv_grad_kernel,
        in_specs=[pl.BlockSpec(memory_space=pltpu.SMEM)] + [vmem] * 6,
        out_specs=[vmem, vmem],
        out_shape=[half, half],
        scratch_shapes=[
            pltpu.VMEM((2, 8, BLK, LEN), BF16),
            pltpu.VMEM((2, 8, 8, 128), F32),
        ],
        compiler_params=params(60),
        cost_estimate=cost(2 * LEN * D * HEADS_W, 8 * MB),
        name="qkv_grad",
    )(info, tok, norm, g_qkv, d_norm, d_vecs, d_fc_bias)


def norm_back_kernel(
    seq_ref, tok_ref, gain_ref, g_res_ref, own_ref, other_ref, in_grad_ref
):
    for seq, ref in ((seq_ref[0], own_ref), (1 - seq_ref[0], other_ref)):
        cut = pl.ds(pl.multiple_of(seq * SPAN, SPAN), SPAN)
        normed, scale = norm_stats(tok_ref[cut].astype(F32))
        in_grad_ref[cut] = g_res_ref[cut].astype(F32) + norm_back(
            normed, scale, gain_ref[...], ref[...].astype(F32)
        )


def norm_back_call(seq, tok, gain, g_res, own, other):
    vmem = pl.BlockSpec(memory_space=pltpu.VMEM)
    return pl.pallas_call(
        norm_back_kernel,
        in_specs=[pl.BlockSpec(memory_space=pltpu.SMEM)] + [vmem] * 5,
        out_specs=vmem,
        out_shape=jax.ShapeDtypeStruct((ROWS, D), F32),
        compiler_params=params(60),
        cost_estimate=cost(40 * ROWS * D, 4 * MB),
        name="norm_back",
    )(seq, tok, gain, g_res, own, other)


def mlp_kernel(
    info_ref,
    tok_ref,
    cot_ref,
    att_ref,
    vec_ref,
    fc_bias_ref,
    wp_ref,
    wf_ref,
    wo_ref,
    out_ref,
    g_res_ref,
    g_att_ref,
    d_vec_ref,
    d_fc_bias_ref,
    rows_ref,
    keep_ref,
    give_ref,
    n2_ref,
    g_out_ref,
    res_ref,
    acc_ref,
    gn_ref,
    wp_all_ref,
    turned_ref,
):
    step = pl.program_id(0)
    core = info_ref[SEQ_GRP + 1]
    proj_shift, gain, shift, out_shift = (vec_ref[k : k + 1] for k in range(4))

    def by_core(turned, first):
        for dp in range(16):
            turned_ref[dp % 2, place_of(dp) // 2] = turned[dp * BLK : (dp + 1) * BLK]
        keep_ref[first : first + 8] = turned_ref[core]
        give_ref[first : first + 8] = turned_ref[1 - core]

    @pl.when(step == 0)
    def _():
        turned = jnp.concatenate(
            [
                jnp.concatenate([att_ref[g, s] for g in range(4)], axis=0)
                for s in range(SEQ_GRP)
            ],
            axis=1,
        )
        att = turn(turned)
        for half in range(2):
            cut = slice(half * COLS, (half + 1) * COLS)
            pack = pack_of(half, PIECE, (BLK, CTX_N * PIECE), 0, 1)
            for dp in range(16):
                pieces = wp_ref[:, place_of(dp)].reshape(CTX_N * PIECE, COLS)
                wp_all_ref[dp * BLK : (dp + 1) * BLK, cut] = dot(pack, pieces).astype(
                    BF16
                )
        residual = tok_ref[...].astype(F32) + dot(att, wp_all_ref[...]) + proj_shift
        res_ref[...] = residual
        normed, _ = norm_stats(residual)
        normed = normed * gain + shift
        n2_ref[...] = normed.astype(BF16)
        by_core(normed.T.astype(BF16), 32)
        by_core(turned, 40)
        for seq in range(SEQ_GRP):
            cut = slice(seq * SPAN, (seq + 1) * SPAN)
            pos = info_ref[SEQ_GRP] + lax.broadcasted_iota(jnp.int32, (SPAN, D), 0)
            g_out_ref[cut] = jnp.where(
                pos < info_ref[seq], cot_ref[cut], jnp.zeros((SPAN, D), BF16)
            )
        rows_ref[:, 4 * D : 5 * D] = g_out_ref[...]
        acc_ref[...] = residual + out_shift
        gn_ref[...] = jnp.zeros_like(gn_ref)

    w_fc = jnp.concatenate([stack_rows(wf_ref, 0), stack_rows(wf_ref, 1)], axis=1)
    pre = dot(n2_ref[...], w_fc) + fc_bias_ref[...]
    root = math.sqrt(2.0 / math.pi)
    square = pre * pre
    bend = jnp.tanh(root * pre * (1.0 + 0.044715 * square))
    gate = 0.5 * (1.0 + bend)
    slope = gate + 0.5 * pre * (1.0 - bend * bend) * root * (
        1.0 + 3.0 * 0.044715 * square
    )
    act = pre * gate
    act_t = act.T.astype(BF16).reshape(2, 2, 4, BLK, ROWS)
    act = act.astype(BF16)
    for c in range(2):
        turned_ref[c] = act_t[:, c].reshape(8, BLK, ROWS)
    keep_ref[pl.ds(step * 8, 8)] = turned_ref[core]
    give_ref[pl.ds(step * 8, 8)] = turned_ref[1 - core]
    w_out = jnp.concatenate(
        [
            jnp.concatenate(
                [
                    wo_ref[z, yh, yl, 0, c, half * 40 : (half + 1) * 40]
                    for yl in range(2)
                    for c in range(2)
                    for z in range(4)
                    for yh in range(2)
                ],
                axis=0,
            )
            for half in range(2)
        ],
        axis=1,
    )
    acc_ref[...] += dot(act, w_out)
    g_act = dot_nt(g_out_ref[...], w_out)
    g_pre = (g_act * slope).astype(BF16)
    rows_ref[:, pl.ds(pl.multiple_of(step * D, D), D)] = g_pre
    d_fc_bias_ref[...] = jnp.sum(g_pre.astype(F32), axis=0, keepdims=True)
    gn_ref[...] += dot_nt(g_pre, w_fc)

    @pl.when(step == pl.num_programs(0) - 1)
    def _():
        out_ref[...] = acc_ref[...].astype(BF16)
        normed, scale = norm_stats(res_ref[...])
        g_norm = gn_ref[...]
        g_out = g_out_ref[...].astype(F32)
        g_res = (g_out + norm_back(normed, scale, gain, g_norm)).astype(BF16)
        g_res_ref[...] = g_res
        rows_ref[:, 5 * D :] = g_res
        d_vec_ref[0:1] = jnp.sum(g_res.astype(F32), axis=0, keepdims=True)
        d_vec_ref[1:2] = jnp.sum(g_norm * normed, axis=0, keepdims=True)
        d_vec_ref[2:3] = jnp.sum(g_norm, axis=0, keepdims=True)
        d_vec_ref[3:4] = jnp.sum(g_out, axis=0, keepdims=True)
        g_att = dot_nt(g_res, wp_all_ref[...])
        for seq in range(SEQ_GRP):
            turned = g_att[seq * SPAN : (seq + 1) * SPAN].T.astype(BF16)
            for g in range(4):
                g_att_ref[g, seq] = turned[g * GROUP_W : (g + 1) * GROUP_W]


def pack_of(half, piece, shape, row_dim, piece_dim):
    row = lax.broadcasted_iota(jnp.int32, shape, row_dim)
    place = lax.broadcasted_iota(jnp.int32, shape, piece_dim)
    offset = place - (piece - 10) * (row // 10) - 10 * half
    return (offset == row).astype(F32).astype(BF16)


def mlp_call(info, tok, cot, att, vecs, fc_bias, weights):
    by_ctx = weights.reshape(CTX_N, 16, 2 * BLK + PIECE, COLS)
    by_chip = weights.reshape(4, 2, 2, 4, 2, 2 * BLK + PIECE, COLS)
    rows = jax.ShapeDtypeStruct((ROWS, D), BF16)
    turned = jax.ShapeDtypeStruct((48, BLK, ROWS), BF16)
    return pl.pallas_call(
        mlp_kernel,
        grid=(4,),
        in_specs=[
            pl.BlockSpec(memory_space=pltpu.SMEM),
            whole((ROWS, D)),
            whole((ROWS, D)),
            whole((4, SEQ_GRP, GROUP_W, SPAN)),
            whole((4, D)),
            pl.BlockSpec((1, D), lambda j: (0, j)),
            pl.BlockSpec((CTX_N, 16, PIECE, COLS), lambda j: (0, 0, 5, 0)),
            pl.BlockSpec((2, 16, BLK, COLS), lambda j: (j, 0, 0, 0)),
            pl.BlockSpec(
                (4, 2, 2, 1, 2, BLK, COLS), lambda j: (0, 0, 0, j, 0, 1, 0)
            ),
        ],
        out_specs=[
            whole((ROWS, D)),
            whole((ROWS, D)),
            whole((4, SEQ_GRP, GROUP_W, SPAN)),
            whole((4, D)),
            pl.BlockSpec((1, D), lambda j: (0, j)),
            whole((ROWS, 6 * D)),
            whole((48, BLK, ROWS)),
            whole((48, BLK, ROWS)),
        ],
        out_shape=[
            rows,
            rows,
            jax.ShapeDtypeStruct((4, SEQ_GRP, GROUP_W, SPAN), BF16),
            jax.ShapeDtypeStruct((4, D), F32),
            jax.ShapeDtypeStruct((1, 4 * D), F32),
            jax.ShapeDtypeStruct((ROWS, 6 * D), BF16),
            turned,
            turned,
        ],
        scratch_shapes=[
            pltpu.VMEM((ROWS, D), BF16),
            pltpu.VMEM((ROWS, D), BF16),
            pltpu.VMEM((ROWS, D), F32),
            pltpu.VMEM((ROWS, D), F32),
            pltpu.VMEM((ROWS, D), F32),
            pltpu.VMEM((D, D), BF16),
            pltpu.VMEM((2, 8, BLK, ROWS), BF16),
        ],
        compiler_params=params(60),
        cost_estimate=cost(2 * ROWS * D * (16 * D + 2 * D), 38 * MB, 2 * ROWS * 4 * D),
        name="mlp",
    )(info, tok, cot, att, vecs, fc_bias, by_ctx, by_ctx, by_chip)


def both(ref, other_ref, axis):
    return jnp.concatenate([ref[...], other_ref[...]], axis=axis)


def fc_grad_kernel(
    n2_ref,
    n2_other_ref,
    g_ref,
    g_other_ref,
    att_ref,
    att_other_ref,
    g_res_ref,
    g_res_other_ref,
    out_ref,
    proj_ref,
):
    step = pl.program_id(0)

    @pl.when(step == 0)
    def _():
        att = both(att_ref, att_other_ref, 2).reshape(D // 2, 2 * ROWS)
        d_w = dot(att, both(g_res_ref, g_res_other_ref, 0)).astype(BF16)
        for chip in range(8):
            piece = None
            for half in range(2):
                unpack = pack_of(half, LAST, (CTX_N * LAST, BLK), 1, 0)
                part = dot(
                    unpack,
                    d_w[
                        chip * BLK : (chip + 1) * BLK, half * COLS : (half + 1) * COLS
                    ],
                )
                piece = part if piece is None else piece + part
            proj_ref[:, chip] = piece.astype(BF16).reshape(CTX_N, LAST, COLS)

    left = both(n2_ref, n2_other_ref, 2).reshape(D // 2, 2 * ROWS)
    d_w = dot(left, both(g_ref, g_other_ref, 0)).astype(BF16)
    for chip in range(8):
        for part in range(2):
            out_ref[chip % 4, part, chip // 4, :BLK] = d_w[
                chip * BLK : (chip + 1) * BLK, part * COLS : (part + 1) * COLS
            ]
            out_ref[chip % 4, part, chip // 4, BLK:] = proj_ref[2 * step + part, chip]


def fc_grad_call(turned, turned_other, rows, rows_other):
    n2_block = pl.BlockSpec((8, BLK, ROWS), lambda j: (4, 0, 0))
    g_block = pl.BlockSpec((ROWS, D), lambda j: (0, j))
    att_block = pl.BlockSpec((8, BLK, ROWS), lambda j: (5, 0, 0))
    g_res_block = pl.BlockSpec((ROWS, D), lambda j: (0, 5))
    last = BLK + LAST
    return pl.pallas_call(
        fc_grad_kernel,
        grid=(4,),
        in_specs=[
            n2_block,
            n2_block,
            g_block,
            g_block,
            att_block,
            att_block,
            g_res_block,
            g_res_block,
        ],
        out_specs=pl.BlockSpec((4, 2, 2, last, COLS), lambda j: (0, j, 0, 0, 0)),
        out_shape=jax.ShapeDtypeStruct((4, 8, 2, last, COLS), BF16),
        scratch_shapes=[pltpu.VMEM((CTX_N, 8, LAST, COLS), BF16)],
        compiler_params=params(60),
        cost_estimate=cost(10 * ROWS * D * D, 16 * MB),
        name="fc_grad",
    )(
        turned, turned_other, rows, rows_other, turned, turned_other, rows, rows_other
    )


def owners_kernel(place_ref, in_ref, *refs):
    *blocks, held = refs
    step = pl.program_id(0)
    rows = 8 * BLK
    row = lax.broadcasted_iota(jnp.int32, (rows, rows), 0)
    source = lax.broadcasted_iota(jnp.int32, (rows, rows), 1)
    wanted = (row // 10) % 8 * BLK + row // BLK * 10 + row % 10
    turn_rows = (source == wanted).astype(F32).astype(BF16)
    result = dot(turn_rows, in_ref[:, 0, :BLK].reshape(rows, COLS)).astype(BF16)
    for z in range(4):
        for yh in range(2):
            ctx = z * 2 + yh
            held[2 * yh + step, z, :BLK] = result[ctx * BLK : (ctx + 1) * BLK]
            held[2 * yh + step, z, BLK:] = in_ref[ctx, 0, BLK:]

    @pl.when(step == 1)
    def _():
        for by in range(4):
            blocks[by][...] = held[(place_ref[1] + by) % 4]


def owners_call(place, array):
    last = BLK + LAST
    return pl.pallas_call(
        owners_kernel,
        grid=(2,),
        in_specs=[
            pl.BlockSpec(memory_space=pltpu.SMEM),
            pl.BlockSpec((8, 1, last, COLS), lambda i: (0, i, 0, 0)),
        ],
        out_specs=[whole((4, last, COLS))] * 4,
        out_shape=[jax.ShapeDtypeStruct((4, last, COLS), BF16)] * 4,
        scratch_shapes=[pltpu.VMEM((4, 4, last, COLS), BF16)],
        compiler_params=params(60),
        cost_estimate=cost(4 * 640**3, 5 * MB),
        name="owners",
    )(place, array)


def out_grad_kernel(
    info_ref, act_ref, act_other_ref, g_ref, g_other_ref, out_ref, first_ref
):
    act = both(act_ref, act_other_ref, 2).reshape(8 * BLK, 2 * ROWS)
    d_w = dot(act, both(g_ref, g_other_ref, 0)).astype(BF16)
    for yl in range(2):
        for z in range(4):
            for yh in range(2):
                row = yl * 4 * BLK + (z * 2 + yh) * 40
                out_ref[yh, yl, z, 0, :40] = d_w[row : row + 40, :COLS]
                out_ref[yh, yl, z, 0, 40:] = d_w[row : row + 40, COLS:]
    first = info_ref[SEQ_GRP + 2]
    first_ref[...] = out_ref[first // 2, first % 2]


def out_grad_call(info, turned, turned_other, rows, rows_other):
    act_block = pl.BlockSpec((8, BLK, ROWS), lambda j: (j, 0, 0))
    g_block = pl.BlockSpec((ROWS, D), lambda j: (0, 4))
    return pl.pallas_call(
        out_grad_kernel,
        grid=(4,),
        in_specs=[
            pl.BlockSpec(memory_space=pltpu.SMEM),
            act_block,
            act_block,
            g_block,
            g_block,
        ],
        out_specs=[
            pl.BlockSpec((2, 2, 4, 1, BLK, COLS), lambda j: (0, 0, 0, j, 0, 0)),
            pl.BlockSpec((4, 1, BLK, COLS), lambda j: (0, j, 0, 0)),
        ],
        out_shape=[
            jax.ShapeDtypeStruct((2, 2, 4, 4, BLK, COLS), BF16),
            jax.ShapeDtypeStruct((4, 4, BLK, COLS), BF16),
        ],
        compiler_params=params(60),
        cost_estimate=cost(8 * ROWS * D * D, 16 * MB),
        name="out_grad",
    )(info, turned, turned_other, rows, rows_other)


def add_kernel(place_ref, arrived_ref, terms_ref, out_ref):
    del place_ref
    total = arrived_ref[...].astype(F32) + terms_ref[0].astype(F32)
    out_ref[...] = total.astype(BF16)


def add_call(place, at, arrived, terms):
    tall, rows, cols = arrived.shape
    part = 8
    block = pl.BlockSpec((part, rows, cols), lambda i, place: (i, 0, 0))
    nbytes = 6 * tall * rows * cols
    return pl.pallas_call(
        add_kernel,
        grid_spec=pltpu.PrefetchScalarGridSpec(
            num_scalar_prefetch=1,
            grid=(tall // part,),
            in_specs=[
                block,
                pl.BlockSpec(
                    (1, part, rows, cols), lambda i, place: (place[at], i, 0, 0)
                ),
            ],
            out_specs=[block],
        ),
        out_shape=[jax.ShapeDtypeStruct(arrived.shape, BF16)],
        compiler_params=params(60),
        cost_estimate=cost(nbytes // 4, nbytes),
        name="add_blocks",
    )(place, arrived, terms)


def add_four_kernel(at, place_ref, *refs):
    *blocks, held = refs[4:]
    total = refs[0][...].astype(F32)
    for ref in refs[1:4]:
        total = total + ref[...].astype(F32)
    held[...] = total.astype(BF16)
    for by in range(4):
        blocks[by][...] = held[(place_ref[at] + by) % 4]


def add_four_call(place, at, parts):
    vmem = pl.BlockSpec(memory_space=pltpu.VMEM)
    shape = parts[0].shape
    nbytes = 10 * math.prod(shape)
    return pl.pallas_call(
        functools.partial(add_four_kernel, at),
        in_specs=[pl.BlockSpec(memory_space=pltpu.SMEM)] + [vmem] * 4,
        out_specs=[vmem] * 4,
        out_shape=[jax.ShapeDtypeStruct(shape[1:], BF16)] * 4,
        scratch_shapes=[pltpu.VMEM(shape, BF16)],
        compiler_params=params(60),
        cost_estimate=cost(nbytes // 4, nbytes),
        name="add_four",
    )(place, *parts)


def ring_perm(axis):
    pairs = []
    for core in range(2):
        for pos in range(4):
            to = (pos + (1 if core == 0 else -1)) % 4
            if axis == "x":
                index = lambda p: p * 2 + core
            elif axis == "z":
                index = lambda p: core * 4 + p
            else:
                index = lambda p: ((p % 2) * 2 + core) * 2 + p // 2
            pairs.append((index(pos), index(to)))
    return {"x": ("x", "c"), "z": ("c", "z"), "y": ("yl", "c", "yh")}[axis], pairs


def swap_cores(array):
    return lax.ppermute(array, "c", [(0, 1), (1, 0)])


def shift_perm(axis, by):
    if axis != "y":
        return axis, [(p, (p + by) % 4) for p in range(4)]
    index = lambda p: (p % 2) * 2 + p // 2
    return ("yl", "yh"), [(index(p), index((p + by) % 4)) for p in range(4)]


def places():
    way = 1 - 2 * lax.axis_index("c")
    y = 2 * lax.axis_index("yh") + lax.axis_index("yl")
    ring = [(y - way * by) % 4 for by in (2, 3, 4, 1)]
    numbers = [lax.axis_index("x"), y, lax.axis_index("z"), *ring]
    return jnp.stack(numbers).astype(jnp.int32)


AT = {"x": 0, "y": 1, "z": 2, "ring": 3}


def directly(blocks, axis):
    return [blocks[0]] + [
        lax.ppermute(blocks[by], *shift_perm(axis, by)) for by in (1, 2, 3)
    ]


def total_of(parts):
    return sum(part.astype(F32) for part in parts)


def tie(first, second):
    return lax.optimization_barrier((first, second))


def per_device(
    tokens,
    lengths,
    cotangent,
    ln1_gain,
    ln1_bias,
    w_qkv,
    q_bias,
    v_bias,
    w_proj,
    proj_bias,
    ln2_gain,
    ln2_bias,
    w_fc,
    fc_bias,
    w_out,
    out_bias,
):
    ctx_rank = lax.axis_index(CTX)
    core = lax.axis_index("c")
    seq_rank = lax.axis_index("yh")
    head_group = lax.axis_index("z")
    tok = tokens.reshape(ROWS, D)
    cot = cotangent.reshape(ROWS, D)

    def exchange(array):
        return lax.all_to_all(array, CTX, 0, 0, tiled=True)

    theirs = lax.dynamic_index_in_dim(tokens, 1 - seq_rank, 0, False)
    mine = lax.dynamic_index_in_dim(tokens, seq_rank, 0, False)
    theirs = lax.ppermute(theirs, "yh", [(0, 1), (1, 0)])
    sequence = jnp.where(
        seq_rank == 0, jnp.stack([mine, theirs]), jnp.stack([theirs, mine])
    )
    sequence = jnp.broadcast_to(sequence[None], (4, 2, SPAN, D))
    groups = w_qkv.reshape(10, 3, 4, GROUP_W).transpose(2, 0, 1, 3)
    groups = groups.reshape(4, 10, HEADS_W)
    vec_one = jnp.concatenate([ln1_gain, ln1_bias, q_bias, v_bias])
    vec_one = jnp.pad(vec_one[None, None], ((0, 0), (0, 0), (0, HEADS_W - 40)))
    groups = jnp.concatenate([groups, jnp.broadcast_to(vec_one, (4, 1, HEADS_W))], axis=1)
    groups = jnp.broadcast_to(groups[:, None], (4, 2, 11, HEADS_W))
    w_cols = w_fc.reshape(10, CTX_N, COLS).transpose(1, 0, 2)
    w_cols = jnp.pad(w_cols, ((0, 0), (0, 0), (0, HEADS_W - COLS)))
    groups = groups.reshape(CTX_N, 11, HEADS_W)
    shards = exchange(jnp.concatenate([groups, w_cols], axis=1))

    vec_two = jnp.concatenate([proj_bias, ln2_gain, ln2_bias, out_bias, fc_bias])
    vec_two = jnp.pad(vec_two[None], ((0, PIECE - 21), (0, COLS - 80)))
    part = jnp.concatenate(
        [
            shards[:, 11:, :COLS].reshape(BLK, COLS),
            w_out.reshape(40, 2, COLS).transpose(1, 0, 2).reshape(BLK, COLS),
            w_proj.reshape(10, 2, COLS).transpose(1, 0, 2).reshape(20, COLS),
            vec_two,
        ],
        axis=0,
    )
    part, sequence = tie(part, sequence)
    weights = lax.all_gather(part, PLACE, axis=0, tiled=False)

    sequence = lax.all_to_all(sequence, "z", 0, 0, tiled=True).reshape(LEN, D)
    sequence, shards = tie(sequence, shards)

    w_group = jnp.concatenate(
        [shards[:, :10].reshape(BLK, HEADS_W), shards[:, 10]], axis=0
    )
    w_group = jnp.broadcast_to(w_group[None], (8, BLK + 8, HEADS_W))
    w_group = lax.all_to_all(w_group, ("x", "yl"), 0, 0, tiled=True)
    other = swap_cores(w_group)
    first = jnp.where(core == 0, w_group, other)
    second = jnp.where(core == 0, other, w_group)
    w_group = jnp.stack([first, second], axis=1).reshape(16, BLK + 8, HEADS_W)

    vecs = w_group[:, BLK:, :40].reshape(128, 4, 10).transpose(1, 0, 2)
    vecs = vecs.reshape(4, D).astype(F32)
    own = lax.dynamic_slice_in_dim(vecs[2:], head_group * GROUP_W, GROUP_W, 1)
    bias = jnp.concatenate([own[0:1], jnp.zeros((1, GROUP_W), F32), own[1:2]], axis=1)
    length = lax.dynamic_slice_in_dim(lengths, seq_rank, 1)
    qkv, att, lse = attend_call(length, sequence, vecs[:2], bias, w_group)
    att = exchange(att).reshape(4, SEQ_GRP, GROUP_W, SPAN)

    more = weights[:, 2 * BLK + 20, :80].reshape(4, 2, 2, 4, 2, 80)
    more = more.transpose(3, 2, 4, 0, 1, 5).reshape(128, 80).astype(F32)
    fc_shift = more[:, 40:].reshape(1, 4 * D)
    more = more[:, :40].reshape(128, 4, 10).transpose(1, 0, 2).reshape(4, D)
    place = places()
    info = jnp.stack([ctx_rank * SPAN, core, place[6], head_group]).astype(jnp.int32)
    info = jnp.concatenate([lengths, info])
    layer_out, g_res, g_att, d_vecs, d_fc_bias, rows, turned, turned_give = mlp_call(
        info, tok, cot, att, more, fc_shift, weights
    )

    turned_other = swap_cores(turned_give)
    rows_other = swap_cores(rows)
    g_att = exchange(g_att.reshape(CTX_N, GROUP_W, SPAN))
    d_out, sent = out_grad_call(info, turned, turned_other, rows, rows_other)
    d_out = d_out.reshape(4, 16, BLK, COLS)
    sent = sent.reshape(16, BLK, COLS)
    flight = lax.ppermute(sent, *ring_perm("y"))

    def ring_step(step, arrived):
        return add_call(place, AT["ring"] + step, arrived, d_out)[0]

    sent, rows_other = tie(sent, rows_other)
    d_fc = fc_grad_call(turned, turned_other, rows, rows_other)
    d_fc, g_att = tie(d_fc, g_att)
    d_fc = lax.psum_scatter(d_fc, "x", scatter_dimension=0, tiled=False)
    g_qkv = attend_back_call(length, qkv, g_att, lse)
    flight, g_qkv = tie(flight, g_qkv)
    sent, g_qkv = tie(ring_step(0, flight), g_qkv)
    flight = lax.ppermute(sent, *ring_perm("y"))
    *g_norm, d_norm = norm_grad_call(place, sequence, w_group, g_qkv)
    g_norm = directly(g_norm, "z")
    d_norm, g_qkv = tie(d_norm, g_qkv)
    group_keep, group_give = qkv_grad_call(
        info, sequence, vecs[:2], g_qkv, d_norm, d_vecs, d_fc_bias
    )
    flight, (group_keep, group_give) = tie(flight, (group_keep, group_give))
    sent, (group_keep, group_give) = tie(ring_step(1, flight), (group_keep, group_give))
    flight = lax.ppermute(sent, *ring_perm("y"))
    group_given = swap_cores(group_give)
    d_group = (group_keep.astype(F32) + group_given.astype(F32)).astype(BF16)
    d_group = lax.all_to_all(d_group, ("x", "yl"), 0, 0, tiled=True)

    flight, d_fc = tie(flight, d_fc)
    d_fc = owners_call(place, d_fc)
    d_fc, flight = tie(d_fc, flight)
    d_out = ring_step(2, flight)
    d_out = lax.all_to_all(d_out, ("z", "x"), 0, 0, tiled=True)
    fc_parts = directly(d_fc, "y")
    _, g_norm = tie(fc_parts, g_norm)
    g_norm = total_of(g_norm).astype(BF16)
    g_own = lax.dynamic_index_in_dim(g_norm, seq_rank, 0, False)
    g_give = lax.dynamic_index_in_dim(g_norm, 1 - seq_rank, 0, False)
    g_other = lax.ppermute(g_give, "yh", [(0, 1), (1, 0)])
    d_group = jnp.sum(d_group.astype(F32), axis=0).astype(BF16)
    d_group = jnp.concatenate(
        [d_group[:BLK].reshape(CTX_N, 10, HEADS_W), d_group[BLK : BLK + 8, None]],
        axis=1,
    )
    d_fc = add_four_call(place, AT["z"], fc_parts)
    d_fc, d_out = tie(d_fc, d_out)
    fc_parts = directly(d_fc, "z")
    d_group = exchange(d_group)
    _, g_other = tie(d_fc[0], g_other)
    input_grad = norm_back_call(
        seq_rank.astype(jnp.int32)[None], tok, vecs[:1], g_res, g_own, g_other
    )
    last_sum = jnp.sum(d_out.astype(F32), axis=0)
    d_fc = total_of(fc_parts)
    d_fc, d_group = tie(d_fc, d_group)
    d_group = d_group.astype(F32)
    d_qkv = jnp.sum(d_group[:, :10].reshape(4, 2, 10, HEADS_W), axis=1)
    d_qkv = d_qkv.reshape(4, 10, 3, GROUP_W)
    d_qkv = d_qkv.transpose(1, 2, 0, 3).reshape(10, 3 * D)
    small = jnp.sum(d_group[:, 10, :120], axis=0)

    d_proj = d_fc[BLK : BLK + 20].reshape(2, 10, COLS).transpose(1, 0, 2).reshape(10, D)
    d_fc = d_fc[:BLK].reshape(CTX_N, 10, COLS).transpose(1, 0, 2)
    d_fc = d_fc.reshape(10, CTX_N * COLS)
    d_out = jnp.concatenate([last_sum[:40], last_sum[40:BLK]], axis=1)
    names = ["g1", "b1", "q", "v", "proj", "g2", "b2", "out"]
    vec = {n: small[10 * k : 10 * (k + 1)] for k, n in enumerate(names)}

    return (
        layer_out.reshape(tokens.shape),
        input_grad.reshape(tokens.shape),
        vec["g1"],
        vec["b1"],
        d_qkv,
        vec["q"],
        vec["v"],
        d_proj,
        vec["proj"],
        vec["g2"],
        vec["b2"],
        d_fc,
        small[80:120],
        d_out,
        vec["out"],
    )


def solution(mesh):
    fine = Mesh(mesh.devices.reshape(SIZES), AXES)
    rows = P(DP, CTX, None)
    mat = P(AXES, None)
    vec = P(AXES)
    in_specs = (
        rows,
        P(DP),
        rows,
        vec,
        vec,
        mat,
        vec,
        vec,
        mat,
        vec,
        vec,
        vec,
        mat,
        vec,
        mat,
        vec,
    )
    out_specs = (
        rows,
        rows,
        vec,
        vec,
        mat,
        vec,
        vec,
        mat,
        vec,
        vec,
        vec,
        mat,
        vec,
        mat,
        vec,
    )
    return jax.shard_map(
        per_device, mesh=fine, in_specs=in_specs, out_specs=out_specs, check_vma=False
    )
```

```python
import functools
import math

import jax
import jax.numpy as jnp
from jax import lax
from jax.experimental import pallas as pl
from jax.experimental.pallas import tpu as pltpu
from jax.sharding import Mesh
from jax.sharding import PartitionSpec as P

HEADS = 20
NORM_EPS = 1e-05
MASKED = -1000000000.0

F32 = jnp.float32
BF16 = jnp.bfloat16

AXES = ("x", "yl", "c", "z", "yh")
SIZES = (4, 2, 2, 4, 2)
DP = ("x", "yl", "c")
CTX = ("z", "yh")
PLACE = ("z", "yh", "yl", "x", "c")

D = 1280
SPAN = 128
SEQ_GRP = 2
ROWS = SEQ_GRP * SPAN
CTX_N = 8
LEN = CTX_N * SPAN
HEAD_DIM = D // HEADS
GROUP_HEADS = 5
GROUP_W = GROUP_HEADS * HEAD_DIM
COLS = 640
BLK = 80
SCALE = 1.0 / math.sqrt(HEAD_DIM)
Q_BLOCK = 256
HEADS_W = 3 * GROUP_W
PIECE = 32
LAST = 24
MB = 1 << 20
SHORT = 1000


def place_of(dp):
    x, yl, c = dp // 4, (dp // 2) % 2, dp % 2
    return (yl * 4 + x) * 2 + c


def dot(left, right):
    return lax.dot_general(
        left, right, (((1,), (0,)), ((), ())), preferred_element_type=F32
    )


def dot_nt(left, right):
    return lax.dot_general(
        left, right, (((1,), (1,)), ((), ())), preferred_element_type=F32
    )


def norm_stats(rows):
    centre = jnp.mean(rows, axis=-1, keepdims=True)
    centred = rows - centre
    spread = jnp.mean(centred * centred, axis=-1, keepdims=True)
    scale = lax.rsqrt(spread + NORM_EPS)
    return centred * scale, scale


def norm_back(normed, scale, gain, grad):
    scaled = gain * grad
    mean_one = jnp.mean(scaled, axis=-1, keepdims=True)
    mean_two = jnp.mean(scaled * normed, axis=-1, keepdims=True)
    return (scaled - mean_one - normed * mean_two) * scale


def stack_rows(ref, *lead):
    return jnp.concatenate([ref[(*lead, place_of(dp))] for dp in range(16)], axis=0)


def params(vmem_mb):
    return pltpu.CompilerParams(vmem_limit_bytes=vmem_mb * MB)


def cost(flops, nbytes, trans=0):
    return pl.CostEstimate(
        flops=flops // SHORT, bytes_accessed=nbytes // SHORT, transcendentals=trans // SHORT
    )


def whole(shape):
    return pl.BlockSpec(shape, lambda *i: (0,) * len(shape))


def turn(block):
    return block.astype(F32).T.astype(BF16)


def allowed_of(length, first_query, key_count, query_count):
    key_pos = lax.broadcasted_iota(jnp.int32, (key_count, query_count), 0)
    query_pos = first_query + lax.broadcasted_iota(
        jnp.int32, (key_count, query_count), 1
    )
    return (key_pos <= query_pos) & (key_pos < length)


def past_of(size):
    key_pos = lax.broadcasted_iota(jnp.int32, (size, size), 0)
    return key_pos <= lax.broadcasted_iota(jnp.int32, (size, size), 1)


def with_length(key, length):
    place = lax.broadcasted_iota(jnp.int32, (LEN, HEAD_DIM), 1)
    key_pos = lax.broadcasted_iota(jnp.int32, (LEN, HEAD_DIM), 0)
    mask = jnp.where((place == 0) & (key_pos >= length), MASKED, 0.0)
    return jnp.concatenate([key.astype(F32), mask], axis=1).astype(BF16)


def with_one(query):
    place = lax.broadcasted_iota(jnp.int32, query.shape, 0)
    one = (place == 0).astype(F32)
    return jnp.concatenate([query.astype(F32) * SCALE, one], axis=0).astype(BF16)


def attend_kernel(
    len_ref, tok_ref, norm_ref, bias_ref, w_ref, qkv_ref, out_ref, lse_ref
):
    head = pl.program_id(0)

    @pl.when(head == 0)
    def _():
        weight = w_ref[...].reshape(D, HEADS_W)
        for block in range(LEN // Q_BLOCK):
            cut = slice(block * Q_BLOCK, (block + 1) * Q_BLOCK)
            normed, _ = norm_stats(tok_ref[cut].astype(F32))
            normed = (normed * norm_ref[0:1] + norm_ref[1:2]).astype(BF16)
            turned = (dot(normed, weight) + bias_ref[...]).T.astype(BF16)
            for row in range(3 * GROUP_HEADS):
                qkv_ref[row // GROUP_HEADS, row % GROUP_HEADS, :, cut] = turned[
                    row * HEAD_DIM : (row + 1) * HEAD_DIM
                ]

    query = with_one(qkv_ref[0, head])
    key = with_length(qkv_ref[1, head].astype(F32).T, len_ref[0])
    value = qkv_ref[2, head]
    past = past_of(Q_BLOCK)
    for block in range(LEN // Q_BLOCK):
        first = block * Q_BLOCK
        last = first + Q_BLOCK
        query_b = query[:, first:last]
        scores = [jnp.where(past, dot(key[first:last], query_b), MASKED)]
        values = [value[:, first:last]]
        if block:
            scores.append(dot(key[:first], query_b))
            values.append(value[:, :first])
        top = functools.reduce(
            jnp.maximum, [jnp.max(part, axis=0, keepdims=True) for part in scores]
        )
        weights = [jnp.exp(part - top) for part in scores]
        total = sum(jnp.sum(part, axis=0, keepdims=True) for part in weights)
        result = sum(dot(v, w.astype(BF16)) for v, w in zip(values, weights)) / total
        lse_ref[0, :, first:last] = top + jnp.log(total)
        result = result.astype(BF16)
        for part in range(Q_BLOCK // SPAN):
            out_ref[first // SPAN + part] = result[:, part * SPAN : (part + 1) * SPAN]


def attend_call(length, tok, norm, bias, w_qkv):
    return pl.pallas_call(
        attend_kernel,
        grid=(GROUP_HEADS,),
        in_specs=[
            pl.BlockSpec(memory_space=pltpu.SMEM),
            whole((LEN, D)),
            whole((2, D)),
            whole((1, HEADS_W)),
            whole((16, BLK, HEADS_W)),
        ],
        out_specs=[
            whole((3, GROUP_HEADS, HEAD_DIM, LEN)),
            pl.BlockSpec((CTX_N, HEAD_DIM, SPAN), lambda h: (0, h, 0)),
            pl.BlockSpec((1, 1, LEN), lambda h: (h, 0, 0)),
        ],
        out_shape=[
            jax.ShapeDtypeStruct((3, GROUP_HEADS, HEAD_DIM, LEN), BF16),
            jax.ShapeDtypeStruct((CTX_N, GROUP_W, SPAN), BF16),
            jax.ShapeDtypeStruct((GROUP_HEADS, 1, LEN), F32),
        ],
        compiler_params=params(60),
        cost_estimate=cost(
            6 * LEN * LEN * 4 * HEAD_DIM + 2 * LEN * D * HEADS_W, 8 * MB, 3 * LEN * LEN
        ),
        name="attend",
    )(length, tok, norm, bias, w_qkv)


def attend_back_kernel(len_ref, qkv_ref, grad_ref, lse_ref, g_ref, gk_ref, gv_ref):
    length = len_ref[0]
    query = qkv_ref[0, 0]
    key_t = qkv_ref[1, 0]
    key = turn(key_t)
    value = turn(qkv_ref[2, 0])
    grad = jnp.concatenate([grad_ref[p] for p in range(CTX_N)], axis=1)
    gk_ref[...] = jnp.zeros_like(gk_ref)
    gv_ref[...] = jnp.zeros_like(gv_ref)
    for block in range(LEN // Q_BLOCK):
        first = block * Q_BLOCK
        last = first + Q_BLOCK
        query_b = query[:, first:last]
        grad_b = grad[:, first:last]
        scores = dot(key[:last], query_b) * SCALE
        probs = jnp.where(
            allowed_of(length, first, last, Q_BLOCK),
            jnp.exp(scores - lse_ref[0, :, first:last]),
            0.0,
        )
        grad_probs = dot(value[:last], grad_b)
        delta = jnp.sum(probs * grad_probs, axis=0, keepdims=True)
        grad_scores = (probs * (grad_probs - delta)).astype(BF16)
        g_ref[0, 0, :, first:last] = (dot(key_t[:, :last], grad_scores) * SCALE).astype(
            BF16
        )
        gk_ref[:, :last] += dot_nt(query_b, grad_scores)
        gv_ref[:, :last] += dot_nt(grad_b, probs.astype(BF16))
    g_ref[1, 0] = (gk_ref[...] * SCALE).astype(BF16)
    g_ref[2, 0] = gv_ref[...].astype(BF16)


def attend_back_call(length, qkv, grad, lse):
    heads = pl.BlockSpec((3, 1, HEAD_DIM, LEN), lambda h: (0, h, 0, 0))
    return pl.pallas_call(
        attend_back_kernel,
        grid=(GROUP_HEADS,),
        in_specs=[
            pl.BlockSpec(memory_space=pltpu.SMEM),
            heads,
            pl.BlockSpec((CTX_N, HEAD_DIM, SPAN), lambda h: (0, h, 0)),
            pl.BlockSpec((1, 1, LEN), lambda h: (h, 0, 0)),
        ],
        out_specs=heads,
        out_shape=jax.ShapeDtypeStruct((3, GROUP_HEADS, HEAD_DIM, LEN), BF16),
        scratch_shapes=[pltpu.VMEM((HEAD_DIM, LEN), F32)] * 2,
        compiler_params=params(60),
        cost_estimate=cost(15 * LEN * LEN * 4 * HEAD_DIM, 5 * MB, 3 * LEN * LEN),
        name="attend_back",
    )(length, qkv, grad, lse)


def norm_grad_kernel(place_ref, tok_ref, w_ref, g_ref, *refs):
    *blocks, d_norm_ref = refs
    step = pl.program_id(0)
    weight = w_ref[...].reshape(D, HEADS_W)
    grads = turn(g_ref[...].reshape(HEADS_W, Q_BLOCK))
    g_norm = dot_nt(grads, weight)
    normed, _ = norm_stats(tok_ref[...].astype(F32))

    @pl.when(step == 0)
    def _():
        d_norm_ref[...] = jnp.zeros_like(d_norm_ref)

    d_norm_ref[0:1] += jnp.sum(g_norm * normed, axis=0, keepdims=True)
    d_norm_ref[1:2] += jnp.sum(g_norm, axis=0, keepdims=True)
    g_norm = g_norm.astype(BF16).reshape(2, SPAN, D)
    for by in range(4):

        @pl.when(step == (place_ref[2] + by) % 4)
        def _():
            blocks[by][...] = g_norm


def norm_grad_call(place, tok, w_qkv, g_qkv):
    return pl.pallas_call(
        norm_grad_kernel,
        grid=(LEN // Q_BLOCK,),
        in_specs=[
            pl.BlockSpec(memory_space=pltpu.SMEM),
            pl.BlockSpec((Q_BLOCK, D), lambda i: (i, 0)),
            whole((16, BLK, HEADS_W)),
            pl.BlockSpec((3, GROUP_HEADS, HEAD_DIM, Q_BLOCK), lambda i: (0, 0, 0, i)),
        ],
        out_specs=[whole((2, SPAN, D))] * 4 + [whole((2, D))],
        out_shape=[jax.ShapeDtypeStruct((2, SPAN, D), BF16)] * 4
        + [jax.ShapeDtypeStruct((2, D), F32)],
        compiler_params=params(60),
        cost_estimate=cost(2 * LEN * D * HEADS_W, 10 * MB),
        name="norm_grad",
    )(place, tok, w_qkv, g_qkv)


def qkv_grad_kernel(
    info_ref,
    tok_ref,
    norm_ref,
    g_ref,
    d_norm_ref,
    d_vec_ref,
    d_fc_bias_ref,
    keep_ref,
    give_ref,
    n1t_ref,
    small_ref,
):
    core = info_ref[SEQ_GRP + 1]
    for block in range(LEN // Q_BLOCK):
        cut = slice(block * Q_BLOCK, (block + 1) * Q_BLOCK)
        normed, _ = norm_stats(tok_ref[cut].astype(F32))
        turned = (normed * norm_ref[0:1] + norm_ref[1:2]).T.astype(BF16)
        for dp in range(16):
            n1t_ref[dp % 2, dp // 2, :, cut] = turned[dp * BLK : (dp + 1) * BLK]
    grads = g_ref[...].reshape(HEADS_W, LEN)

    d_bias = dot_nt(jnp.ones((8, LEN), BF16), grads)
    own = lax.broadcasted_iota(jnp.int32, (1, D), 1) // GROUP_W == info_ref[SEQ_GRP + 3]
    vectors = [d_norm_ref[0:1], d_norm_ref[1:2]]
    for third in (0, 2):
        part = d_bias[0:1, third * GROUP_W : (third + 1) * GROUP_W]
        vectors.append(jnp.where(own, jnp.concatenate([part] * 4, axis=1), 0.0))
    vectors += [d_vec_ref[k : k + 1] for k in range(4)]
    small = None
    for k, vector in enumerate(vectors + [d_fc_bias_ref[...]]):
        each = 10 if k < 8 else 40
        width = 128 * each
        owner = lax.broadcasted_iota(jnp.int32, (128, width), 1) // each
        mask = owner == lax.broadcasted_iota(jnp.int32, (128, width), 0)
        feature = lax.broadcasted_iota(jnp.int32, (width, 128), 0) % each
        lane = lax.broadcasted_iota(jnp.int32, (width, 128), 1)
        place = (feature + 10 * k == lane).astype(F32).astype(BF16)
        part = dot(jnp.where(mask, vector, 0.0).astype(BF16), place)
        small = part if small is None else small + part
    for dp in range(16):
        small_ref[dp % 2, dp // 2] = small[dp * 8 : (dp + 1) * 8]

    for side, ref in ((core, keep_ref), (1 - core, give_ref)):
        for half in range(2):
            rows = n1t_ref[side, 4 * half : 4 * half + 4].reshape(4 * BLK, LEN)
            ref[4 * half : 4 * half + 4, :BLK] = (
                dot_nt(rows, grads).astype(BF16).reshape(4, BLK, HEADS_W)
            )
        ref[:, BLK:] = jnp.zeros((8, 16, HEADS_W), BF16)
        ref[:, BLK : BLK + 8, :128] = small_ref[side].astype(BF16)


def qkv_grad_call(info, tok, norm, g_qkv, d_norm, d_vecs, d_fc_bias):
    half = jax.ShapeDtypeStruct((8, BLK + 16, HEADS_W), BF16)
    vmem = pl.BlockSpec(memory_space=pltpu.VMEM)
    return pl.pallas_call(
        qkv_grad_kernel,
        in_specs=[pl.BlockSpec(memory_space=pltpu.SMEM)] + [vmem] * 6,
        out_specs=[vmem, vmem],
        out_shape=[half, half],
        scratch_shapes=[
            pltpu.VMEM((2, 8, BLK, LEN), BF16),
            pltpu.VMEM((2, 8, 8, 128), F32),
        ],
        compiler_params=params(60),
        cost_estimate=cost(2 * LEN * D * HEADS_W, 8 * MB),
        name="qkv_grad",
    )(info, tok, norm, g_qkv, d_norm, d_vecs, d_fc_bias)


def norm_back_kernel(
    seq_ref, tok_ref, gain_ref, g_res_ref, own_ref, other_ref, in_grad_ref
):
    for seq, ref in ((seq_ref[0], own_ref), (1 - seq_ref[0], other_ref)):
        cut = pl.ds(pl.multiple_of(seq * SPAN, SPAN), SPAN)
        normed, scale = norm_stats(tok_ref[cut].astype(F32))
        in_grad_ref[cut] = g_res_ref[cut].astype(F32) + norm_back(
            normed, scale, gain_ref[...], ref[...].astype(F32)
        )


def norm_back_call(seq, tok, gain, g_res, own, other):
    vmem = pl.BlockSpec(memory_space=pltpu.VMEM)
    return pl.pallas_call(
        norm_back_kernel,
        in_specs=[pl.BlockSpec(memory_space=pltpu.SMEM)] + [vmem] * 5,
        out_specs=vmem,
        out_shape=jax.ShapeDtypeStruct((ROWS, D), F32),
        compiler_params=params(60),
        cost_estimate=cost(40 * ROWS * D, 4 * MB),
        name="norm_back",
    )(seq, tok, gain, g_res, own, other)


def mlp_kernel(
    info_ref,
    tok_ref,
    cot_ref,
    att_ref,
    vec_ref,
    fc_bias_ref,
    wp_ref,
    wf_ref,
    wo_ref,
    out_ref,
    g_res_ref,
    g_att_ref,
    d_vec_ref,
    d_fc_bias_ref,
    rows_ref,
    keep_ref,
    give_ref,
    n2_ref,
    g_out_ref,
    res_ref,
    acc_ref,
    gn_ref,
    wp_all_ref,
    turned_ref,
):
    step = pl.program_id(0)
    core = info_ref[SEQ_GRP + 1]
    proj_shift, gain, shift, out_shift = (vec_ref[k : k + 1] for k in range(4))

    def by_core(turned, first):
        for dp in range(16):
            turned_ref[dp % 2, place_of(dp) // 2] = turned[dp * BLK : (dp + 1) * BLK]
        keep_ref[first : first + 8] = turned_ref[core]
        give_ref[first : first + 8] = turned_ref[1 - core]

    @pl.when(step == 0)
    def _():
        turned = jnp.concatenate(
            [
                jnp.concatenate([att_ref[g, s] for g in range(4)], axis=0)
                for s in range(SEQ_GRP)
            ],
            axis=1,
        )
        att = turn(turned)
        for half in range(2):
            cut = slice(half * COLS, (half + 1) * COLS)
            pack = pack_of(half, PIECE, (BLK, CTX_N * PIECE), 0, 1)
            for dp in range(16):
                pieces = wp_ref[:, place_of(dp)].reshape(CTX_N * PIECE, COLS)
                wp_all_ref[dp * BLK : (dp + 1) * BLK, cut] = dot(pack, pieces).astype(
                    BF16
                )
        residual = tok_ref[...].astype(F32) + dot(att, wp_all_ref[...]) + proj_shift
        res_ref[...] = residual
        normed, _ = norm_stats(residual)
        normed = normed * gain + shift
        n2_ref[...] = normed.astype(BF16)
        by_core(normed.T.astype(BF16), 32)
        by_core(turned, 40)
        for seq in range(SEQ_GRP):
            cut = slice(seq * SPAN, (seq + 1) * SPAN)
            pos = info_ref[SEQ_GRP] + lax.broadcasted_iota(jnp.int32, (SPAN, D), 0)
            g_out_ref[cut] = jnp.where(
                pos < info_ref[seq], cot_ref[cut], jnp.zeros((SPAN, D), BF16)
            )
        rows_ref[:, 4 * D : 5 * D] = g_out_ref[...]
        acc_ref[...] = residual + out_shift
        gn_ref[...] = jnp.zeros_like(gn_ref)

    w_fc = jnp.concatenate([stack_rows(wf_ref, 0), stack_rows(wf_ref, 1)], axis=1)
    pre = dot(n2_ref[...], w_fc) + fc_bias_ref[...]
    root = math.sqrt(2.0 / math.pi)
    square = pre * pre
    bend = jnp.tanh(root * pre * (1.0 + 0.044715 * square))
    gate = 0.5 * (1.0 + bend)
    slope = gate + 0.5 * pre * (1.0 - bend * bend) * root * (
        1.0 + 3.0 * 0.044715 * square
    )
    act = pre * gate
    act_t = act.T.astype(BF16).reshape(2, 2, 4, BLK, ROWS)
    act = act.astype(BF16)
    for c in range(2):
        turned_ref[c] = act_t[:, c].reshape(8, BLK, ROWS)
    keep_ref[pl.ds(step * 8, 8)] = turned_ref[core]
    give_ref[pl.ds(step * 8, 8)] = turned_ref[1 - core]
    w_out = jnp.concatenate(
        [
            jnp.concatenate(
                [
                    wo_ref[z, yh, yl, 0, c, half * 40 : (half + 1) * 40]
                    for yl in range(2)
                    for c in range(2)
                    for z in range(4)
                    for yh in range(2)
                ],
                axis=0,
            )
            for half in range(2)
        ],
        axis=1,
    )
    acc_ref[...] += dot(act, w_out)
    g_act = dot_nt(g_out_ref[...], w_out)
    g_pre = (g_act * slope).astype(BF16)
    rows_ref[:, pl.ds(pl.multiple_of(step * D, D), D)] = g_pre
    d_fc_bias_ref[...] = jnp.sum(g_pre.astype(F32), axis=0, keepdims=True)
    gn_ref[...] += dot_nt(g_pre, w_fc)

    @pl.when(step == pl.num_programs(0) - 1)
    def _():
        out_ref[...] = acc_ref[...].astype(BF16)
        normed, scale = norm_stats(res_ref[...])
        g_norm = gn_ref[...]
        g_out = g_out_ref[...].astype(F32)
        g_res = (g_out + norm_back(normed, scale, gain, g_norm)).astype(BF16)
        g_res_ref[...] = g_res
        rows_ref[:, 5 * D :] = g_res
        d_vec_ref[0:1] = jnp.sum(g_res.astype(F32), axis=0, keepdims=True)
        d_vec_ref[1:2] = jnp.sum(g_norm * normed, axis=0, keepdims=True)
        d_vec_ref[2:3] = jnp.sum(g_norm, axis=0, keepdims=True)
        d_vec_ref[3:4] = jnp.sum(g_out, axis=0, keepdims=True)
        g_att = dot_nt(g_res, wp_all_ref[...])
        for seq in range(SEQ_GRP):
            turned = g_att[seq * SPAN : (seq + 1) * SPAN].T.astype(BF16)
            for g in range(4):
                g_att_ref[g, seq] = turned[g * GROUP_W : (g + 1) * GROUP_W]


def pack_of(half, piece, shape, row_dim, piece_dim):
    row = lax.broadcasted_iota(jnp.int32, shape, row_dim)
    place = lax.broadcasted_iota(jnp.int32, shape, piece_dim)
    offset = place - (piece - 10) * (row // 10) - 10 * half
    return (offset == row).astype(F32).astype(BF16)


def mlp_call(info, tok, cot, att, vecs, fc_bias, weights):
    by_ctx = weights.reshape(CTX_N, 16, 2 * BLK + PIECE, COLS)
    by_chip = weights.reshape(4, 2, 2, 4, 2, 2 * BLK + PIECE, COLS)
    rows = jax.ShapeDtypeStruct((ROWS, D), BF16)
    turned = jax.ShapeDtypeStruct((48, BLK, ROWS), BF16)
    return pl.pallas_call(
        mlp_kernel,
        grid=(4,),
        in_specs=[
            pl.BlockSpec(memory_space=pltpu.SMEM),
            whole((ROWS, D)),
            whole((ROWS, D)),
            whole((4, SEQ_GRP, GROUP_W, SPAN)),
            whole((4, D)),
            pl.BlockSpec((1, D), lambda j: (0, j)),
            pl.BlockSpec((CTX_N, 16, PIECE, COLS), lambda j: (0, 0, 5, 0)),
            pl.BlockSpec((2, 16, BLK, COLS), lambda j: (j, 0, 0, 0)),
            pl.BlockSpec(
                (4, 2, 2, 1, 2, BLK, COLS), lambda j: (0, 0, 0, j, 0, 1, 0)
            ),
        ],
        out_specs=[
            whole((ROWS, D)),
            whole((ROWS, D)),
            whole((4, SEQ_GRP, GROUP_W, SPAN)),
            whole((4, D)),
            pl.BlockSpec((1, D), lambda j: (0, j)),
            whole((ROWS, 6 * D)),
            whole((48, BLK, ROWS)),
            whole((48, BLK, ROWS)),
        ],
        out_shape=[
            rows,
            rows,
            jax.ShapeDtypeStruct((4, SEQ_GRP, GROUP_W, SPAN), BF16),
            jax.ShapeDtypeStruct((4, D), F32),
            jax.ShapeDtypeStruct((1, 4 * D), F32),
            jax.ShapeDtypeStruct((ROWS, 6 * D), BF16),
            turned,
            turned,
        ],
        scratch_shapes=[
            pltpu.VMEM((ROWS, D), BF16),
            pltpu.VMEM((ROWS, D), BF16),
            pltpu.VMEM((ROWS, D), F32),
            pltpu.VMEM((ROWS, D), F32),
            pltpu.VMEM((ROWS, D), F32),
            pltpu.VMEM((D, D), BF16),
            pltpu.VMEM((2, 8, BLK, ROWS), BF16),
        ],
        compiler_params=params(60),
        cost_estimate=cost(2 * ROWS * D * (16 * D + 2 * D), 38 * MB, 2 * ROWS * 4 * D),
        name="mlp",
    )(info, tok, cot, att, vecs, fc_bias, by_ctx, by_ctx, by_chip)


def both(ref, other_ref, axis):
    return jnp.concatenate([ref[...], other_ref[...]], axis=axis)


def fc_grad_kernel(
    n2_ref,
    n2_other_ref,
    g_ref,
    g_other_ref,
    att_ref,
    att_other_ref,
    g_res_ref,
    g_res_other_ref,
    out_ref,
    proj_ref,
):
    step = pl.program_id(0)

    @pl.when(step == 0)
    def _():
        att = both(att_ref, att_other_ref, 2).reshape(D // 2, 2 * ROWS)
        d_w = dot(att, both(g_res_ref, g_res_other_ref, 0)).astype(BF16)
        for chip in range(8):
            piece = None
            for half in range(2):
                unpack = pack_of(half, LAST, (CTX_N * LAST, BLK), 1, 0)
                part = dot(
                    unpack,
                    d_w[
                        chip * BLK : (chip + 1) * BLK, half * COLS : (half + 1) * COLS
                    ],
                )
                piece = part if piece is None else piece + part
            proj_ref[:, chip] = piece.astype(BF16).reshape(CTX_N, LAST, COLS)

    left = both(n2_ref, n2_other_ref, 2).reshape(D // 2, 2 * ROWS)
    d_w = dot(left, both(g_ref, g_other_ref, 0)).astype(BF16)
    for chip in range(8):
        for part in range(2):
            out_ref[chip % 4, part, chip // 4, :BLK] = d_w[
                chip * BLK : (chip + 1) * BLK, part * COLS : (part + 1) * COLS
            ]
            out_ref[chip % 4, part, chip // 4, BLK:] = proj_ref[2 * step + part, chip]


def fc_grad_call(turned, turned_other, rows, rows_other):
    n2_block = pl.BlockSpec((8, BLK, ROWS), lambda j: (4, 0, 0))
    g_block = pl.BlockSpec((ROWS, D), lambda j: (0, j))
    att_block = pl.BlockSpec((8, BLK, ROWS), lambda j: (5, 0, 0))
    g_res_block = pl.BlockSpec((ROWS, D), lambda j: (0, 5))
    last = BLK + LAST
    return pl.pallas_call(
        fc_grad_kernel,
        grid=(4,),
        in_specs=[
            n2_block,
            n2_block,
            g_block,
            g_block,
            att_block,
            att_block,
            g_res_block,
            g_res_block,
        ],
        out_specs=pl.BlockSpec((4, 2, 2, last, COLS), lambda j: (0, j, 0, 0, 0)),
        out_shape=jax.ShapeDtypeStruct((4, 8, 2, last, COLS), BF16),
        scratch_shapes=[pltpu.VMEM((CTX_N, 8, LAST, COLS), BF16)],
        compiler_params=params(60),
        cost_estimate=cost(10 * ROWS * D * D, 16 * MB),
        name="fc_grad",
    )(
        turned, turned_other, rows, rows_other, turned, turned_other, rows, rows_other
    )


def owners_kernel(place_ref, in_ref, *refs):
    *blocks, held = refs
    step = pl.program_id(0)
    rows = 8 * BLK
    row = lax.broadcasted_iota(jnp.int32, (rows, rows), 0)
    source = lax.broadcasted_iota(jnp.int32, (rows, rows), 1)
    wanted = (row // 10) % 8 * BLK + row // BLK * 10 + row % 10
    turn_rows = (source == wanted).astype(F32).astype(BF16)
    result = dot(turn_rows, in_ref[:, 0, :BLK].reshape(rows, COLS)).astype(BF16)
    for z in range(4):
        for yh in range(2):
            ctx = z * 2 + yh
            held[2 * yh + step, z, :BLK] = result[ctx * BLK : (ctx + 1) * BLK]
            held[2 * yh + step, z, BLK:] = in_ref[ctx, 0, BLK:]

    @pl.when(step == 1)
    def _():
        for by in range(4):
            blocks[by][...] = held[(place_ref[1] + by) % 4]


def owners_call(place, array):
    last = BLK + LAST
    return pl.pallas_call(
        owners_kernel,
        grid=(2,),
        in_specs=[
            pl.BlockSpec(memory_space=pltpu.SMEM),
            pl.BlockSpec((8, 1, last, COLS), lambda i: (0, i, 0, 0)),
        ],
        out_specs=[whole((4, last, COLS))] * 4,
        out_shape=[jax.ShapeDtypeStruct((4, last, COLS), BF16)] * 4,
        scratch_shapes=[pltpu.VMEM((4, 4, last, COLS), BF16)],
        compiler_params=params(60),
        cost_estimate=cost(4 * 640**3, 5 * MB),
        name="owners",
    )(place, array)


def out_grad_kernel(
    info_ref, act_ref, act_other_ref, g_ref, g_other_ref, out_ref, first_ref
):
    act = both(act_ref, act_other_ref, 2).reshape(8 * BLK, 2 * ROWS)
    d_w = dot(act, both(g_ref, g_other_ref, 0)).astype(BF16)
    for yl in range(2):
        for z in range(4):
            for yh in range(2):
                row = yl * 4 * BLK + (z * 2 + yh) * 40
                out_ref[yh, yl, z, 0, :40] = d_w[row : row + 40, :COLS]
                out_ref[yh, yl, z, 0, 40:] = d_w[row : row + 40, COLS:]
    first = info_ref[SEQ_GRP + 2]
    first_ref[...] = out_ref[first // 2, first % 2]


def out_grad_call(info, turned, turned_other, rows, rows_other):
    act_block = pl.BlockSpec((8, BLK, ROWS), lambda j: (j, 0, 0))
    g_block = pl.BlockSpec((ROWS, D), lambda j: (0, 4))
    return pl.pallas_call(
        out_grad_kernel,
        grid=(4,),
        in_specs=[
            pl.BlockSpec(memory_space=pltpu.SMEM),
            act_block,
            act_block,
            g_block,
            g_block,
        ],
        out_specs=[
            pl.BlockSpec((2, 2, 4, 1, BLK, COLS), lambda j: (0, 0, 0, j, 0, 0)),
            pl.BlockSpec((4, 1, BLK, COLS), lambda j: (0, j, 0, 0)),
        ],
        out_shape=[
            jax.ShapeDtypeStruct((2, 2, 4, 4, BLK, COLS), BF16),
            jax.ShapeDtypeStruct((4, 4, BLK, COLS), BF16),
        ],
        compiler_params=params(60),
        cost_estimate=cost(8 * ROWS * D * D, 16 * MB),
        name="out_grad",
    )(info, turned, turned_other, rows, rows_other)


def add_kernel(place_ref, arrived_ref, terms_ref, out_ref):
    del place_ref
    total = arrived_ref[...].astype(F32) + terms_ref[0].astype(F32)
    out_ref[...] = total.astype(BF16)


def add_call(place, at, arrived, terms):
    tall, rows, cols = arrived.shape
    part = 8
    block = pl.BlockSpec((part, rows, cols), lambda i, place: (i, 0, 0))
    nbytes = 6 * tall * rows * cols
    return pl.pallas_call(
        add_kernel,
        grid_spec=pltpu.PrefetchScalarGridSpec(
            num_scalar_prefetch=1,
            grid=(tall // part,),
            in_specs=[
                block,
                pl.BlockSpec(
                    (1, part, rows, cols), lambda i, place: (place[at], i, 0, 0)
                ),
            ],
            out_specs=[block],
        ),
        out_shape=[jax.ShapeDtypeStruct(arrived.shape, BF16)],
        compiler_params=params(60),
        cost_estimate=cost(nbytes // 4, nbytes),
        name="add_blocks",
    )(place, arrived, terms)


def add_four_kernel(at, place_ref, *refs):
    *blocks, held = refs[4:]
    total = refs[0][...].astype(F32)
    for ref in refs[1:4]:
        total = total + ref[...].astype(F32)
    held[...] = total.astype(BF16)
    for by in range(4):
        blocks[by][...] = held[(place_ref[at] + by) % 4]


def add_four_call(place, at, parts):
    vmem = pl.BlockSpec(memory_space=pltpu.VMEM)
    shape = parts[0].shape
    nbytes = 10 * math.prod(shape)
    return pl.pallas_call(
        functools.partial(add_four_kernel, at),
        in_specs=[pl.BlockSpec(memory_space=pltpu.SMEM)] + [vmem] * 4,
        out_specs=[vmem] * 4,
        out_shape=[jax.ShapeDtypeStruct(shape[1:], BF16)] * 4,
        scratch_shapes=[pltpu.VMEM(shape, BF16)],
        compiler_params=params(60),
        cost_estimate=cost(nbytes // 4, nbytes),
        name="add_four",
    )(place, *parts)


def ring_perm(axis):
    pairs = []
    for core in range(2):
        for pos in range(4):
            to = (pos + (1 if core == 0 else -1)) % 4
            if axis == "x":
                index = lambda p: p * 2 + core
            elif axis == "z":
                index = lambda p: core * 4 + p
            else:
                index = lambda p: ((p % 2) * 2 + core) * 2 + p // 2
            pairs.append((index(pos), index(to)))
    return {"x": ("x", "c"), "z": ("c", "z"), "y": ("yl", "c", "yh")}[axis], pairs


def swap_cores(array):
    return lax.ppermute(array, "c", [(0, 1), (1, 0)])


def shift_perm(axis, by):
    if axis != "y":
        return axis, [(p, (p + by) % 4) for p in range(4)]
    index = lambda p: (p % 2) * 2 + p // 2
    return ("yl", "yh"), [(index(p), index((p + by) % 4)) for p in range(4)]


def places():
    way = 1 - 2 * lax.axis_index("c")
    y = 2 * lax.axis_index("yh") + lax.axis_index("yl")
    ring = [(y - way * by) % 4 for by in (2, 3, 4, 1)]
    numbers = [lax.axis_index("x"), y, lax.axis_index("z"), *ring]
    return jnp.stack(numbers).astype(jnp.int32)


AT = {"x": 0, "y": 1, "z": 2, "ring": 3}


def directly(blocks, axis):
    return [blocks[0]] + [
        lax.ppermute(blocks[by], *shift_perm(axis, by)) for by in (1, 2, 3)
    ]


def total_of(parts):
    return sum(part.astype(F32) for part in parts)


def tie(first, second):
    return lax.optimization_barrier((first, second))


def per_device(
    tokens,
    lengths,
    cotangent,
    ln1_gain,
    ln1_bias,
    w_qkv,
    q_bias,
    v_bias,
    w_proj,
    proj_bias,
    ln2_gain,
    ln2_bias,
    w_fc,
    fc_bias,
    w_out,
    out_bias,
):
    ctx_rank = lax.axis_index(CTX)
    core = lax.axis_index("c")
    seq_rank = lax.axis_index("yh")
    head_group = lax.axis_index("z")
    tok = tokens.reshape(ROWS, D)
    cot = cotangent.reshape(ROWS, D)

    def exchange(array):
        return lax.all_to_all(array, CTX, 0, 0, tiled=True)

    groups = w_qkv.reshape(10, 3, 4, GROUP_W).transpose(2, 0, 1, 3)
    groups = groups.reshape(4, 10, HEADS_W)
    vec_one = jnp.concatenate([ln1_gain, ln1_bias, q_bias, v_bias])
    vec_one = jnp.pad(vec_one[None, None], ((0, 0), (0, 0), (0, HEADS_W - 40)))
    groups = jnp.concatenate([groups, jnp.broadcast_to(vec_one, (4, 1, HEADS_W))], axis=1)
    groups = jnp.broadcast_to(groups[:, None], (4, 2, 11, HEADS_W))
    w_cols = w_fc.reshape(10, CTX_N, COLS).transpose(1, 0, 2)
    w_cols = jnp.pad(w_cols, ((0, 0), (0, 0), (0, HEADS_W - COLS)))
    groups = groups.reshape(CTX_N, 11, HEADS_W)
    shards = exchange(jnp.concatenate([groups, w_cols], axis=1))

    vec_two = jnp.concatenate([proj_bias, ln2_gain, ln2_bias, out_bias, fc_bias])
    vec_two = jnp.pad(vec_two[None], ((0, PIECE - 21), (0, COLS - 80)))
    part = jnp.concatenate(
        [
            shards[:, 11:, :COLS].reshape(BLK, COLS),
            w_out.reshape(40, 2, COLS).transpose(1, 0, 2).reshape(BLK, COLS),
            w_proj.reshape(10, 2, COLS).transpose(1, 0, 2).reshape(20, COLS),
            vec_two,
        ],
        axis=0,
    )
    part, tokens = tie(part, tokens)
    weights = lax.all_gather(part, PLACE, axis=0, tiled=False)

    theirs = lax.dynamic_index_in_dim(tokens, 1 - seq_rank, 0, False)
    mine = lax.dynamic_index_in_dim(tokens, seq_rank, 0, False)
    theirs = lax.ppermute(theirs, "yh", [(0, 1), (1, 0)])
    sequence = jnp.where(
        seq_rank == 0, jnp.stack([mine, theirs]), jnp.stack([theirs, mine])
    )
    sequence = jnp.broadcast_to(sequence[None], (4, 2, SPAN, D))
    sequence = lax.all_to_all(sequence, "z", 0, 0, tiled=True).reshape(LEN, D)
    sequence, shards = tie(sequence, shards)

    w_group = jnp.concatenate(
        [shards[:, :10].reshape(BLK, HEADS_W), shards[:, 10]], axis=0
    )
    w_group = jnp.broadcast_to(w_group[None], (8, BLK + 8, HEADS_W))
    w_group = lax.all_to_all(w_group, ("x", "yl"), 0, 0, tiled=True)
    other = swap_cores(w_group)
    first = jnp.where(core == 0, w_group, other)
    second = jnp.where(core == 0, other, w_group)
    w_group = jnp.stack([first, second], axis=1).reshape(16, BLK + 8, HEADS_W)

    vecs = w_group[:, BLK:, :40].reshape(128, 4, 10).transpose(1, 0, 2)
    vecs = vecs.reshape(4, D).astype(F32)
    own = lax.dynamic_slice_in_dim(vecs[2:], head_group * GROUP_W, GROUP_W, 1)
    bias = jnp.concatenate([own[0:1], jnp.zeros((1, GROUP_W), F32), own[1:2]], axis=1)
    length = lax.dynamic_slice_in_dim(lengths, seq_rank, 1)
    qkv, att, lse = attend_call(length, sequence, vecs[:2], bias, w_group)
    att = exchange(att).reshape(4, SEQ_GRP, GROUP_W, SPAN)

    more = weights[:, 2 * BLK + 20, :80].reshape(4, 2, 2, 4, 2, 80)
    more = more.transpose(3, 2, 4, 0, 1, 5).reshape(128, 80).astype(F32)
    fc_shift = more[:, 40:].reshape(1, 4 * D)
    more = more[:, :40].reshape(128, 4, 10).transpose(1, 0, 2).reshape(4, D)
    place = places()
    info = jnp.stack([ctx_rank * SPAN, core, place[6], head_group]).astype(jnp.int32)
    info = jnp.concatenate([lengths, info])
    layer_out, g_res, g_att, d_vecs, d_fc_bias, rows, turned, turned_give = mlp_call(
        info, tok, cot, att, more, fc_shift, weights
    )

    turned_other = swap_cores(turned_give)
    rows_other = swap_cores(rows)
    g_att = exchange(g_att.reshape(CTX_N, GROUP_W, SPAN))
    d_fc = fc_grad_call(turned, turned_other, rows, rows_other)
    d_fc, (rows_other, g_att) = tie(d_fc, (rows_other, g_att))
    d_fc = lax.psum_scatter(d_fc, "x", scatter_dimension=0, tiled=False)
    d_out, sent = out_grad_call(info, turned, turned_other, rows, rows_other)
    d_out = d_out.reshape(4, 16, BLK, COLS)
    sent = sent.reshape(16, BLK, COLS)
    flight = lax.ppermute(sent, *ring_perm("y"))

    def ring_step(step, arrived):
        return add_call(place, AT["ring"] + step, arrived, d_out)[0]

    g_qkv = attend_back_call(length, qkv, g_att, lse)
    flight, g_qkv = tie(flight, g_qkv)
    sent, g_qkv = tie(ring_step(0, flight), g_qkv)
    flight = lax.ppermute(sent, *ring_perm("y"))
    *g_norm, d_norm = norm_grad_call(place, sequence, w_group, g_qkv)
    g_norm = directly(g_norm, "z")
    d_norm, g_qkv = tie(d_norm, g_qkv)
    group_keep, group_give = qkv_grad_call(
        info, sequence, vecs[:2], g_qkv, d_norm, d_vecs, d_fc_bias
    )
    flight, (group_keep, group_give) = tie(flight, (group_keep, group_give))
    sent, (group_keep, group_give) = tie(ring_step(1, flight), (group_keep, group_give))
    flight = lax.ppermute(sent, *ring_perm("y"))
    group_given = swap_cores(group_give)
    d_group = (group_keep.astype(F32) + group_given.astype(F32)).astype(BF16)
    d_group = lax.all_to_all(d_group, ("x", "yl"), 0, 0, tiled=True)

    d_fc = list(owners_call(place, d_fc))
    fc_parts = directly(d_fc, "y")
    d_fc[0], flight = tie(d_fc[0], flight)
    d_out = ring_step(2, flight)
    d_out = lax.all_to_all(d_out, ("z", "x"), 0, 0, tiled=True)
    _, g_norm = tie(fc_parts, g_norm)
    g_norm = total_of(g_norm).astype(BF16)
    g_own = lax.dynamic_index_in_dim(g_norm, seq_rank, 0, False)
    g_give = lax.dynamic_index_in_dim(g_norm, 1 - seq_rank, 0, False)
    g_other = lax.ppermute(g_give, "yh", [(0, 1), (1, 0)])
    d_group = jnp.sum(d_group.astype(F32), axis=0).astype(BF16)
    d_group = jnp.concatenate(
        [d_group[:BLK].reshape(CTX_N, 10, HEADS_W), d_group[BLK : BLK + 8, None]],
        axis=1,
    )
    d_fc = add_four_call(place, AT["z"], fc_parts)
    d_fc, d_out = tie(d_fc, d_out)
    fc_parts = directly(d_fc, "z")
    d_group = exchange(d_group)
    _, g_other = tie(d_fc[0], g_other)
    input_grad = norm_back_call(
        seq_rank.astype(jnp.int32)[None], tok, vecs[:1], g_res, g_own, g_other
    )
    last_sum = jnp.sum(d_out.astype(F32), axis=0)
    d_fc = total_of(fc_parts)
    d_fc, d_group = tie(d_fc, d_group)
    d_group = d_group.astype(F32)
    d_qkv = jnp.sum(d_group[:, :10].reshape(4, 2, 10, HEADS_W), axis=1)
    d_qkv = d_qkv.reshape(4, 10, 3, GROUP_W)
    d_qkv = d_qkv.transpose(1, 2, 0, 3).reshape(10, 3 * D)
    small = jnp.sum(d_group[:, 10, :120], axis=0)

    d_proj = d_fc[BLK : BLK + 20].reshape(2, 10, COLS).transpose(1, 0, 2).reshape(10, D)
    d_fc = d_fc[:BLK].reshape(CTX_N, 10, COLS).transpose(1, 0, 2)
    d_fc = d_fc.reshape(10, CTX_N * COLS)
    d_out = jnp.concatenate([last_sum[:40], last_sum[40:BLK]], axis=1)
    names = ["g1", "b1", "q", "v", "proj", "g2", "b2", "out"]
    vec = {n: small[10 * k : 10 * (k + 1)] for k, n in enumerate(names)}

    return (
        layer_out.reshape(tokens.shape),
        input_grad.reshape(tokens.shape),
        vec["g1"],
        vec["b1"],
        d_qkv,
        vec["q"],
        vec["v"],
        d_proj,
        vec["proj"],
        vec["g2"],
        vec["b2"],
        d_fc,
        small[80:120],
        d_out,
        vec["out"],
    )


def solution(mesh):
    fine = Mesh(mesh.devices.reshape(SIZES), AXES)
    rows = P(DP, CTX, None)
    mat = P(AXES, None)
    vec = P(AXES)
    in_specs = (
        rows,
        P(DP),
        rows,
        vec,
        vec,
        mat,
        vec,
        vec,
        mat,
        vec,
        vec,
        vec,
        mat,
        vec,
        mat,
        vec,
    )
    out_specs = (
        rows,
        rows,
        vec,
        vec,
        mat,
        vec,
        vec,
        mat,
        vec,
        vec,
        vec,
        mat,
        vec,
        mat,
        vec,
    )
    return jax.shard_map(
        per_device, mesh=fine, in_specs=in_specs, out_specs=out_specs, check_vma=False
    )
```

```python
import functools
import math

import jax
import jax.numpy as jnp
from jax import lax
from jax.experimental import pallas as pl
from jax.experimental.pallas import tpu as pltpu
from jax.sharding import Mesh
from jax.sharding import PartitionSpec as P

HEADS = 20
NORM_EPS = 1e-05
MASKED = -1000000000.0

F32 = jnp.float32
BF16 = jnp.bfloat16

AXES = ("x", "yl", "c", "z", "yh")
SIZES = (4, 2, 2, 4, 2)
DP = ("x", "yl", "c")
CTX = ("z", "yh")
PLACE = ("z", "yh", "yl", "x", "c")

D = 1280
SPAN = 128
SEQ_GRP = 2
ROWS = SEQ_GRP * SPAN
CTX_N = 8
LEN = CTX_N * SPAN
HEAD_DIM = D // HEADS
GROUP_HEADS = 5
GROUP_W = GROUP_HEADS * HEAD_DIM
COLS = 640
BLK = 80
SCALE = 1.0 / math.sqrt(HEAD_DIM)
Q_BLOCK = 256
QKV_BLOCK = 512
HEADS_W = 3 * GROUP_W
PIECE = 32
LAST = 24
MB = 1 << 20
SHORT = 1000


def place_of(dp):
    x, yl, c = dp // 4, (dp // 2) % 2, dp % 2
    return (yl * 4 + x) * 2 + c


def dot(left, right):
    return lax.dot_general(
        left, right, (((1,), (0,)), ((), ())), preferred_element_type=F32
    )


def dot_nt(left, right):
    return lax.dot_general(
        left, right, (((1,), (1,)), ((), ())), preferred_element_type=F32
    )


def norm_stats(rows):
    centre = jnp.mean(rows, axis=-1, keepdims=True)
    centred = rows - centre
    spread = jnp.mean(centred * centred, axis=-1, keepdims=True)
    scale = lax.rsqrt(spread + NORM_EPS)
    return centred * scale, scale


def norm_back(normed, scale, gain, grad):
    scaled = gain * grad
    mean_one = jnp.mean(scaled, axis=-1, keepdims=True)
    mean_two = jnp.mean(scaled * normed, axis=-1, keepdims=True)
    return (scaled - mean_one - normed * mean_two) * scale


def stack_rows(ref, *lead):
    return jnp.concatenate([ref[(*lead, place_of(dp))] for dp in range(16)], axis=0)


def params(vmem_mb):
    return pltpu.CompilerParams(vmem_limit_bytes=vmem_mb * MB)


def cost(flops, nbytes, trans=0):
    return pl.CostEstimate(
        flops=flops // SHORT, bytes_accessed=nbytes // SHORT, transcendentals=trans // SHORT
    )


def whole(shape):
    return pl.BlockSpec(shape, lambda *i: (0,) * len(shape))


def turn(block):
    return block.astype(F32).T.astype(BF16)


def allowed_of(length, first_query, key_count, query_count):
    key_pos = lax.broadcasted_iota(jnp.int32, (key_count, query_count), 0)
    query_pos = first_query + lax.broadcasted_iota(
        jnp.int32, (key_count, query_count), 1
    )
    return (key_pos <= query_pos) & (key_pos < length)


def past_of(size):
    key_pos = lax.broadcasted_iota(jnp.int32, (size, size), 0)
    return key_pos <= lax.broadcasted_iota(jnp.int32, (size, size), 1)


def with_length(key, length):
    place = lax.broadcasted_iota(jnp.int32, (LEN, HEAD_DIM), 1)
    key_pos = lax.broadcasted_iota(jnp.int32, (LEN, HEAD_DIM), 0)
    mask = jnp.where((place == 0) & (key_pos >= length), MASKED, 0.0)
    return jnp.concatenate([key.astype(F32), mask], axis=1).astype(BF16)


def with_one(query):
    place = lax.broadcasted_iota(jnp.int32, query.shape, 0)
    one = (place == 0).astype(F32)
    return jnp.concatenate([query.astype(F32) * SCALE, one], axis=0).astype(BF16)


def attend_kernel(
    len_ref, tok_ref, norm_ref, bias_ref, w_ref, qkv_ref, out_ref, lse_ref
):
    head = pl.program_id(0)

    @pl.when(head == 0)
    def _():
        weight = w_ref[...].reshape(D, HEADS_W)
        for block in range(LEN // QKV_BLOCK):
            cut = slice(block * QKV_BLOCK, (block + 1) * QKV_BLOCK)
            normed, _ = norm_stats(tok_ref[cut].astype(F32))
            normed = (normed * norm_ref[0:1] + norm_ref[1:2]).astype(BF16)
            turned = (dot(normed, weight) + bias_ref[...]).T.astype(BF16)
            for row in range(3 * GROUP_HEADS):
                qkv_ref[row // GROUP_HEADS, row % GROUP_HEADS, :, cut] = turned[
                    row * HEAD_DIM : (row + 1) * HEAD_DIM
                ]

    query = with_one(qkv_ref[0, head])
    key = with_length(qkv_ref[1, head].astype(F32).T, len_ref[0])
    value = qkv_ref[2, head]
    past = past_of(Q_BLOCK)
    for block in range(LEN // Q_BLOCK):
        first = block * Q_BLOCK
        last = first + Q_BLOCK
        query_b = query[:, first:last]
        scores = [jnp.where(past, dot(key[first:last], query_b), MASKED)]
        values = [value[:, first:last]]
        if block:
            scores.append(dot(key[:first], query_b))
            values.append(value[:, :first])
        top = functools.reduce(
            jnp.maximum, [jnp.max(part, axis=0, keepdims=True) for part in scores]
        )
        weights = [jnp.exp(part - top) for part in scores]
        total = sum(jnp.sum(part, axis=0, keepdims=True) for part in weights)
        result = sum(dot(v, w.astype(BF16)) for v, w in zip(values, weights)) / total
        lse_ref[0, :, first:last] = top + jnp.log(total)
        result = result.astype(BF16)
        for part in range(Q_BLOCK // SPAN):
            out_ref[first // SPAN + part] = result[:, part * SPAN : (part + 1) * SPAN]


def attend_call(length, tok, norm, bias, w_qkv):
    return pl.pallas_call(
        attend_kernel,
        grid=(GROUP_HEADS,),
        in_specs=[
            pl.BlockSpec(memory_space=pltpu.SMEM),
            whole((LEN, D)),
            whole((2, D)),
            whole((1, HEADS_W)),
            whole((16, BLK, HEADS_W)),
        ],
        out_specs=[
            whole((3, GROUP_HEADS, HEAD_DIM, LEN)),
            pl.BlockSpec((CTX_N, HEAD_DIM, SPAN), lambda h: (0, h, 0)),
            pl.BlockSpec((1, 1, LEN), lambda h: (h, 0, 0)),
        ],
        out_shape=[
            jax.ShapeDtypeStruct((3, GROUP_HEADS, HEAD_DIM, LEN), BF16),
            jax.ShapeDtypeStruct((CTX_N, GROUP_W, SPAN), BF16),
            jax.ShapeDtypeStruct((GROUP_HEADS, 1, LEN), F32),
        ],
        compiler_params=params(60),
        cost_estimate=cost(
            6 * LEN * LEN * 4 * HEAD_DIM + 2 * LEN * D * HEADS_W, 8 * MB, 3 * LEN * LEN
        ),
        name="attend",
    )(length, tok, norm, bias, w_qkv)


def attend_back_kernel(len_ref, qkv_ref, grad_ref, lse_ref, g_ref, gk_ref, gv_ref):
    length = len_ref[0]
    query = qkv_ref[0, 0]
    key_t = qkv_ref[1, 0]
    key = turn(key_t)
    value = turn(qkv_ref[2, 0])
    grad = jnp.concatenate([grad_ref[p] for p in range(CTX_N)], axis=1)
    gk_ref[...] = jnp.zeros_like(gk_ref)
    gv_ref[...] = jnp.zeros_like(gv_ref)
    for block in range(LEN // Q_BLOCK):
        first = block * Q_BLOCK
        last = first + Q_BLOCK
        query_b = query[:, first:last]
        grad_b = grad[:, first:last]
        scores = dot(key[:last], query_b) * SCALE
        probs = jnp.where(
            allowed_of(length, first, last, Q_BLOCK),
            jnp.exp(scores - lse_ref[0, :, first:last]),
            0.0,
        )
        grad_probs = dot(value[:last], grad_b)
        delta = jnp.sum(probs * grad_probs, axis=0, keepdims=True)
        grad_scores = (probs * (grad_probs - delta)).astype(BF16)
        g_ref[0, 0, :, first:last] = (dot(key_t[:, :last], grad_scores) * SCALE).astype(
            BF16
        )
        gk_ref[:, :last] += dot_nt(query_b, grad_scores)
        gv_ref[:, :last] += dot_nt(grad_b, probs.astype(BF16))
    g_ref[1, 0] = (gk_ref[...] * SCALE).astype(BF16)
    g_ref[2, 0] = gv_ref[...].astype(BF16)


def attend_back_call(length, qkv, grad, lse):
    heads = pl.BlockSpec((3, 1, HEAD_DIM, LEN), lambda h: (0, h, 0, 0))
    return pl.pallas_call(
        attend_back_kernel,
        grid=(GROUP_HEADS,),
        in_specs=[
            pl.BlockSpec(memory_space=pltpu.SMEM),
            heads,
            pl.BlockSpec((CTX_N, HEAD_DIM, SPAN), lambda h: (0, h, 0)),
            pl.BlockSpec((1, 1, LEN), lambda h: (h, 0, 0)),
        ],
        out_specs=heads,
        out_shape=jax.ShapeDtypeStruct((3, GROUP_HEADS, HEAD_DIM, LEN), BF16),
        scratch_shapes=[pltpu.VMEM((HEAD_DIM, LEN), F32)] * 2,
        compiler_params=params(60),
        cost_estimate=cost(15 * LEN * LEN * 4 * HEAD_DIM, 5 * MB, 3 * LEN * LEN),
        name="attend_back",
    )(length, qkv, grad, lse)


def norm_grad_kernel(place_ref, tok_ref, w_ref, g_ref, *refs):
    *blocks, d_norm_ref = refs
    step = pl.program_id(0)
    weight = w_ref[...].reshape(D, HEADS_W)
    grads = turn(g_ref[...].reshape(HEADS_W, Q_BLOCK))
    g_norm = dot_nt(grads, weight)
    normed, _ = norm_stats(tok_ref[...].astype(F32))

    @pl.when(step == 0)
    def _():
        d_norm_ref[...] = jnp.zeros_like(d_norm_ref)

    d_norm_ref[0:1] += jnp.sum(g_norm * normed, axis=0, keepdims=True)
    d_norm_ref[1:2] += jnp.sum(g_norm, axis=0, keepdims=True)
    g_norm = g_norm.astype(BF16).reshape(2, SPAN, D)
    for by in range(4):

        @pl.when(step == (place_ref[2] + by) % 4)
        def _():
            blocks[by][...] = g_norm


def norm_grad_call(place, tok, w_qkv, g_qkv):
    return pl.pallas_call(
        norm_grad_kernel,
        grid=(LEN // Q_BLOCK,),
        in_specs=[
            pl.BlockSpec(memory_space=pltpu.SMEM),
            pl.BlockSpec((Q_BLOCK, D), lambda i: (i, 0)),
            whole((16, BLK, HEADS_W)),
            pl.BlockSpec((3, GROUP_HEADS, HEAD_DIM, Q_BLOCK), lambda i: (0, 0, 0, i)),
        ],
        out_specs=[whole((2, SPAN, D))] * 4 + [whole((2, D))],
        out_shape=[jax.ShapeDtypeStruct((2, SPAN, D), BF16)] * 4
        + [jax.ShapeDtypeStruct((2, D), F32)],
        compiler_params=params(60),
        cost_estimate=cost(2 * LEN * D * HEADS_W, 10 * MB),
        name="norm_grad",
    )(place, tok, w_qkv, g_qkv)


def qkv_grad_kernel(
    info_ref,
    tok_ref,
    norm_ref,
    g_ref,
    d_norm_ref,
    d_vec_ref,
    d_fc_bias_ref,
    keep_ref,
    give_ref,
    n1t_ref,
    small_ref,
):
    core = info_ref[SEQ_GRP + 1]
    for block in range(LEN // Q_BLOCK):
        cut = slice(block * Q_BLOCK, (block + 1) * Q_BLOCK)
        normed, _ = norm_stats(tok_ref[cut].astype(F32))
        turned = (normed * norm_ref[0:1] + norm_ref[1:2]).T.astype(BF16)
        for dp in range(16):
            n1t_ref[dp % 2, dp // 2, :, cut] = turned[dp * BLK : (dp + 1) * BLK]
    grads = g_ref[...].reshape(HEADS_W, LEN)

    d_bias = dot_nt(jnp.ones((8, LEN), BF16), grads)
    own = lax.broadcasted_iota(jnp.int32, (1, D), 1) // GROUP_W == info_ref[SEQ_GRP + 3]
    vectors = [d_norm_ref[0:1], d_norm_ref[1:2]]
    for third in (0, 2):
        part = d_bias[0:1, third * GROUP_W : (third + 1) * GROUP_W]
        vectors.append(jnp.where(own, jnp.concatenate([part] * 4, axis=1), 0.0))
    vectors += [d_vec_ref[k : k + 1] for k in range(4)]
    small = None
    for k, vector in enumerate(vectors + [d_fc_bias_ref[...]]):
        each = 10 if k < 8 else 40
        width = 128 * each
        owner = lax.broadcasted_iota(jnp.int32, (128, width), 1) // each
        mask = owner == lax.broadcasted_iota(jnp.int32, (128, width), 0)
        feature = lax.broadcasted_iota(jnp.int32, (width, 128), 0) % each
        lane = lax.broadcasted_iota(jnp.int32, (width, 128), 1)
        place = (feature + 10 * k == lane).astype(F32).astype(BF16)
        part = dot(jnp.where(mask, vector, 0.0).astype(BF16), place)
        small = part if small is None else small + part
    for dp in range(16):
        small_ref[dp % 2, dp // 2] = small[dp * 8 : (dp + 1) * 8]

    for side, ref in ((core, keep_ref), (1 - core, give_ref)):
        for half in range(2):
            rows = n1t_ref[side, 4 * half : 4 * half + 4].reshape(4 * BLK, LEN)
            ref[4 * half : 4 * half + 4, :BLK] = (
                dot_nt(rows, grads).astype(BF16).reshape(4, BLK, HEADS_W)
            )
        ref[:, BLK:] = jnp.zeros((8, 16, HEADS_W), BF16)
        ref[:, BLK : BLK + 8, :128] = small_ref[side].astype(BF16)


def qkv_grad_call(info, tok, norm, g_qkv, d_norm, d_vecs, d_fc_bias):
    half = jax.ShapeDtypeStruct((8, BLK + 16, HEADS_W), BF16)
    vmem = pl.BlockSpec(memory_space=pltpu.VMEM)
    return pl.pallas_call(
        qkv_grad_kernel,
        in_specs=[pl.BlockSpec(memory_space=pltpu.SMEM)] + [vmem] * 6,
        out_specs=[vmem, vmem],
        out_shape=[half, half],
        scratch_shapes=[
            pltpu.VMEM((2, 8, BLK, LEN), BF16),
            pltpu.VMEM((2, 8, 8, 128), F32),
        ],
        compiler_params=params(60),
        cost_estimate=cost(2 * LEN * D * HEADS_W, 8 * MB),
        name="qkv_grad",
    )(info, tok, norm, g_qkv, d_norm, d_vecs, d_fc_bias)


def norm_back_kernel(
    seq_ref, tok_ref, gain_ref, g_res_ref, own_ref, other_ref, in_grad_ref
):
    for seq, ref in ((seq_ref[0], own_ref), (1 - seq_ref[0], other_ref)):
        cut = pl.ds(pl.multiple_of(seq * SPAN, SPAN), SPAN)
        normed, scale = norm_stats(tok_ref[cut].astype(F32))
        in_grad_ref[cut] = g_res_ref[cut].astype(F32) + norm_back(
            normed, scale, gain_ref[...], ref[...].astype(F32)
        )


def norm_back_call(seq, tok, gain, g_res, own, other):
    vmem = pl.BlockSpec(memory_space=pltpu.VMEM)
    return pl.pallas_call(
        norm_back_kernel,
        in_specs=[pl.BlockSpec(memory_space=pltpu.SMEM)] + [vmem] * 5,
        out_specs=vmem,
        out_shape=jax.ShapeDtypeStruct((ROWS, D), F32),
        compiler_params=params(60),
        cost_estimate=cost(40 * ROWS * D, 4 * MB),
        name="norm_back",
    )(seq, tok, gain, g_res, own, other)


def mlp_kernel(
    info_ref,
    tok_ref,
    cot_ref,
    att_ref,
    vec_ref,
    fc_bias_ref,
    wp_ref,
    wf_ref,
    wo_ref,
    out_ref,
    g_res_ref,
    g_att_ref,
    d_vec_ref,
    d_fc_bias_ref,
    rows_ref,
    keep_ref,
    give_ref,
    n2_ref,
    g_out_ref,
    res_ref,
    acc_ref,
    gn_ref,
    wp_all_ref,
    turned_ref,
):
    step = pl.program_id(0)
    core = info_ref[SEQ_GRP + 1]
    proj_shift, gain, shift, out_shift = (vec_ref[k : k + 1] for k in range(4))

    def by_core(turned, first):
        for dp in range(16):
            turned_ref[dp % 2, place_of(dp) // 2] = turned[dp * BLK : (dp + 1) * BLK]
        keep_ref[first : first + 8] = turned_ref[core]
        give_ref[first : first + 8] = turned_ref[1 - core]

    @pl.when(step == 0)
    def _():
        turned = jnp.concatenate(
            [
                jnp.concatenate([att_ref[g, s] for g in range(4)], axis=0)
                for s in range(SEQ_GRP)
            ],
            axis=1,
        )
        att = turn(turned)
        pack = jnp.concatenate(
            [pack_of(half, PIECE, (BLK, CTX_N * PIECE), 0, 1) for half in range(2)],
            axis=0,
        )
        for dp in range(16):
            pieces = wp_ref[:, place_of(dp)].reshape(CTX_N * PIECE, COLS)
            halves = dot(pack, pieces).astype(BF16)
            rows = slice(dp * BLK, (dp + 1) * BLK)
            wp_all_ref[rows, :COLS] = halves[:BLK]
            wp_all_ref[rows, COLS:] = halves[BLK:]
        residual = tok_ref[...].astype(F32) + dot(att, wp_all_ref[...]) + proj_shift
        res_ref[...] = residual
        normed, _ = norm_stats(residual)
        normed = normed * gain + shift
        n2_ref[...] = normed.astype(BF16)
        by_core(normed.T.astype(BF16), 32)
        by_core(turned, 40)
        for seq in range(SEQ_GRP):
            cut = slice(seq * SPAN, (seq + 1) * SPAN)
            pos = info_ref[SEQ_GRP] + lax.broadcasted_iota(jnp.int32, (SPAN, D), 0)
            g_out_ref[cut] = jnp.where(
                pos < info_ref[seq], cot_ref[cut], jnp.zeros((SPAN, D), BF16)
            )
        rows_ref[:, 4 * D : 5 * D] = g_out_ref[...]
        acc_ref[...] = residual + out_shift
        gn_ref[...] = jnp.zeros_like(gn_ref)

    w_fc = jnp.concatenate([stack_rows(wf_ref, 0), stack_rows(wf_ref, 1)], axis=1)
    pre = dot(n2_ref[...], w_fc) + fc_bias_ref[...]
    root = math.sqrt(2.0 / math.pi)
    square = pre * pre
    bend = jnp.tanh(root * pre * (1.0 + 0.044715 * square))
    gate = 0.5 * (1.0 + bend)
    slope = gate + 0.5 * pre * (1.0 - bend * bend) * root * (
        1.0 + 3.0 * 0.044715 * square
    )
    act = pre * gate
    act_t = act.T.astype(BF16).reshape(2, 2, 4, BLK, ROWS)
    act = act.astype(BF16)
    for c in range(2):
        turned_ref[c] = act_t[:, c].reshape(8, BLK, ROWS)
    keep_ref[pl.ds(step * 8, 8)] = turned_ref[core]
    give_ref[pl.ds(step * 8, 8)] = turned_ref[1 - core]
    w_out = jnp.concatenate(
        [
            jnp.concatenate(
                [
                    wo_ref[z, yh, yl, 0, c, half * 40 : (half + 1) * 40]
                    for yl in range(2)
                    for c in range(2)
                    for z in range(4)
                    for yh in range(2)
                ],
                axis=0,
            )
            for half in range(2)
        ],
        axis=1,
    )
    acc_ref[...] += dot(act, w_out)
    g_act = dot_nt(g_out_ref[...], w_out)
    g_pre = (g_act * slope).astype(BF16)
    rows_ref[:, pl.ds(pl.multiple_of(step * D, D), D)] = g_pre
    d_fc_bias_ref[...] = jnp.sum(g_pre.astype(F32), axis=0, keepdims=True)
    gn_ref[...] += dot_nt(g_pre, w_fc)

    @pl.when(step == pl.num_programs(0) - 1)
    def _():
        out_ref[...] = acc_ref[...].astype(BF16)
        normed, scale = norm_stats(res_ref[...])
        g_norm = gn_ref[...]
        g_out = g_out_ref[...].astype(F32)
        g_res = (g_out + norm_back(normed, scale, gain, g_norm)).astype(BF16)
        g_res_ref[...] = g_res
        rows_ref[:, 5 * D :] = g_res
        d_vec_ref[0:1] = jnp.sum(g_res.astype(F32), axis=0, keepdims=True)
        d_vec_ref[1:2] = jnp.sum(g_norm * normed, axis=0, keepdims=True)
        d_vec_ref[2:3] = jnp.sum(g_norm, axis=0, keepdims=True)
        d_vec_ref[3:4] = jnp.sum(g_out, axis=0, keepdims=True)
        g_att = dot_nt(g_res, wp_all_ref[...])
        for seq in range(SEQ_GRP):
            turned = g_att[seq * SPAN : (seq + 1) * SPAN].T.astype(BF16)
            for g in range(4):
                g_att_ref[g, seq] = turned[g * GROUP_W : (g + 1) * GROUP_W]


def pack_of(half, piece, shape, row_dim, piece_dim):
    row = lax.broadcasted_iota(jnp.int32, shape, row_dim)
    place = lax.broadcasted_iota(jnp.int32, shape, piece_dim)
    offset = place - (piece - 10) * (row // 10) - 10 * half
    return (offset == row).astype(F32).astype(BF16)


def mlp_call(info, tok, cot, att, vecs, fc_bias, weights):
    by_ctx = weights.reshape(CTX_N, 16, 2 * BLK + PIECE, COLS)
    by_chip = weights.reshape(4, 2, 2, 4, 2, 2 * BLK + PIECE, COLS)
    rows = jax.ShapeDtypeStruct((ROWS, D), BF16)
    turned = jax.ShapeDtypeStruct((48, BLK, ROWS), BF16)
    return pl.pallas_call(
        mlp_kernel,
        grid=(4,),
        in_specs=[
            pl.BlockSpec(memory_space=pltpu.SMEM),
            whole((ROWS, D)),
            whole((ROWS, D)),
            whole((4, SEQ_GRP, GROUP_W, SPAN)),
            whole((4, D)),
            pl.BlockSpec((1, D), lambda j: (0, j)),
            pl.BlockSpec((CTX_N, 16, PIECE, COLS), lambda j: (0, 0, 5, 0)),
            pl.BlockSpec((2, 16, BLK, COLS), lambda j: (j, 0, 0, 0)),
            pl.BlockSpec(
                (4, 2, 2, 1, 2, BLK, COLS), lambda j: (0, 0, 0, j, 0, 1, 0)
            ),
        ],
        out_specs=[
            whole((ROWS, D)),
            whole((ROWS, D)),
            whole((4, SEQ_GRP, GROUP_W, SPAN)),
            whole((4, D)),
            pl.BlockSpec((1, D), lambda j: (0, j)),
            whole((ROWS, 6 * D)),
            whole((48, BLK, ROWS)),
            whole((48, BLK, ROWS)),
        ],
        out_shape=[
            rows,
            rows,
            jax.ShapeDtypeStruct((4, SEQ_GRP, GROUP_W, SPAN), BF16),
            jax.ShapeDtypeStruct((4, D), F32),
            jax.ShapeDtypeStruct((1, 4 * D), F32),
            jax.ShapeDtypeStruct((ROWS, 6 * D), BF16),
            turned,
            turned,
        ],
        scratch_shapes=[
            pltpu.VMEM((ROWS, D), BF16),
            pltpu.VMEM((ROWS, D), BF16),
            pltpu.VMEM((ROWS, D), F32),
            pltpu.VMEM((ROWS, D), F32),
            pltpu.VMEM((ROWS, D), F32),
            pltpu.VMEM((D, D), BF16),
            pltpu.VMEM((2, 8, BLK, ROWS), BF16),
        ],
        compiler_params=params(60),
        cost_estimate=cost(2 * ROWS * D * (16 * D + 2 * D), 38 * MB, 2 * ROWS * 4 * D),
        name="mlp",
    )(info, tok, cot, att, vecs, fc_bias, by_ctx, by_ctx, by_chip)


def both(ref, other_ref, axis):
    return jnp.concatenate([ref[...], other_ref[...]], axis=axis)


def fc_grad_kernel(
    n2_ref,
    n2_other_ref,
    g_ref,
    g_other_ref,
    att_ref,
    att_other_ref,
    g_res_ref,
    g_res_other_ref,
    out_ref,
    proj_ref,
):
    step = pl.program_id(0)

    @pl.when(step == 0)
    def _():
        att = both(att_ref, att_other_ref, 2).reshape(D // 2, 2 * ROWS)
        d_w = dot(att, both(g_res_ref, g_res_other_ref, 0)).astype(BF16)
        for chip in range(8):
            piece = None
            for half in range(2):
                unpack = pack_of(half, LAST, (CTX_N * LAST, BLK), 1, 0)
                part = dot(
                    unpack,
                    d_w[
                        chip * BLK : (chip + 1) * BLK, half * COLS : (half + 1) * COLS
                    ],
                )
                piece = part if piece is None else piece + part
            proj_ref[:, chip] = piece.astype(BF16).reshape(CTX_N, LAST, COLS)

    left = both(n2_ref, n2_other_ref, 2).reshape(D // 2, 2 * ROWS)
    d_w = dot(left, both(g_ref, g_other_ref, 0)).astype(BF16)
    for chip in range(8):
        for part in range(2):
            out_ref[chip % 4, part, chip // 4, :BLK] = d_w[
                chip * BLK : (chip + 1) * BLK, part * COLS : (part + 1) * COLS
            ]
            out_ref[chip % 4, part, chip // 4, BLK:] = proj_ref[2 * step + part, chip]


def fc_grad_call(turned, turned_other, rows, rows_other):
    n2_block = pl.BlockSpec((8, BLK, ROWS), lambda j: (4, 0, 0))
    g_block = pl.BlockSpec((ROWS, D), lambda j: (0, j))
    att_block = pl.BlockSpec((8, BLK, ROWS), lambda j: (5, 0, 0))
    g_res_block = pl.BlockSpec((ROWS, D), lambda j: (0, 5))
    last = BLK + LAST
    return pl.pallas_call(
        fc_grad_kernel,
        grid=(4,),
        in_specs=[
            n2_block,
            n2_block,
            g_block,
            g_block,
            att_block,
            att_block,
            g_res_block,
            g_res_block,
        ],
        out_specs=pl.BlockSpec((4, 2, 2, last, COLS), lambda j: (0, j, 0, 0, 0)),
        out_shape=jax.ShapeDtypeStruct((4, 8, 2, last, COLS), BF16),
        scratch_shapes=[pltpu.VMEM((CTX_N, 8, LAST, COLS), BF16)],
        compiler_params=params(60),
        cost_estimate=cost(10 * ROWS * D * D, 16 * MB),
        name="fc_grad",
    )(
        turned, turned_other, rows, rows_other, turned, turned_other, rows, rows_other
    )


def owners_kernel(place_ref, in_ref, *refs):
    *blocks, held = refs
    step = pl.program_id(0)
    rows = 8 * BLK
    row = lax.broadcasted_iota(jnp.int32, (rows, rows), 0)
    source = lax.broadcasted_iota(jnp.int32, (rows, rows), 1)
    wanted = (row // 10) % 8 * BLK + row // BLK * 10 + row % 10
    turn_rows = (source == wanted).astype(F32).astype(BF16)
    result = dot(turn_rows, in_ref[:, 0, :BLK].reshape(rows, COLS)).astype(BF16)
    for z in range(4):
        for yh in range(2):
            ctx = z * 2 + yh
            held[2 * yh + step, z, :BLK] = result[ctx * BLK : (ctx + 1) * BLK]
            held[2 * yh + step, z, BLK:] = in_ref[ctx, 0, BLK:]

    @pl.when(step == 1)
    def _():
        for by in range(4):
            blocks[by][...] = held[(place_ref[1] + by) % 4]


def owners_call(place, array):
    last = BLK + LAST
    return pl.pallas_call(
        owners_kernel,
        grid=(2,),
        in_specs=[
            pl.BlockSpec(memory_space=pltpu.SMEM),
            pl.BlockSpec((8, 1, last, COLS), lambda i: (0, i, 0, 0)),
        ],
        out_specs=[whole((4, last, COLS))] * 4,
        out_shape=[jax.ShapeDtypeStruct((4, last, COLS), BF16)] * 4,
        scratch_shapes=[pltpu.VMEM((4, 4, last, COLS), BF16)],
        compiler_params=params(60),
        cost_estimate=cost(4 * 640**3, 5 * MB),
        name="owners",
    )(place, array)


def out_grad_kernel(
    info_ref, act_ref, act_other_ref, g_ref, g_other_ref, out_ref, first_ref
):
    act = both(act_ref, act_other_ref, 2).reshape(8 * BLK, 2 * ROWS)
    d_w = dot(act, both(g_ref, g_other_ref, 0)).astype(BF16)
    for yl in range(2):
        for z in range(4):
            for yh in range(2):
                row = yl * 4 * BLK + (z * 2 + yh) * 40
                out_ref[yh, yl, z, 0, :40] = d_w[row : row + 40, :COLS]
                out_ref[yh, yl, z, 0, 40:] = d_w[row : row + 40, COLS:]
    first = info_ref[SEQ_GRP + 2]
    first_ref[...] = out_ref[first // 2, first % 2]


def out_grad_call(info, turned, turned_other, rows, rows_other):
    act_block = pl.BlockSpec((8, BLK, ROWS), lambda j: (j, 0, 0))
    g_block = pl.BlockSpec((ROWS, D), lambda j: (0, 4))
    return pl.pallas_call(
        out_grad_kernel,
        grid=(4,),
        in_specs=[
            pl.BlockSpec(memory_space=pltpu.SMEM),
            act_block,
            act_block,
            g_block,
            g_block,
        ],
        out_specs=[
            pl.BlockSpec((2, 2, 4, 1, BLK, COLS), lambda j: (0, 0, 0, j, 0, 0)),
            pl.BlockSpec((4, 1, BLK, COLS), lambda j: (0, j, 0, 0)),
        ],
        out_shape=[
            jax.ShapeDtypeStruct((2, 2, 4, 4, BLK, COLS), BF16),
            jax.ShapeDtypeStruct((4, 4, BLK, COLS), BF16),
        ],
        compiler_params=params(60),
        cost_estimate=cost(8 * ROWS * D * D, 16 * MB),
        name="out_grad",
    )(info, turned, turned_other, rows, rows_other)


def add_kernel(place_ref, arrived_ref, terms_ref, out_ref):
    del place_ref
    total = arrived_ref[...].astype(F32) + terms_ref[0].astype(F32)
    out_ref[...] = total.astype(BF16)


def add_call(place, at, arrived, terms):
    tall, rows, cols = arrived.shape
    part = 8
    block = pl.BlockSpec((part, rows, cols), lambda i, place: (i, 0, 0))
    nbytes = 6 * tall * rows * cols
    return pl.pallas_call(
        add_kernel,
        grid_spec=pltpu.PrefetchScalarGridSpec(
            num_scalar_prefetch=1,
            grid=(tall // part,),
            in_specs=[
                block,
                pl.BlockSpec(
                    (1, part, rows, cols), lambda i, place: (place[at], i, 0, 0)
                ),
            ],
            out_specs=[block],
        ),
        out_shape=[jax.ShapeDtypeStruct(arrived.shape, BF16)],
        compiler_params=params(60),
        cost_estimate=cost(nbytes // 4, nbytes),
        name="add_blocks",
    )(place, arrived, terms)


def add_four_kernel(at, place_ref, *refs):
    *blocks, held = refs[4:]
    total = refs[0][...].astype(F32)
    for ref in refs[1:4]:
        total = total + ref[...].astype(F32)
    held[...] = total.astype(BF16)
    for by in range(4):
        blocks[by][...] = held[(place_ref[at] + by) % 4]


def add_four_call(place, at, parts):
    vmem = pl.BlockSpec(memory_space=pltpu.VMEM)
    shape = parts[0].shape
    nbytes = 10 * math.prod(shape)
    return pl.pallas_call(
        functools.partial(add_four_kernel, at),
        in_specs=[pl.BlockSpec(memory_space=pltpu.SMEM)] + [vmem] * 4,
        out_specs=[vmem] * 4,
        out_shape=[jax.ShapeDtypeStruct(shape[1:], BF16)] * 4,
        scratch_shapes=[pltpu.VMEM(shape, BF16)],
        compiler_params=params(60),
        cost_estimate=cost(nbytes // 4, nbytes),
        name="add_four",
    )(place, *parts)


def ring_perm(axis):
    pairs = []
    for core in range(2):
        for pos in range(4):
            to = (pos + (1 if core == 0 else -1)) % 4
            if axis == "x":
                index = lambda p: p * 2 + core
            elif axis == "z":
                index = lambda p: core * 4 + p
            else:
                index = lambda p: ((p % 2) * 2 + core) * 2 + p // 2
            pairs.append((index(pos), index(to)))
    return {"x": ("x", "c"), "z": ("c", "z"), "y": ("yl", "c", "yh")}[axis], pairs


def swap_cores(array):
    return lax.ppermute(array, "c", [(0, 1), (1, 0)])


def shift_perm(axis, by):
    if axis != "y":
        return axis, [(p, (p + by) % 4) for p in range(4)]
    index = lambda p: (p % 2) * 2 + p // 2
    return ("yl", "yh"), [(index(p), index((p + by) % 4)) for p in range(4)]


def places():
    way = 1 - 2 * lax.axis_index("c")
    y = 2 * lax.axis_index("yh") + lax.axis_index("yl")
    ring = [(y - way * by) % 4 for by in (2, 3, 4, 1)]
    numbers = [lax.axis_index("x"), y, lax.axis_index("z"), *ring]
    return jnp.stack(numbers).astype(jnp.int32)


AT = {"x": 0, "y": 1, "z": 2, "ring": 3}


def directly(blocks, axis):
    return [blocks[0]] + [
        lax.ppermute(blocks[by], *shift_perm(axis, by)) for by in (1, 2, 3)
    ]


def total_of(parts):
    return sum(part.astype(F32) for part in parts)


def tie(first, second):
    return lax.optimization_barrier((first, second))


def per_device(
    tokens,
    lengths,
    cotangent,
    ln1_gain,
    ln1_bias,
    w_qkv,
    q_bias,
    v_bias,
    w_proj,
    proj_bias,
    ln2_gain,
    ln2_bias,
    w_fc,
    fc_bias,
    w_out,
    out_bias,
):
    ctx_rank = lax.axis_index(CTX)
    core = lax.axis_index("c")
    seq_rank = lax.axis_index("yh")
    head_group = lax.axis_index("z")
    tok = tokens.reshape(ROWS, D)
    cot = cotangent.reshape(ROWS, D)

    def exchange(array):
        return lax.all_to_all(array, CTX, 0, 0, tiled=True)

    groups = w_qkv.reshape(10, 3, 4, GROUP_W).transpose(2, 0, 1, 3)
    groups = groups.reshape(4, 10, HEADS_W)
    vec_one = jnp.concatenate([ln1_gain, ln1_bias, q_bias, v_bias])
    vec_one = jnp.pad(vec_one[None, None], ((0, 0), (0, 0), (0, HEADS_W - 40)))
    groups = jnp.concatenate([groups, jnp.broadcast_to(vec_one, (4, 1, HEADS_W))], axis=1)
    groups = jnp.broadcast_to(groups[:, None], (4, 2, 11, HEADS_W))
    w_cols = w_fc.reshape(10, CTX_N, COLS).transpose(1, 0, 2)
    w_cols = jnp.pad(w_cols, ((0, 0), (0, 0), (0, HEADS_W - COLS)))
    groups = groups.reshape(CTX_N, 11, HEADS_W)
    shards = exchange(jnp.concatenate([groups, w_cols], axis=1))

    vec_two = jnp.concatenate([proj_bias, ln2_gain, ln2_bias, out_bias, fc_bias])
    vec_two = jnp.pad(vec_two[None], ((0, PIECE - 21), (0, COLS - 80)))
    part = jnp.concatenate(
        [
            shards[:, 11:, :COLS].reshape(BLK, COLS),
            w_out.reshape(40, 2, COLS).transpose(1, 0, 2).reshape(BLK, COLS),
            w_proj.reshape(10, 2, COLS).transpose(1, 0, 2).reshape(20, COLS),
            vec_two,
        ],
        axis=0,
    )
    part, tokens = tie(part, tokens)
    weights = lax.all_gather(part, PLACE, axis=0, tiled=False)

    theirs = lax.dynamic_index_in_dim(tokens, 1 - seq_rank, 0, False)
    mine = lax.dynamic_index_in_dim(tokens, seq_rank, 0, False)
    theirs = lax.ppermute(theirs, "yh", [(0, 1), (1, 0)])
    sequence = jnp.where(
        seq_rank == 0, jnp.stack([mine, theirs]), jnp.stack([theirs, mine])
    )
    sequence = jnp.broadcast_to(sequence[None], (4, 2, SPAN, D))
    sequence = lax.all_to_all(sequence, "z", 0, 0, tiled=True).reshape(LEN, D)
    sequence, shards = tie(sequence, shards)

    w_group = jnp.concatenate(
        [shards[:, :10].reshape(BLK, HEADS_W), shards[:, 10]], axis=0
    )
    w_group = jnp.broadcast_to(w_group[None], (8, BLK + 8, HEADS_W))
    w_group = lax.all_to_all(w_group, ("x", "yl"), 0, 0, tiled=True)
    other = swap_cores(w_group)
    first = jnp.where(core == 0, w_group, other)
    second = jnp.where(core == 0, other, w_group)
    w_group = jnp.stack([first, second], axis=1).reshape(16, BLK + 8, HEADS_W)

    vecs = w_group[:, BLK:, :40].reshape(128, 4, 10).transpose(1, 0, 2)
    vecs = vecs.reshape(4, D).astype(F32)
    own = lax.dynamic_slice_in_dim(vecs[2:], head_group * GROUP_W, GROUP_W, 1)
    bias = jnp.concatenate([own[0:1], jnp.zeros((1, GROUP_W), F32), own[1:2]], axis=1)
    length = lax.dynamic_slice_in_dim(lengths, seq_rank, 1)
    qkv, att, lse = attend_call(length, sequence, vecs[:2], bias, w_group)
    att = exchange(att).reshape(4, SEQ_GRP, GROUP_W, SPAN)

    more = weights[:, 2 * BLK + 20, :80].reshape(4, 2, 2, 4, 2, 80)
    more = more.transpose(3, 2, 4, 0, 1, 5).reshape(128, 80).astype(F32)
    fc_shift = more[:, 40:].reshape(1, 4 * D)
    more = more[:, :40].reshape(128, 4, 10).transpose(1, 0, 2).reshape(4, D)
    place = places()
    info = jnp.stack([ctx_rank * SPAN, core, place[6], head_group]).astype(jnp.int32)
    info = jnp.concatenate([lengths, info])
    layer_out, g_res, g_att, d_vecs, d_fc_bias, rows, turned, turned_give = mlp_call(
        info, tok, cot, att, more, fc_shift, weights
    )

    turned_other = swap_cores(turned_give)
    rows_other = swap_cores(rows)
    g_att = exchange(g_att.reshape(CTX_N, GROUP_W, SPAN))
    d_fc = fc_grad_call(turned, turned_other, rows, rows_other)
    d_fc, (rows_other, g_att) = tie(d_fc, (rows_other, g_att))
    d_fc = lax.psum_scatter(d_fc, "x", scatter_dimension=0, tiled=False)
    d_out, sent = out_grad_call(info, turned, turned_other, rows, rows_other)
    d_out = d_out.reshape(4, 16, BLK, COLS)
    sent = sent.reshape(16, BLK, COLS)
    flight = lax.ppermute(sent, *ring_perm("y"))

    def ring_step(step, arrived):
        return add_call(place, AT["ring"] + step, arrived, d_out)[0]

    g_qkv = attend_back_call(length, qkv, g_att, lse)
    flight, g_qkv = tie(flight, g_qkv)
    sent, g_qkv = tie(ring_step(0, flight), g_qkv)
    flight = lax.ppermute(sent, *ring_perm("y"))
    *g_norm, d_norm = norm_grad_call(place, sequence, w_group, g_qkv)
    g_norm = directly(g_norm, "z")
    d_norm, g_qkv = tie(d_norm, g_qkv)
    group_keep, group_give = qkv_grad_call(
        info, sequence, vecs[:2], g_qkv, d_norm, d_vecs, d_fc_bias
    )
    flight, (group_keep, group_give) = tie(flight, (group_keep, group_give))
    sent, (group_keep, group_give) = tie(ring_step(1, flight), (group_keep, group_give))
    flight = lax.ppermute(sent, *ring_perm("y"))
    group_given = swap_cores(group_give)
    d_group = (group_keep.astype(F32) + group_given.astype(F32)).astype(BF16)
    d_group = lax.all_to_all(d_group, ("x", "yl"), 0, 0, tiled=True)

    d_fc = list(owners_call(place, d_fc))
    fc_parts = directly(d_fc, "y")
    d_fc[0], flight = tie(d_fc[0], flight)
    d_out = ring_step(2, flight)
    d_out = lax.all_to_all(d_out, ("z", "x"), 0, 0, tiled=True)
    _, g_norm = tie(fc_parts, g_norm)
    g_norm = total_of(g_norm).astype(BF16)
    g_own = lax.dynamic_index_in_dim(g_norm, seq_rank, 0, False)
    g_give = lax.dynamic_index_in_dim(g_norm, 1 - seq_rank, 0, False)
    g_other = lax.ppermute(g_give, "yh", [(0, 1), (1, 0)])
    d_group = jnp.sum(d_group.astype(F32), axis=0).astype(BF16)
    d_group = jnp.concatenate(
        [d_group[:BLK].reshape(CTX_N, 10, HEADS_W), d_group[BLK : BLK + 8, None]],
        axis=1,
    )
    d_fc = add_four_call(place, AT["z"], fc_parts)
    d_fc, d_out = tie(d_fc, d_out)
    fc_parts = directly(d_fc, "z")
    d_group = exchange(d_group)
    _, g_other = tie(d_fc[0], g_other)
    input_grad = norm_back_call(
        seq_rank.astype(jnp.int32)[None], tok, vecs[:1], g_res, g_own, g_other
    )
    last_sum = jnp.sum(d_out.astype(F32), axis=0)
    d_fc = total_of(fc_parts)
    d_fc, d_group = tie(d_fc, d_group)
    d_group = d_group.astype(F32)
    d_qkv = jnp.sum(d_group[:, :10].reshape(4, 2, 10, HEADS_W), axis=1)
    d_qkv = d_qkv.reshape(4, 10, 3, GROUP_W)
    d_qkv = d_qkv.transpose(1, 2, 0, 3).reshape(10, 3 * D)
    small = jnp.sum(d_group[:, 10, :120], axis=0)

    d_proj = d_fc[BLK : BLK + 20].reshape(2, 10, COLS).transpose(1, 0, 2).reshape(10, D)
    d_fc = d_fc[:BLK].reshape(CTX_N, 10, COLS).transpose(1, 0, 2)
    d_fc = d_fc.reshape(10, CTX_N * COLS)
    d_out = jnp.concatenate([last_sum[:40], last_sum[40:BLK]], axis=1)
    names = ["g1", "b1", "q", "v", "proj", "g2", "b2", "out"]
    vec = {n: small[10 * k : 10 * (k + 1)] for k, n in enumerate(names)}

    return (
        layer_out.reshape(tokens.shape),
        input_grad.reshape(tokens.shape),
        vec["g1"],
        vec["b1"],
        d_qkv,
        vec["q"],
        vec["v"],
        d_proj,
        vec["proj"],
        vec["g2"],
        vec["b2"],
        d_fc,
        small[80:120],
        d_out,
        vec["out"],
    )


def solution(mesh):
    fine = Mesh(mesh.devices.reshape(SIZES), AXES)
    rows = P(DP, CTX, None)
    mat = P(AXES, None)
    vec = P(AXES)
    in_specs = (
        rows,
        P(DP),
        rows,
        vec,
        vec,
        mat,
        vec,
        vec,
        mat,
        vec,
        vec,
        vec,
        mat,
        vec,
        mat,
        vec,
    )
    out_specs = (
        rows,
        rows,
        vec,
        vec,
        mat,
        vec,
        vec,
        mat,
        vec,
        vec,
        vec,
        mat,
        vec,
        mat,
        vec,
    )
    return jax.shard_map(
        per_device, mesh=fine, in_specs=in_specs, out_specs=out_specs, check_vma=False
    )
```
